128 devices in a mesh: dp: 32 (over x, z, core), col: 4 (over y).
Axes of the slice: x: 4, y: 4, z: 4, core: 2. Of those that a mesh axis runs over, the one named last changes fastest.
Arguments:
- act: bfloat16 [8192, 4096], P('dp'), may hold values from -6 to 6
- grad: bfloat16 [8192, 4096], P('dp'), may hold values from -6 to 6
- lengths: int32 [64], P('dp'), may hold values from 1 to 128, 6144 in all
- basis_in: bfloat16 [4096, 4096], P(None, 'col')
- basis_out: bfloat16 [4096, 4096], P(None, 'col')
- query_act: bfloat16 [1024, 4096], P('dp'), may hold values from -6 to 6
- query_grad: bfloat16 [1024, 4096], P('dp'), may hold values from -6 to 6
Outputs:
- scores: float32 [64, 32], P('dp')
The draws below stay inside these ranges and needn't reach their ends.
All inputs are finite; a program needn't handle non-finite values. No bound on the sum of `lengths` on one device may be relied on, other than what follows from the above.
Results may differ from the reference program's by a relative error of at most 0.0015.
The reference program's roundings to bfloat16 on the way (of `masked`, `scaled` and `solved`) count: a program that leaves them out, or rounds other values in their place, can miss the bound.
Values may be sent and summed in bfloat16 or wider, within the bound.
A program may use at most 192 MiB of HBM per device.

```python
import math
import jax
import jax.numpy as jnp
import numpy as np
from jax import lax

DI = 4096
DO = 4096
RANK = 32
RLEN = 128
RESPONSES = 64
TOKENS = 8192
QUERIES = 32
QTOKENS = 1024


def draw_basis_in(key, part):
    key = jax.random.fold_in(key, 11)
    first, second = jax.random.split(key)
    values = jax.random.normal(first, (DI, DI), jnp.float32)
    spread = 1.3862944
    column = jnp.exp(jax.random.uniform(second, (1, DI), jnp.float32) * spread)
    return (values * column / math.sqrt(DI)).astype(jnp.bfloat16)


def draw_basis_out(key, part):
    key = jax.random.fold_in(key, 23)
    first, second = jax.random.split(key)
    values = jax.random.normal(first, (DO, DO), jnp.float32)
    spread = 1.3862944
    column = jnp.exp(jax.random.uniform(second, (1, DO), jnp.float32) * spread)
    return (values * column / math.sqrt(DO)).astype(jnp.bfloat16)


def shard_levels(rng, extent, shards, smallest, high):
    factor_of = 1.0
    for dim, parts in shards:
        draws = jax.random.uniform(jax.random.fold_in(jax.random.fold_in(rng, 6), dim), (parts,), jnp.float32, smallest / len(shards), high / len(shards))
        factor_of = factor_of * jnp.repeat(jnp.exp(draws), extent[dim] // parts).reshape((-1,) + (1,) * (len(extent) - 1 - dim))
    return factor_of


def length_profile(amount, total, bound, skew):
    portions = [(1 << 20) // math.isqrt(standing ** skew) + 1 for standing in range(2, amount + 1)]
    spare, holding = total - bound - (amount - 1), [1] * (amount - 1)
    while spare > 0:
        movable = [i for i in range(amount - 1) if holding[i] < bound]
        whole, budget = sum([portions[i] for i in movable]), spare
        for i in movable:
            more = min(bound - holding[i], max(1, budget * portions[i] // whole), spare)
            holding[i] = holding[i] + more
            spare = spare - more
    return np.array([bound] + holding)


def ragged_sizes(own_key, number_of, total, reach, lean):
    if number_of == 2:
        one = jax.random.randint(own_key, (), max(1, total - reach), min(reach, total - 1) + 1)
        return jnp.stack([one, total - one])
    sizes = jnp.asarray(length_profile(number_of, total, reach, lean), jnp.int32)
    twos = (number_of - 1) // 2
    source_of, sink = sizes[1:1 + 2 * twos:2], sizes[2:2 + 2 * twos:2]
    margin = jnp.minimum(source_of - 1, reach - sink)
    passed = jax.random.randint(jax.random.fold_in(own_key, 1), (twos,), 0, 1 << 20) % (margin + 1)
    sizes = sizes.at[1:1 + 2 * twos:2].set(source_of - passed).at[2:2 + 2 * twos:2].set(sink + passed)
    return sizes[jax.random.permutation(jax.random.fold_in(own_key, 2), number_of)]


def scatter_about(key, shape, width, bound, shards=(), held_as=jnp.bfloat16):
    level = shard_levels(key, shape, shards, -0.22, 0.18) if shards else 1.0
    result = jax.random.normal(key, shape, jnp.float32) * width * level
    return jnp.minimum(jnp.maximum(result, -bound), bound).astype(held_as)


def setup_inputs(seed: int = 0) -> dict:
    streams_of = jax.random.split(jax.random.key(seed), 8)
    act = scatter_about(streams_of[0], (TOKENS, DI), 1.0, 6.0, ((0, 32),))
    grad = scatter_about(streams_of[1], (TOKENS, DO), 1.0, 6.0, ((0, 32),))
    lengths = ragged_sizes(streams_of[2], RESPONSES, RESPONSES * RLEN * 3 // 4, RLEN, 1).astype(jnp.int32)
    basis_in = draw_basis_in(jax.random.fold_in(streams_of[7], 71), 0)
    basis_out = draw_basis_out(jax.random.fold_in(streams_of[7], 71), 0)
    query_act = scatter_about(streams_of[5], (QTOKENS, DI), 1.0, 6.0, ((0, 32),))
    query_grad = scatter_about(streams_of[6], (QTOKENS, DO), 1.0, 6.0, ((0, 32),))
    return dict(act=act, grad=grad, lengths=lengths, basis_in=basis_in, basis_out=basis_out, query_act=query_act, query_grad=query_grad)


damping_share = 0.1
ridge_share = 0.05
epsilon_add = 1e-06

def reference(act, grad, lengths, basis_in, basis_out, query_act, query_grad):
    live_mask = (jnp.arange(RLEN, dtype=jnp.int32)[None, :] < lengths[:, None]).reshape(TOKENS, 1).astype(jnp.bfloat16)
    masked = grad * live_mask
    rot_in = jnp.dot(act.astype(jnp.float32), basis_in.astype(jnp.float32), preferred_element_type=jnp.float32).astype(jnp.bfloat16)
    rot_out = jnp.dot(masked.astype(jnp.float32), basis_out.astype(jnp.float32), preferred_element_type=jnp.float32).astype(jnp.bfloat16)

    def accumulate(carry, pair):
        grad_rows, act_rows = pair
        product = lax.dot_general(grad_rows.astype(jnp.float32), act_rows.astype(jnp.float32), (((0,), (0,)), ((), ())), preferred_element_type=jnp.float32)
        return (carry + product * product, None)
    squares, unused = lax.scan(accumulate, jnp.zeros((DO, DI), jnp.float32), (rot_out.reshape(RESPONSES, RLEN, DO), rot_in.reshape(RESPONSES, RLEN, DI)))
    corr = squares / RESPONSES
    damping_add = damping_share * jnp.mean(corr) + epsilon_add
    query_out = jnp.dot(query_grad.astype(jnp.float32), basis_out.astype(jnp.float32), preferred_element_type=jnp.float32).astype(jnp.bfloat16)
    query_in = jnp.dot(query_act.astype(jnp.float32), basis_in.astype(jnp.float32), preferred_element_type=jnp.float32).astype(jnp.bfloat16)
    ridge_eye = ridge_share * DO * jnp.eye(RANK, dtype=jnp.float32)

    def precondition(pair):
        left_rows, right_rows = pair
        rotated = lax.dot_general(left_rows.astype(jnp.float32), right_rows.astype(jnp.float32), (((0,), (0,)), ((), ())), preferred_element_type=jnp.float32)
        scaled = (rotated / (corr + damping_add)).astype(jnp.bfloat16)
        projected = jnp.dot(left_rows.astype(jnp.float32), scaled.astype(jnp.float32), preferred_element_type=jnp.float32)
        gram = jnp.dot(left_rows.astype(jnp.float32), left_rows.T.astype(jnp.float32), preferred_element_type=jnp.float32) + ridge_eye
        factor = jnp.linalg.cholesky(gram)
        middle = lax.linalg.triangular_solve(factor, projected, left_side=True, lower=True)
        solved = lax.linalg.triangular_solve(factor, middle, left_side=True, lower=True, transpose_a=True)
        return solved.astype(jnp.bfloat16)
    solved = lax.map(precondition, (query_out.reshape(QUERIES, RANK, DO), query_in.reshape(QUERIES, RANK, DI)))
    left_side = jnp.dot(rot_out.astype(jnp.float32), query_out.T.astype(jnp.float32), preferred_element_type=jnp.float32)
    right_side = jnp.dot(rot_in.astype(jnp.float32), solved.reshape(QTOKENS, DI).T.astype(jnp.float32), preferred_element_type=jnp.float32)
    joined = (left_side * right_side).reshape(TOKENS, QUERIES, RANK).sum(axis=2)
    return joined.reshape(RESPONSES, RLEN, QUERIES).sum(axis=1) / RLEN
```

```python
import functools

import jax
import jax.numpy as jnp
from jax import lax
from jax.experimental import pallas as pl
from jax.experimental.pallas import tpu as pltpu
from jax.sharding import PartitionSpec as P


RLEN = 128
RANK = 32
DIM = 4096
WIDTH = 1024
TOK = 256
PARTS = 8
damping_share = 0.1
ridge_share = 0.05
epsilon_add = 1e-06
BF = jnp.bfloat16
F32 = jnp.float32
MESH = pl.DeviceIdType.MESH
HIGH = lax.Precision.HIGHEST


def dot(a, b, dims, precision=None):
    return lax.dot_general(a, b, (dims, ((), ())), preferred_element_type=F32, precision=precision)


NN = ((1,), (0,))
TN = ((0,), (0,))
NT = ((1,), (1,))


class Slots:
    def __init__(self):
        self.count = 0

    def take(self, n):
        first = self.count
        self.count += n
        return first


SL = Slots()
S_SWAP_I = SL.take(2)
S_SWAP_A = SL.take(1)
S_SWAP_G = SL.take(4)
S_Y_I = SL.take(6)
S_L1 = SL.take(3)
S_L2 = SL.take(3)
S_LS = SL.take(1)
S_A = SL.take(15)
S_AY = SL.take(3)
S_FAR = SL.take(2 * PARTS)
S_NEAR = SL.take(2 * PARTS)
S_FAR2 = SL.take(2 * PARTS)
S_NEAR2 = SL.take(2 * PARTS)
S_GRAM = SL.take(3)
S_LEFT = SL.take(3)
S_LEFTS = SL.take(1)
S_D1 = SL.take(7)
S_D2 = SL.take(15)
S_PROJ = SL.take(3)
S_S1 = SL.take(3)
S_S2 = SL.take(3)
S_FIN = SL.take(7)
N_SEM = SL.count


def kernel(
    act, grad, lens, b_in, b_out, q_act, q_grad,
    out,
    xin, xout, bin_, bout, send_i, ibuf, gbuf, lb, at_send, a_own, a_recv, a4,
    acc, snd, far, near, snd2, far2, near2, corr,
    gram_s, gram_r, left_s, left_r, left_f, damp_1, damp_2, inv_bd, proj_s, proj_r, sb, fin,
    load_sem, ss, rs,
):
    dp = lax.axis_index("dp")
    y = lax.axis_index("col")
    x, z, h = dp // 8, (dp // 2) % 4, dp % 2
    u = x * (1 - h) + z * h
    v = z * (1 - h) + x * h
    me = u * 4 + v

    def dev_xz(xx, zz, hh, yy):
        return ((xx % 4) * 8 + (zz % 4) * 2 + hh, yy % 4)

    def dev(du, dv):
        uu, vv = u + du, v + dv
        return dev_xz(uu * (1 - h) + vv * h, vv * (1 - h) + uu * h, h, y)

    def dev_y(dy, dh=0):
        return dev_xz(x, z, (h + dh) % 2, y + dy)

    sibling = dev_y(0, 1)
    pending = []

    def copy(src, dst, idx, to):
        return pltpu.make_async_remote_copy(
            src_ref=src, dst_ref=dst, send_sem=ss.at[idx], recv_sem=rs.at[idx], device_id=to, device_id_type=MESH
        )

    def send(src, dst, idx, to):
        c = copy(src, dst, idx, to)
        c.start()
        pending.append(c)

    def tile_in(k):
        half = (1 - h) * (1 - k // 2) + h * (k // 2)
        return half * 2 + k % 2

    def load_in(k):
        cols = pl.ds(pl.multiple_of(tile_in(k) * 256, 256), 256)
        return pltpu.make_async_copy(b_in.at[:, cols], bin_.at[k], load_sem.at[4 + k])

    def load_out(k):
        cols = pl.ds(pl.multiple_of(k * 256, 256), 256)
        return pltpu.make_async_copy(b_out.at[:, cols], bout.at[k], load_sem.at[8 + k])

    rows_of = [
        pltpu.make_async_copy(act, xin.at[pl.ds(0, TOK)], load_sem.at[0]),
        pltpu.make_async_copy(q_act, xin.at[pl.ds(TOK, RANK)], load_sem.at[1]),
        pltpu.make_async_copy(grad, xout.at[pl.ds(0, TOK)], load_sem.at[2]),
        pltpu.make_async_copy(q_grad, xout.at[pl.ds(TOK, RANK)], load_sem.at[3]),
    ]
    rows_of[0].start()
    rows_of[1].start()
    for k in range(4):
        load_in(k).start()
    rows_of[2].start()
    rows_of[3].start()
    for k in range(4):
        load_out(k).start()

    barrier = pltpu.get_barrier_semaphore()
    peers = [dev(du, dv) for du in range(4) for dv in range(4) if du or dv]
    peers += [dev_y(dy, dh) for dy in range(4) for dh in range(2) if dy or dh]
    for to in peers:
        pl.semaphore_signal(barrier, inc=1, device_id=to, device_id_type=MESH)
    pl.semaphore_wait(barrier, len(peers))

    lane = lax.broadcasted_iota(jnp.int32, (RANK, 128), 1)
    spread = (lane == lax.broadcasted_iota(jnp.int32, (RANK, 128), 0) + RANK * u).astype(BF)

    rows_of[0].wait()
    rows_of[1].wait()
    own_rows = pl.ds(pl.multiple_of(h * TOK, TOK), TOK)

    def swap_i(k):
        return copy(send_i.at[k], ibuf.at[k, own_rows], S_SWAP_I + k, sibling)

    def step_in(k, carry):
        load_in(k).wait()
        r = dot(xin[...], bin_[k], NN).astype(BF)
        at = dot(r[TOK:], spread, TN).astype(BF).reshape(16, 16, 128)

        @pl.when(k < 2)
        def _():
            send_i[k] = r[:TOK]
            at_send[k] = at
            swap_i(k).start()

        @pl.when(k >= 2)
        def _():
            ibuf[k - 2, own_rows] = r[:TOK]
            a_own[h, k - 2] = at

        return carry

    lax.fori_loop(0, 4, step_in, 0)
    send(at_send, a_own.at[h], S_SWAP_A, sibling)
    for k in range(2):
        swap_i(k).wait_recv()
    send(ibuf.at[0], ibuf.at[2], S_Y_I + 0, dev_y(1))
    send(ibuf.at[1], ibuf.at[3], S_Y_I + 1, dev_y(3))
    send(ibuf.at[1], ibuf.at[4], S_Y_I + 2, dev_y(1))
    send(ibuf.at[0], ibuf.at[5], S_Y_I + 3, dev_y(3))

    rows_of[2].wait()
    rows_of[3].wait()
    row = lax.broadcasted_iota(jnp.int32, (TOK, 256), 0)
    live = (row < lens[0]) | ((row >= RLEN) & (row < RLEN + lens[1]))
    live = live & ((row >= RLEN) | (row < lens[0]))

    def swap_g(k):
        part = gbuf.at[own_rows, pl.ds(pl.multiple_of(k * 256, 256), 256)]
        return copy(part, part, S_SWAP_G + k, sibling)

    def step_out(k, carry):
        load_out(k).wait()
        cols = pl.ds(pl.multiple_of(k * 256, 256), 256)
        r = dot(xout[...], bout[k], NN)
        gbuf[own_rows, cols] = jnp.where(live, r[:TOK], 0.0).astype(BF)
        swap_g(k).start()
        lb[h, v, u, :, cols] = r[TOK:].astype(BF)
        return carry

    lax.fori_loop(0, 4, step_out, 0)

    for d in range(1, 4):
        part = lb.at[h, v, u]
        send(part, part, S_L1 + d - 1, dev(d, 0))
    copy(at_send, a_own.at[1 - h], S_SWAP_A, sibling).wait_recv()
    others = [(du, dv) for du in range(4) for dv in range(4) if du or dv]
    for n, (du, dv) in enumerate(others):
        there = ((u + du) % 4) * 4 + (v + dv) % 4
        send(a_own.at[:, :, there], a_recv.at[me], S_A + n, dev(du, dv))
    a_recv[me] = a_own[:, :, me]

    def swap_g_wait(k, carry):
        swap_g(k).wait_recv()
        return carry

    lax.fori_loop(0, 4, swap_g_wait, 0)

    damp_1[0] = jnp.zeros((8, 128), F32)
    group = lax.broadcasted_iota(jnp.int32, (128, 128), 1) // RANK

    def place(i):
        first = (i < 2) * 1
        last = (i >= 6) * 1
        mid = 1 - first - last
        back = 1 - i % 2
        sigma = (y + last * 2 + mid * (back * 3 + (1 - back))) % 4
        k = (first + last) * (i % 2) + mid * ((i == 3) * 1 + (i == 4) * 1)
        return sigma * 2 + k

    def rows64(uu):
        return pl.ds(pl.multiple_of((uu % 4) * 64, 64), 64)

    def far_copies(i):
        over = (u + 2) % 4
        return (
            copy(snd.at[i, pl.ds(pl.multiple_of(over * 64, 64), 32)], far.at[i, 0], S_FAR + 2 * i, dev(1, 0)),
            copy(snd.at[i, pl.ds(pl.multiple_of(over * 64 + 32, 32), 32)], far.at[i, 1], S_FAR + 2 * i + 1, dev(3, 0)),
        )

    def near_copies(i):
        return (
            copy(snd.at[i, rows64(u + 1)], near.at[i, 0], S_NEAR + 2 * i, dev(1, 0)),
            copy(snd.at[i, rows64(u + 3)], near.at[i, 1], S_NEAR + 2 * i + 1, dev(3, 0)),
        )

    def far2_copies(i):
        over = (v + 2) % 4
        return (
            copy(snd2.at[i, over, :, pl.ds(0, 512)], far2.at[i, 0], S_FAR2 + 2 * i, dev(0, 1)),
            copy(snd2.at[i, over, :, pl.ds(512, 512)], far2.at[i, 1], S_FAR2 + 2 * i + 1, dev(0, 3)),
        )

    def near2_copies(i):
        return (
            copy(snd2.at[i, (v + 1) % 4], near2.at[i, 0], S_NEAR2 + 2 * i, dev(0, 1)),
            copy(snd2.at[i, (v + 3) % 4], near2.at[i, 1], S_NEAR2 + 2 * i + 1, dev(0, 3)),
        )

    def relay(i):
        return copy(ibuf.at[i], ibuf.at[i + 4], S_Y_I + i + 2, dev_y(1 + 2 * (i - 2)))

    def stage_squares(i):
        @pl.when(i >= 2)
        def _():
            copy(ibuf.at[i], ibuf.at[i], S_Y_I + i - 2, dev_y(1)).wait_recv()

        @pl.when((i == 2) | (i == 3))
        def _():
            relay(i).start()

        def tile(t, total):
            cols = pl.ds(pl.multiple_of(t * 256, 256), 256)
            value = None
            for n in range(4):
                r = dot(ibuf[i, n * RLEN : (n + 1) * RLEN], gbuf[n * RLEN : (n + 1) * RLEN, cols], TN)
                value = r * r if value is None else value + r * r
            acc[i, :, cols] = value
            return total + value.reshape(32, 8, 256).sum(axis=0)

        total = lax.fori_loop(0, 4, tile, jnp.zeros((8, 256), F32))
        damp_1[0] += total[:, :128] + total[:, 128:]
        over = rows64(u + 2)
        snd[i, over] = acc[i, over].astype(BF)
        for c in far_copies(i):
            c.start()

    def stage_near(i):
        for c in far_copies(i):
            c.wait_recv()
        a = pl.multiple_of(((u + 1) % 4) * 64, 64)
        snd[i, pl.ds(a, 32)] = (acc[i, pl.ds(a, 32)] + far[i, 0].astype(F32)).astype(BF)
        snd[i, pl.ds(a + 32, 32)] = acc[i, pl.ds(a + 32, 32)].astype(BF)
        b = pl.multiple_of(((u + 3) % 4) * 64, 64)
        snd[i, pl.ds(b, 32)] = acc[i, pl.ds(b, 32)].astype(BF)
        snd[i, pl.ds(b + 32, 32)] = (acc[i, pl.ds(b + 32, 32)] + far[i, 1].astype(F32)).astype(BF)
        for c in near_copies(i):
            c.start()

    def own16(vv):
        return pl.ds(pl.multiple_of(u * 64 + (vv % 4) * 16, 16), 16)

    def stage_far2(i):
        for c in near_copies(i):
            c.wait_recv()
        acc[i, rows64(u)] += near[i, 0].astype(F32) + near[i, 1].astype(F32)
        snd2[i, (v + 2) % 4] = acc[i, own16(v + 2)].astype(BF)
        for c in far2_copies(i):
            c.start()

    def stage_near2(i):
        for c in far2_copies(i):
            c.wait_recv()
        a, b = (v + 1) % 4, (v + 3) % 4
        snd2[i, a, :, :512] = (acc[i, own16(a), :512] + far2[i, 0].astype(F32)).astype(BF)
        snd2[i, a, :, 512:] = acc[i, own16(a), 512:].astype(BF)
        snd2[i, b, :, :512] = acc[i, own16(b), :512].astype(BF)
        snd2[i, b, :, 512:] = (acc[i, own16(b), 512:] + far2[i, 1].astype(F32)).astype(BF)
        for c in near2_copies(i):
            c.start()

    def stage_last(i):
        for c in near2_copies(i):
            c.wait_recv()
        corr[place(i)] = acc[i, own16(v)] + near2[i, 0].astype(F32) + near2[i, 1].astype(F32)

    def query_second():
        for d in range(1, 4):
            part = lb.at[h, v, u]
            copy(part, part, S_L1 + d - 1, dev(d, 0)).wait_recv()
        for d in range(1, 4):
            part = lb.at[h, v]
            copy(part, part, S_L2 + d - 1, dev(0, d)).start()

    def query_third():
        for d in range(1, 4):
            part = lb.at[h, v]
            copy(part, part, S_L2 + d - 1, dev(0, d)).wait_recv()
        copy(lb.at[h], lb.at[h], S_LS, sibling).start()
        for n, (du, dv) in enumerate(others):
            copy(a_own.at[:, :, me], a_recv.at[me], S_A + n, dev(du, dv)).wait_recv()
        for other in range(2):
            for vv in range(4):
                same = 1 - (other - h) * (other - h)
                total = jnp.zeros((32, 128), F32)
                for uu in range(4):
                    slot = same * (uu * 4 + vv) + (1 - same) * (vv * 4 + uu)
                    total = total + a_recv[slot, other].reshape(32, 128).astype(F32)
                a4[y, other * 4 + vv] = total.astype(BF)
        for d in range(1, 4):
            copy(a4.at[y], a4.at[y], S_AY + d - 1, dev_y(d)).start()

    def lgroup(g):
        return lb[g // 4, g % 4].reshape(128, WIDTH)

    def query_products():
        copy(lb.at[h], lb.at[1 - h], S_LS, sibling).wait_recv()

        def one(g, carry):
            rows = lgroup(g)
            full = dot(rows, rows, NT)
            packed = jnp.zeros((RANK, 128), F32)
            for q in range(4):
                packed = packed + jnp.where(lane // RANK == q, full[q * RANK : (q + 1) * RANK], 0.0)
            gram_s[g // 2, g % 2] = packed
            left_s[g // 2, :, pl.ds(pl.multiple_of((g % 2) * 128, 128), 128)] = dot(gbuf[own_rows], rows, NT)
            return carry

        lax.fori_loop(0, 8, one, 0)
        for d in (2, 1, 3):
            there = (y + d) % 4
            copy(gram_s.at[there], gram_r.at[d - 1], S_GRAM + d - 1, dev_y(d)).start()
        for d in (2, 1, 3):
            there = (y + d) % 4
            copy(left_s.at[there], left_r.at[d - 1], S_LEFT + d - 1, dev_y(d)).start()

    line = [(dy, dh) for dy in range(4) for dh in range(2) if dy or dh]

    def damping_first():
        for n, (dy, dh) in enumerate(line):
            copy(damp_1.at[0], damp_1.at[1 + n], S_D1 + n, dev_y(dy, dh)).start()

    def damping_second():
        for n, (dy, dh) in enumerate(line):
            copy(damp_1.at[0], damp_1.at[1 + n], S_D1 + n, dev_y(dy, dh)).wait_recv()
        damp_2[0] = damp_1[...].sum(axis=0)
        for n, (du, dv) in enumerate(others):
            copy(damp_2.at[0], damp_2.at[1 + n], S_D2 + n, dev(du, dv)).start()

    def gram_inverse():
        for d in range(1, 4):
            copy(gram_s.at[y], gram_r.at[d - 1], S_GRAM + d - 1, dev_y(d)).wait_recv()
        gram = gram_s[y] + gram_r[0] + gram_r[1] + gram_r[2]
        lane2 = lax.broadcasted_iota(jnp.int32, (128, 128), 1)
        sub2 = lax.broadcasted_iota(jnp.int32, (128, 128), 0)
        fold = ((sub2 % RANK == lane2) & (lane2 < RANK)).astype(F32)
        block = sub2 // RANK == lane2 // RANK
        wide = []
        for e in range(2):
            tall = jnp.concatenate([gram[e]] * 4, axis=0)
            wide.append(dot(jnp.where(block, tall, 0.0), fold, NN, HIGH).reshape(4, RANK, 128))
        w = jnp.concatenate(wide, axis=0)
        li = lax.broadcasted_iota(jnp.int32, (8, RANK, 128), 2)
        ri = lax.broadcasted_iota(jnp.int32, (8, RANK, 128), 1)
        w = w + jnp.where(li == ri, ridge_share * DIM, 0.0)

        def sweep(k, w):
            at_k = li == k
            col = jnp.where(at_k, w, 0.0).sum(axis=2, keepdims=True)
            rowk = jnp.where(ri == k, w, 0.0).sum(axis=1, keepdims=True)
            pivot = jnp.where(at_k[:, :1], rowk, 0.0).sum(axis=2, keepdims=True)
            rowk = jnp.where(at_k[:, :1], 1.0, rowk) / pivot
            return jnp.where(ri == k, rowk, jnp.where(at_k, 0.0, w) - col * rowk)

        w = lax.fori_loop(0, RANK, sweep, w)
        for e in range(2):
            flat = w[e * 4 : (e + 1) * 4].reshape(128, 128)
            inv_bd[e] = jnp.where(block, dot(flat, fold, NT, HIGH), 0.0)

    def left_sum():
        for d in range(1, 4):
            copy(left_s.at[y], left_r.at[d - 1], S_LEFT + d - 1, dev_y(d)).wait_recv()
        left_f[own_rows] = left_s[y] + left_r[0] + left_r[1] + left_r[2]
        copy(left_f.at[own_rows], left_f.at[own_rows], S_LEFTS, sibling).start()

    def step(i, carry):
        @pl.when(i < PARTS)
        def _():
            stage_squares(i)

        @pl.when((i >= 1) & (i < PARTS + 1))
        def _():
            stage_near(i - 1)

        @pl.when((i >= 2) & (i < PARTS + 2))
        def _():
            stage_far2(i - 2)

        @pl.when((i >= 3) & (i < PARTS + 3))
        def _():
            stage_near2(i - 3)

        @pl.when(i >= 4)
        def _():
            stage_last(i - 4)

        pl.when(i == 1)(query_second)
        pl.when(i == 3)(query_third)
        pl.when(i == 5)(query_products)
        pl.when(i == 7)(damping_first)

        @pl.when(i == 8)
        def _():
            gram_inverse()
            damping_second()

        pl.when(i == 9)(left_sum)
        return carry

    lax.fori_loop(0, PARTS + 4, step, 0)

    for n, (du, dv) in enumerate(others):
        copy(damp_2.at[0], damp_2.at[1 + n], S_D2 + n, dev(du, dv)).wait_recv()
    total = jnp.sum(damp_2[...])
    damping = damping_share * (total / 64.0 / (DIM * DIM)) + epsilon_add
    corr[...] = 1.0 / (corr[...] / 64.0 + damping)
    for d in range(1, 4):
        copy(a4.at[y], a4.at[y], S_AY + d - 1, dev_y(d)).wait_recv()

    def solve_group(g):
        a = a4[:, g].reshape(128, 128)
        a_all = jnp.concatenate([jnp.where(group == q, a, jnp.zeros_like(a)) for q in range(4)], axis=0)

        def tile(t, p):
            cols = pl.ds(pl.multiple_of(t * 256, 256), 256)
            rows = lb[g // 4, g % 4, :, :, cols].reshape(128, 256)
            rotated = dot(a_all, rows, NN)
            weight = corr[:, :, cols].reshape(1, 128, 256)
            scaled = (rotated.reshape(4, 128, 256) * weight).reshape(512, 256).astype(BF)
            return p + dot(scaled, rows, NT)

        p = lax.fori_loop(0, 4, tile, jnp.zeros((512, 128), F32))
        packed = jnp.zeros((128, 128), F32)
        for q in range(4):
            packed = packed + jnp.where(group == q, p[q * 128 : (q + 1) * 128], 0.0)
        proj_s[g // 2, g % 2] = packed

    def proj_copy(d):
        there = (y + d) % 4
        return copy(proj_s.at[there], proj_r.at[d - 1], S_PROJ + d - 1, dev_y(d))

    def solve_plane(n, carry):
        d = (n == 0) * 2 + (n == 1) * 1 + (n == 2) * 3
        there = (y + d) % 4
        solve_group(there * 2)
        solve_group(there * 2 + 1)

        @pl.when(n < 3)
        def _():
            proj_copy(d).start()

        return carry

    lax.fori_loop(0, 4, solve_plane, 0)
    for d in range(1, 4):
        proj_copy(d).wait_recv()
    mine = pl.ds(pl.multiple_of(me * 16, 16), 16)
    for e in range(2):
        whole = proj_s[y, e] + proj_r[0, e] + proj_r[1, e] + proj_r[2, e]
        solved = dot(whole, inv_bd[e], NN, HIGH).astype(BF)
        sb[:, mine, e * 128 : (e + 1) * 128] = solved.reshape(PARTS, 16, 128)

    def solved_first(d):
        return copy(sb.at[:, mine], sb.at[:, mine], S_S1 + d - 1, dev(0, d))

    def solved_second(d):
        part = sb.at[:, pl.ds(pl.multiple_of(u * 64, 64), 64)]
        return copy(part, part, S_S2 + d - 1, dev(d, 0))

    for d in range(1, 4):
        solved_first(d).start()
    for d in range(1, 4):
        solved_first(d).wait_recv()
    for d in range(1, 4):
        solved_second(d).start()
    copy(left_f.at[own_rows], left_f.at[own_rows], S_LEFTS, sibling).wait_recv()
    for d in range(1, 4):
        solved_second(d).wait_recv()

    def right_part(i, total):
        return total + dot(ibuf[i], sb[place(i)], NN)

    right = lax.fori_loop(0, PARTS, right_part, jnp.zeros((2 * TOK, 256), F32))
    joined = (left_f[...] * right).reshape(4, RLEN, 256).sum(axis=1)
    fin[y, h] = jnp.concatenate([joined, jnp.zeros((4, 256), F32)], axis=0)
    for n, (dy, dh) in enumerate(line):
        copy(fin.at[y, h], fin.at[y, h], S_FIN + n, dev_y(dy, dh)).start()
    p_of = lax.broadcasted_iota(jnp.int32, (256, 128), 0) // RANK
    q_of = lax.broadcasted_iota(jnp.int32, (256, 128), 1)
    for n, (dy, dh) in enumerate(line):
        copy(fin.at[y, h], fin.at[y, h], S_FIN + n, dev_y(dy, dh)).wait_recv()
    scores = jnp.zeros((8, 128), F32)
    for plane in range(4):
        p = p_of + plane * 8
        hh, first, second = p // 16, p % 4, (p // 4) % 4
        xx = first * (1 - hh) + second * hh
        zz = second * (1 - hh) + first * hh
        pick = (q_of == xx * 8 + zz * 2 + hh).astype(F32)
        scores = scores + dot(fin[plane, 0] + fin[plane, 1], pick, NN, HIGH)
    scores = scores / RLEN
    out[...] = jnp.where(h == 0, scores[0:2, :32], scores[2:4, :32])

    for c in pending:
        c.wait_send()

    def leave(k, carry):
        @pl.when(k < 2)
        def _():
            swap_i(k).wait_send()
            relay(k + 2).wait_send()

        @pl.when(k < 4)
        def _():
            swap_g(k).wait_send()

        for c in far_copies(k) + near_copies(k) + far2_copies(k) + near2_copies(k):
            c.wait_send()
        return carry

    lax.fori_loop(0, PARTS, leave, 0)
    for d in range(1, 4):
        copy(lb.at[h, v], lb.at[h, v], S_L2 + d - 1, dev(0, d)).wait_send()
        copy(a4.at[y], a4.at[y], S_AY + d - 1, dev_y(d)).wait_send()
        copy(gram_s.at[y], gram_r.at[d - 1], S_GRAM + d - 1, dev_y(d)).wait_send()
        copy(left_s.at[y], left_r.at[d - 1], S_LEFT + d - 1, dev_y(d)).wait_send()
        proj_copy(d).wait_send()
        solved_first(d).wait_send()
        solved_second(d).wait_send()
    copy(lb.at[h], lb.at[h], S_LS, sibling).wait_send()
    copy(left_f.at[own_rows], left_f.at[own_rows], S_LEFTS, sibling).wait_send()
    for n, (dy, dh) in enumerate(line):
        copy(damp_1.at[0], damp_1.at[1 + n], S_D1 + n, dev_y(dy, dh)).wait_send()
        copy(fin.at[y, h], fin.at[y, h], S_FIN + n, dev_y(dy, dh)).wait_send()
    for n, (du, dv) in enumerate(others):
        copy(damp_2.at[0], damp_2.at[1 + n], S_D2 + n, dev(du, dv)).wait_send()


def shards(act, grad, lengths, basis_in, basis_out, query_act, query_grad):
    vm = pltpu.VMEM
    anywhere = pl.BlockSpec(memory_space=pl.ANY)
    return pl.pallas_call(
        kernel,
        out_shape=jax.ShapeDtypeStruct((2, 32), F32),
        in_specs=[anywhere, anywhere, pl.BlockSpec(memory_space=pltpu.SMEM)] + [anywhere] * 4,
        out_specs=pl.BlockSpec(memory_space=pltpu.VMEM),
        scratch_shapes=[
            vm((TOK + RANK, DIM), BF),
            vm((TOK + RANK, DIM), BF),
            vm((4, DIM, 256), BF),
            vm((4, DIM, 256), BF),
            vm((2, TOK, 256), BF),
            vm((PARTS, 2 * TOK, 256), BF),
            vm((2 * TOK, WIDTH), BF),
            vm((2, 4, 4, RANK, WIDTH), BF),
            vm((2, 16, 16, 128), BF),
            vm((2, 2, 16, 16, 128), BF),
            vm((16, 2, 2, 16, 128), BF),
            vm((4, 8, 32, 128), BF),
            vm((PARTS, 256, WIDTH), F32),
            vm((PARTS, 256, WIDTH), BF),
            vm((PARTS, 2, 32, WIDTH), BF),
            vm((PARTS, 2, 64, WIDTH), BF),
            vm((PARTS, 4, 16, WIDTH), BF),
            vm((PARTS, 2, 16, 512), BF),
            vm((PARTS, 2, 16, WIDTH), BF),
            vm((PARTS, 16, WIDTH), F32),
            vm((4, 2, RANK, 128), F32),
            vm((3, 2, RANK, 128), F32),
            vm((4, TOK, 256), F32),
            vm((3, TOK, 256), F32),
            vm((2 * TOK, 256), F32),
            vm((8, 8, 128), F32),
            vm((16, 8, 128), F32),
            vm((2, 128, 128), F32),
            vm((4, 2, 128, 128), F32),
            vm((3, 2, 128, 128), F32),
            vm((PARTS, 256, 256), BF),
            vm((4, 2, 8, 256), F32),
            pltpu.SemaphoreType.DMA((12,)),
            pltpu.SemaphoreType.DMA((N_SEM,)),
            pltpu.SemaphoreType.DMA((N_SEM,)),
        ],
        compiler_params=pltpu.CompilerParams(
            collective_id=0, has_side_effects=True, vmem_limit_bytes=60 * 2**20
        ),
    )(act, grad, lengths, basis_in, basis_out, query_act, query_grad)


def solution(mesh):
    return jax.shard_map(
        shards,
        mesh=mesh,
        in_specs=(
            P("dp", None),
            P("dp", None),
            P("dp"),
            P(None, "col"),
            P(None, "col"),
            P("dp", None),
            P("dp", None),
        ),
        out_specs=P("dp", None),
        check_vma=False,
    )
```

```python
import functools

import jax
import jax.numpy as jnp
from jax import lax
from jax.experimental import pallas as pl
from jax.experimental.pallas import tpu as pltpu
from jax.sharding import PartitionSpec as P


RLEN = 128
RANK = 32
DIM = 4096
WIDTH = 1024
TOK = 256
PARTS = 8
damping_share = 0.1
ridge_share = 0.05
epsilon_add = 1e-06
BF = jnp.bfloat16
F32 = jnp.float32
MESH = pl.DeviceIdType.MESH
HIGH = lax.Precision.HIGHEST


def dot(a, b, dims, precision=None):
    return lax.dot_general(a, b, (dims, ((), ())), preferred_element_type=F32, precision=precision)


NN = ((1,), (0,))
TN = ((0,), (0,))
NT = ((1,), (1,))


class Slots:
    def __init__(self):
        self.count = 0

    def take(self, n):
        first = self.count
        self.count += n
        return first


SL = Slots()
S_SWAP_I = SL.take(2)
S_SWAP_A = SL.take(1)
S_SWAP_G = SL.take(1)
S_Y_I = SL.take(6)
S_L1 = SL.take(3)
S_L2 = SL.take(3)
S_LS = SL.take(1)
S_A1 = SL.take(3)
S_A2 = SL.take(3)
S_AY = SL.take(3)
S_FAR = SL.take(2 * PARTS)
S_NEAR = SL.take(2 * PARTS)
S_OUT2 = SL.take(3 * PARTS)
S_GRAM = SL.take(3)
S_LEFT = SL.take(3)
S_LEFTS = SL.take(1)
S_D1 = SL.take(7)
S_D2 = SL.take(3)
S_D3 = SL.take(3)
S_PROJ = SL.take(6)
S_S1 = SL.take(6)
S_S2 = SL.take(6)
S_FIN = SL.take(7)
N_SEM = SL.count


def kernel(
    act, grad, lens, b_in, b_out, q_act, q_grad,
    out,
    xin, xout, bin_, bout, send_i, ibuf, gbuf, lb, at_send, a_own, a_mid, a_recv, a4,
    acc, snd, far, near, snd2, got2, corr,
    gram_s, gram_r, left_s, left_r, left_f, damp_1, damp_2, damp_3, inv_bd, proj_s, proj_r, sb, pick, fin,
    load_sem, ss, rs,
):
    dp = lax.axis_index("dp")
    y = lax.axis_index("col")
    x, z, h = dp // 8, (dp // 2) % 4, dp % 2
    u = x * (1 - h) + z * h
    v = z * (1 - h) + x * h
    me = u * 4 + v

    def dev_xz(xx, zz, hh, yy):
        return ((xx % 4) * 8 + (zz % 4) * 2 + hh, yy % 4)

    def dev(du, dv):
        uu, vv = u + du, v + dv
        return dev_xz(uu * (1 - h) + vv * h, vv * (1 - h) + uu * h, h, y)

    def dev_y(dy, dh=0):
        return dev_xz(x, z, (h + dh) % 2, y + dy)

    sibling = dev_y(0, 1)
    pending = []

    def copy(src, dst, idx, to):
        return pltpu.make_async_remote_copy(
            src_ref=src, dst_ref=dst, send_sem=ss.at[idx], recv_sem=rs.at[idx], device_id=to, device_id_type=MESH
        )

    def send(src, dst, idx, to):
        c = copy(src, dst, idx, to)
        c.start()
        pending.append(c)

    def tile_in(k):
        half = (1 - h) * (1 - k // 2) + h * (k // 2)
        return half * 2 + k % 2

    def load_in(k):
        cols = pl.ds(pl.multiple_of(tile_in(k) * 256, 256), 256)
        return pltpu.make_async_copy(b_in.at[:, cols], bin_.at[k], load_sem.at[4 + k])

    def load_out(k):
        cols = pl.ds(pl.multiple_of(k * 256, 256), 256)
        return pltpu.make_async_copy(b_out.at[:, cols], bout.at[k], load_sem.at[8 + k])

    rows_of = [
        pltpu.make_async_copy(act, xin.at[pl.ds(0, TOK)], load_sem.at[0]),
        pltpu.make_async_copy(q_act, xin.at[pl.ds(TOK, RANK)], load_sem.at[1]),
        pltpu.make_async_copy(grad, xout.at[pl.ds(0, TOK)], load_sem.at[2]),
        pltpu.make_async_copy(q_grad, xout.at[pl.ds(TOK, RANK)], load_sem.at[3]),
    ]
    rows_of[2].start()
    rows_of[3].start()
    for k in range(4):
        load_out(k).start()
    rows_of[0].start()
    rows_of[1].start()
    for k in range(4):
        load_in(k).start()

    line = [(dy, dh) for dy in range(4) for dh in range(2) if dy or dh]
    barrier = pltpu.get_barrier_semaphore()
    peers = [dev(d, 0) for d in range(1, 4)] + [dev(0, d) for d in range(1, 4)] + [dev_y(dy, dh) for dy, dh in line]
    for to in peers:
        pl.semaphore_signal(barrier, inc=1, device_id=to, device_id_type=MESH)

    lane = lax.broadcasted_iota(jnp.int32, (RANK, 128), 1)
    spread = (lane == lax.broadcasted_iota(jnp.int32, (RANK, 128), 0) + RANK * u).astype(BF)

    own_rows = pl.ds(pl.multiple_of(h * TOK, TOK), TOK)

    rows_of[2].wait()
    rows_of[3].wait()
    row = lax.broadcasted_iota(jnp.int32, (TOK, 256), 0)
    live = (row < lens[0]) | ((row >= RLEN) & (row < RLEN + lens[1]))

    def step_out(k, carry):
        load_out(k).wait()
        cols = pl.ds(pl.multiple_of(k * 256, 256), 256)
        r = dot(xout[...], bout[k], NN)
        gbuf[own_rows, cols] = jnp.where(live, r[:TOK], 0.0).astype(BF)
        lb[h, v, u, :, cols] = r[TOK:].astype(BF)
        return carry

    lax.fori_loop(0, 4, step_out, 0)

    rows_of[0].wait()
    rows_of[1].wait()

    def swap_i(k):
        return copy(send_i.at[k], ibuf.at[k, own_rows], S_SWAP_I + k, sibling)

    def step_in(k, carry):
        load_in(k).wait()
        r = dot(xin[...], bin_[k], NN).astype(BF)
        at = dot(r[TOK:], spread, TN).astype(BF).reshape(16, 16, 128)

        @pl.when(k < 2)
        def _():
            send_i[k] = r[:TOK]
            at_send[k] = at

        @pl.when(k >= 2)
        def _():
            ibuf[k - 2, own_rows] = r[:TOK]
            a_own[h, k - 2] = at

        return carry

    lax.fori_loop(0, 2, step_in, 0)
    pl.semaphore_wait(barrier, len(peers))
    for d in range(1, 4):
        part = lb.at[h, v, u]
        send(part, part, S_L1 + d - 1, dev(d, 0))
    for k in range(2):
        pending.append(swap_i(k))
        pending[-1].start()
    send(at_send, a_own.at[h], S_SWAP_A, sibling)
    send(gbuf.at[own_rows], gbuf.at[own_rows], S_SWAP_G, sibling)
    lax.fori_loop(2, 4, step_in, 0)
    for k in range(2):
        swap_i(k).wait_recv()
    send(ibuf.at[0], ibuf.at[2], S_Y_I + 0, dev_y(1))
    send(ibuf.at[1], ibuf.at[3], S_Y_I + 1, dev_y(3))
    send(ibuf.at[1], ibuf.at[4], S_Y_I + 2, dev_y(1))
    send(ibuf.at[0], ibuf.at[5], S_Y_I + 3, dev_y(3))

    copy(at_send, a_own.at[1 - h], S_SWAP_A, sibling).wait_recv()
    for d in range(1, 4):
        there = pl.ds(((u + d) % 4) * 4, 4)
        send(a_own.at[:, :, there], a_mid.at[u], S_A1 + d - 1, dev(d, 0))
    a_mid[u] = a_own[:, :, pl.ds(u * 4, 4)]
    for d in range(1, 4):
        part = lb.at[h, v, u]
        copy(part, part, S_L1 + d - 1, dev(d, 0)).wait_recv()
    for d in range(1, 4):
        send(lb.at[h, v], lb.at[h, v], S_L2 + d - 1, dev(0, d))
    copy(gbuf.at[own_rows], gbuf.at[own_rows], S_SWAP_G, sibling).wait_recv()

    damp_1[0] = jnp.zeros((8, 128), F32)
    group = lax.broadcasted_iota(jnp.int32, (128, 128), 1) // RANK

    def place(i):
        first = (i < 2) * 1
        last = (i >= 6) * 1
        mid = 1 - first - last
        back = 1 - i % 2
        sigma = (y + last * 2 + mid * (back * 3 + (1 - back))) % 4
        k = (first + last) * (i % 2) + mid * ((i == 3) * 1 + (i == 4) * 1)
        return sigma * 2 + k

    def rows64(uu):
        return pl.ds(pl.multiple_of((uu % 4) * 64, 64), 64)

    def far_copies(i):
        over = (u + 2) % 4
        return (
            copy(snd.at[i, pl.ds(pl.multiple_of(over * 64, 64), 32)], far.at[i, 0], S_FAR + 2 * i, dev(1, 0)),
            copy(snd.at[i, pl.ds(pl.multiple_of(over * 64 + 32, 32), 32)], far.at[i, 1], S_FAR + 2 * i + 1, dev(3, 0)),
        )

    def near_copies(i):
        return (
            copy(snd.at[i, rows64(u + 1)], near.at[i, 0], S_NEAR + 2 * i, dev(1, 0)),
            copy(snd.at[i, rows64(u + 3)], near.at[i, 1], S_NEAR + 2 * i + 1, dev(3, 0)),
        )

    def out2_copies(i):
        return [
            copy(snd2.at[i, (v + d) % 4], got2.at[i, d - 1], S_OUT2 + 3 * i + d - 1, dev(0, d)) for d in (2, 1, 3)
        ]

    def relay(i):
        return copy(ibuf.at[i], ibuf.at[i + 4], S_Y_I + i + 2, dev_y(1 + 2 * (i - 2)))

    def stage_squares(i):
        @pl.when(i >= 2)
        def _():
            copy(ibuf.at[i], ibuf.at[i], S_Y_I + i - 2, dev_y(1)).wait_recv()

        @pl.when((i == 2) | (i == 3))
        def _():
            relay(i).start()

        for n in range(4):
            r = dot(ibuf[i, n * RLEN : (n + 1) * RLEN], gbuf[n * RLEN : (n + 1) * RLEN], TN)
            if n == 0:
                acc[i] = r * r
            else:
                acc[i] += r * r
        total = acc[i].reshape(32, 8, WIDTH).sum(axis=0)
        for n in range(WIDTH // 128):
            damp_1[0] += total[:, n * 128 : (n + 1) * 128]
        over = rows64(u + 2)
        snd[i, over] = acc[i, over].astype(BF)
        for c in far_copies(i):
            c.start()

    def stage_near(i):
        for c in far_copies(i):
            c.wait_recv()
        a = pl.multiple_of(((u + 1) % 4) * 64, 64)
        snd[i, pl.ds(a, 32)] = (acc[i, pl.ds(a, 32)] + far[i, 0].astype(F32)).astype(BF)
        snd[i, pl.ds(a + 32, 32)] = acc[i, pl.ds(a + 32, 32)].astype(BF)
        b = pl.multiple_of(((u + 3) % 4) * 64, 64)
        snd[i, pl.ds(b, 32)] = acc[i, pl.ds(b, 32)].astype(BF)
        snd[i, pl.ds(b + 32, 32)] = (acc[i, pl.ds(b + 32, 32)] + far[i, 1].astype(F32)).astype(BF)
        for c in near_copies(i):
            c.start()

    def own16(vv):
        return pl.ds(pl.multiple_of(u * 64 + (vv % 4) * 16, 16), 16)

    def stage_out2(i):
        for c in near_copies(i):
            c.wait_recv()
        mine64 = rows64(u)
        total = acc[i, mine64] + near[i, 0].astype(F32) + near[i, 1].astype(F32)
        acc[i, mine64] = total
        snd2[i] = total.astype(BF).reshape(4, 16, WIDTH)
        for c in out2_copies(i):
            c.start()

    def stage_last(i, carry):
        for c in out2_copies(i):
            c.wait_recv()
        got = got2[i, 0].astype(F32) + got2[i, 1].astype(F32) + got2[i, 2].astype(F32)
        corr[place(i)] = 1.0 / ((acc[i, own16(v)] + got) / 64.0 + damping)
        return carry

    def query_second():
        for d in range(1, 4):
            copy(a_own.at[:, :, pl.ds(0, 4)], a_mid.at[u], S_A1 + d - 1, dev(d, 0)).wait_recv()
        for d in range(1, 4):
            copy(a_mid.at[:, :, :, (v + d) % 4], a_recv.at[v], S_A2 + d - 1, dev(0, d)).start()
        a_recv[v] = a_mid[:, :, :, v]

    def query_third():
        for d in range(1, 4):
            copy(lb.at[h, v], lb.at[h, v], S_L2 + d - 1, dev(0, d)).wait_recv()
        copy(lb.at[h], lb.at[h], S_LS, sibling).start()
        for d in range(1, 4):
            copy(a_mid.at[:, :, :, v], a_recv.at[v], S_A2 + d - 1, dev(0, d)).wait_recv()
        for other in range(2):
            for vv in range(4):
                same = 1 - (other - h) * (other - h)
                total = jnp.zeros((32, 128), F32)
                for uu in range(4):
                    first = same * vv + (1 - same) * uu
                    second = same * uu + (1 - same) * vv
                    total = total + a_recv[first, second, other].reshape(32, 128).astype(F32)
                a4[y, other * 4 + vv] = total.astype(BF)
        for d in range(1, 4):
            copy(a4.at[y], a4.at[y], S_AY + d - 1, dev_y(d)).start()

    def query_products():
        copy(lb.at[h], lb.at[1 - h], S_LS, sibling).wait_recv()

        def one(yy, carry):
            rows = lb[yy // 2, pl.ds((yy % 2) * 2, 2)].reshape(256, WIDTH)
            left_s[yy] = dot(gbuf[own_rows], rows, NT)
            full = dot(rows, rows, NT)
            for e in range(2):
                packed = jnp.zeros((RANK, 128), F32)
                for q in range(4):
                    at = e * 128 + q * RANK
                    packed = packed + jnp.where(lane // RANK == q, full[at : at + RANK, e * 128 : e * 128 + 128], 0.0)
                gram_s[yy, e] = packed
            return carry

        lax.fori_loop(0, 4, one, 0)
        for d in (2, 1, 3):
            there = (y + d) % 4
            copy(gram_s.at[there], gram_r.at[d - 1], S_GRAM + d - 1, dev_y(d)).start()
        for d in (2, 1, 3):
            there = (y + d) % 4
            copy(left_s.at[there], left_r.at[d - 1], S_LEFT + d - 1, dev_y(d)).start()

    def damping_first():
        for n, (dy, dh) in enumerate(line):
            copy(damp_1.at[0], damp_1.at[1 + n], S_D1 + n, dev_y(dy, dh)).start()

    def damping_second():
        for n, (dy, dh) in enumerate(line):
            copy(damp_1.at[0], damp_1.at[1 + n], S_D1 + n, dev_y(dy, dh)).wait_recv()
        damp_2[0] = damp_1[...].sum(axis=0)
        for d in range(1, 4):
            copy(damp_2.at[0], damp_2.at[d], S_D2 + d - 1, dev(d, 0)).start()

    def damping_third():
        for d in range(1, 4):
            copy(damp_2.at[0], damp_2.at[d], S_D2 + d - 1, dev(d, 0)).wait_recv()
        damp_3[0] = damp_2[...].sum(axis=0)
        for d in range(1, 4):
            copy(damp_3.at[0], damp_3.at[d], S_D3 + d - 1, dev(0, d)).start()

    def gram_inverse():
        for d in range(1, 4):
            copy(gram_s.at[y], gram_r.at[d - 1], S_GRAM + d - 1, dev_y(d)).wait_recv()
        gram = gram_s[y] + gram_r[0] + gram_r[1] + gram_r[2]
        lane2 = lax.broadcasted_iota(jnp.int32, (128, 128), 1)
        sub2 = lax.broadcasted_iota(jnp.int32, (128, 128), 0)
        fold = ((sub2 % RANK == lane2) & (lane2 < RANK)).astype(F32)
        block = sub2 // RANK == lane2 // RANK
        wide = []
        for e in range(2):
            tall = jnp.concatenate([gram[e]] * 4, axis=0)
            wide.append(dot(jnp.where(block, tall, 0.0), fold, NN, HIGH).reshape(4, RANK, 128))
        w = jnp.concatenate(wide, axis=0)
        li = lax.broadcasted_iota(jnp.int32, (8, RANK, 128), 2)
        ri = lax.broadcasted_iota(jnp.int32, (8, RANK, 128), 1)
        w = w + jnp.where(li == ri, ridge_share * DIM, 0.0)

        def sweep(k, w):
            at_k = li == k
            col = jnp.where(at_k, w, 0.0).sum(axis=2, keepdims=True)
            rowk = jnp.where(ri == k, w, 0.0).sum(axis=1, keepdims=True)
            pivot = jnp.where(at_k[:, :1], rowk, 0.0).sum(axis=2, keepdims=True)
            rowk = jnp.where(at_k[:, :1], 1.0, rowk) / pivot
            return jnp.where(ri == k, rowk, jnp.where(at_k, 0.0, w) - col * rowk)

        w = lax.fori_loop(0, RANK, sweep, w)
        for e in range(2):
            flat = w[e * 4 : (e + 1) * 4].reshape(128, 128)
            inv_bd[e] = jnp.where(block, dot(flat, fold, NT, HIGH), 0.0)

    def left_sum():
        for d in range(1, 4):
            copy(left_s.at[y], left_r.at[d - 1], S_LEFT + d - 1, dev_y(d)).wait_recv()
        left_f[own_rows] = left_s[y] + left_r[0] + left_r[1] + left_r[2]
        copy(left_f.at[own_rows], left_f.at[own_rows], S_LEFTS, sibling).start()

    def selection():
        p = lax.broadcasted_iota(jnp.int32, (256, 128), 0) // RANK + y * 8
        hh, first, second = p // 16, p % 4, (p // 4) % 4
        xx = first * (1 - hh) + second * hh
        zz = second * (1 - hh) + first * hh
        pick[...] = (lax.broadcasted_iota(jnp.int32, (256, 128), 1) == xx * 8 + zz * 2 + hh).astype(F32)

    def step(i, carry):
        @pl.when(i < PARTS)
        def _():
            stage_squares(i)

        @pl.when((i >= 2) & (i < PARTS + 2))
        def _():
            stage_near(i - 2)

        @pl.when(i >= 4)
        def _():
            stage_out2(i - 4)

        pl.when(i == 1)(query_second)
        pl.when(i == 3)(query_third)
        pl.when(i == 5)(query_products)
        pl.when(i == 7)(damping_first)
        pl.when(i == 8)(damping_second)

        @pl.when(i == 9)
        def _():
            damping_third()
            gram_inverse()

        @pl.when(i == 10)
        def _():
            left_sum()
            selection()

        return carry

    lax.fori_loop(0, PARTS + 4, step, 0)

    for d in range(1, 4):
        copy(damp_3.at[0], damp_3.at[d], S_D3 + d - 1, dev(0, d)).wait_recv()
    damping = damping_share * (jnp.sum(damp_3[...]) / 64.0 / (DIM * DIM)) + epsilon_add
    for d in range(1, 4):
        copy(a4.at[y], a4.at[y], S_AY + d - 1, dev_y(d)).wait_recv()
    lax.fori_loop(0, PARTS, stage_last, 0)

    def proj_copy(e, d):
        there = (y + d) % 4
        return copy(proj_s.at[there, e], proj_r.at[d - 1, e], S_PROJ + 3 * e + d - 1, dev_y(d))

    def solve_group(n, carry):
        e, m = n // 4, n % 4
        d = (m == 0) * 2 + (m == 1) * 1 + (m == 2) * 3
        there = (y + d) % 4
        g = there * 2 + e
        a = a4[:, g].reshape(128, 128)
        a_all = jnp.concatenate([jnp.where(group == q, a, jnp.zeros_like(a)) for q in range(4)], axis=0)
        rows = lb[g // 4, g % 4].reshape(128, WIDTH)
        rotated = dot(a_all, rows, NN)
        weight = corr[...].reshape(1, 128, WIDTH)
        scaled = (rotated.reshape(4, 128, WIDTH) * weight).reshape(512, WIDTH).astype(BF)
        p = dot(scaled, rows, NT)
        packed = jnp.zeros((128, 128), F32)
        for q in range(4):
            packed = packed + jnp.where(group == q, p[q * 128 : (q + 1) * 128], 0.0)
        proj_s[there, e] = packed

        @pl.when(m < 3)
        def _():
            proj_copy(e, d).start()

        return carry

    lax.fori_loop(0, 8, solve_group, 0)

    mine = pl.ds(pl.multiple_of(me * 16, 16), 16)

    def solved_first(e, d):
        return copy(sb.at[e, :, mine], sb.at[e, :, mine], S_S1 + 3 * e + d - 1, dev(0, d))

    def solved_second(e, d):
        part = sb.at[e, :, pl.ds(pl.multiple_of(u * 64, 64), 64)]
        return copy(part, part, S_S2 + 3 * e + d - 1, dev(d, 0))

    for e in range(2):
        for d in range(1, 4):
            proj_copy(e, d).wait_recv()
        whole = proj_s[y, e] + proj_r[0, e] + proj_r[1, e] + proj_r[2, e]
        solved = dot(whole, inv_bd[e], NN, HIGH).astype(BF)
        sb[e, :, mine] = solved.reshape(PARTS, 16, 128)
        for d in (2, 1, 3):
            solved_first(e, d).start()
    for e in range(2):
        for d in range(1, 4):
            solved_first(e, d).wait_recv()
        for d in (2, 1, 3):
            solved_second(e, d).start()
    copy(left_f.at[own_rows], left_f.at[own_rows], S_LEFTS, sibling).wait_recv()

    for c in pending:
        c.wait_send()

    def leave(k, carry):
        @pl.when(k < 2)
        def _():
            relay(k + 2).wait_send()

        for c in far_copies(k) + near_copies(k):
            c.wait_send()
        for c in out2_copies(k):
            c.wait_send()
        return carry

    lax.fori_loop(0, PARTS, leave, 0)
    for d in range(1, 4):
        copy(a_mid.at[:, :, :, (v + d) % 4], a_recv.at[v], S_A2 + d - 1, dev(0, d)).wait_send()
        copy(a4.at[y], a4.at[y], S_AY + d - 1, dev_y(d)).wait_send()
        copy(gram_s.at[y], gram_r.at[d - 1], S_GRAM + d - 1, dev_y(d)).wait_send()
        copy(left_s.at[y], left_r.at[d - 1], S_LEFT + d - 1, dev_y(d)).wait_send()
        copy(damp_2.at[0], damp_2.at[d], S_D2 + d - 1, dev(d, 0)).wait_send()
        copy(damp_3.at[0], damp_3.at[d], S_D3 + d - 1, dev(0, d)).wait_send()
        for e in range(2):
            proj_copy(e, d).wait_send()
            solved_first(e, d).wait_send()
    copy(lb.at[h], lb.at[h], S_LS, sibling).wait_send()
    copy(left_f.at[own_rows], left_f.at[own_rows], S_LEFTS, sibling).wait_send()
    for n, (dy, dh) in enumerate(line):
        copy(damp_1.at[0], damp_1.at[1 + n], S_D1 + n, dev_y(dy, dh)).wait_send()

    joined = []
    for e in range(2):
        for d in range(1, 4):
            solved_second(e, d).wait_recv()

        def right_part(i, total, e=e):
            return total + dot(ibuf[i], sb[e, place(i)], NN)

        right = lax.fori_loop(0, PARTS, right_part, jnp.zeros((2 * TOK, 128), F32))
        joined.append((left_f[:, e * 128 : (e + 1) * 128] * right).reshape(4, RLEN, 128).sum(axis=1))
    joined = jnp.concatenate([jnp.concatenate(joined, axis=1), jnp.zeros((4, 256), F32)], axis=0)
    fin[y, h] = dot(joined, pick[...], NN, HIGH)
    for n, (dy, dh) in enumerate(line):
        copy(fin.at[y, h], fin.at[y, h], S_FIN + n, dev_y(dy, dh)).start()
    for n, (dy, dh) in enumerate(line):
        copy(fin.at[y, h], fin.at[y, h], S_FIN + n, dev_y(dy, dh)).wait_recv()
    scores = fin[...].reshape(8, 8, 128).sum(axis=0) / RLEN
    out[...] = jnp.where(h == 0, scores[0:2, :32], scores[2:4, :32])
    for e in range(2):
        for d in range(1, 4):
            solved_second(e, d).wait_send()
    for n, (dy, dh) in enumerate(line):
        copy(fin.at[y, h], fin.at[y, h], S_FIN + n, dev_y(dy, dh)).wait_send()


def shards(act, grad, lengths, basis_in, basis_out, query_act, query_grad):
    vm = pltpu.VMEM
    anywhere = pl.BlockSpec(memory_space=pl.ANY)
    return pl.pallas_call(
        kernel,
        out_shape=jax.ShapeDtypeStruct((2, 32), F32),
        in_specs=[anywhere, anywhere, pl.BlockSpec(memory_space=pltpu.SMEM)] + [anywhere] * 4,
        out_specs=pl.BlockSpec(memory_space=pltpu.VMEM),
        scratch_shapes=[
            vm((TOK + RANK, DIM), BF),
            vm((TOK + RANK, DIM), BF),
            vm((4, DIM, 256), BF),
            vm((4, DIM, 256), BF),
            vm((2, TOK, 256), BF),
            vm((PARTS, 2 * TOK, 256), BF),
            vm((2 * TOK, WIDTH), BF),
            vm((2, 4, 4, RANK, WIDTH), BF),
            vm((2, 16, 16, 128), BF),
            vm((2, 2, 16, 16, 128), BF),
            vm((4, 2, 2, 4, 16, 128), BF),
            vm((4, 4, 2, 2, 16, 128), BF),
            vm((4, 8, 32, 128), BF),
            vm((PARTS, 256, WIDTH), F32),
            vm((PARTS, 256, WIDTH), BF),
            vm((PARTS, 2, 32, WIDTH), BF),
            vm((PARTS, 2, 64, WIDTH), BF),
            vm((PARTS, 4, 16, WIDTH), BF),
            vm((PARTS, 3, 16, WIDTH), BF),
            vm((PARTS, 16, WIDTH), F32),
            vm((4, 2, RANK, 128), F32),
            vm((3, 2, RANK, 128), F32),
            vm((4, TOK, 256), F32),
            vm((3, TOK, 256), F32),
            vm((2 * TOK, 256), F32),
            vm((8, 8, 128), F32),
            vm((4, 8, 128), F32),
            vm((4, 8, 128), F32),
            vm((2, 128, 128), F32),
            vm((4, 2, 128, 128), F32),
            vm((3, 2, 128, 128), F32),
            vm((2, PARTS, 256, 128), BF),
            vm((256, 128), F32),
            vm((4, 2, 8, 128), F32),
            pltpu.SemaphoreType.DMA((12,)),
            pltpu.SemaphoreType.DMA((N_SEM,)),
            pltpu.SemaphoreType.DMA((N_SEM,)),
        ],
        compiler_params=pltpu.CompilerParams(
            collective_id=0, has_side_effects=True, vmem_limit_bytes=60 * 2**20
        ),
    )(act, grad, lengths, basis_in, basis_out, query_act, query_grad)


def solution(mesh):
    return jax.shard_map(
        shards,
        mesh=mesh,
        in_specs=(
            P("dp", None),
            P("dp", None),
            P("dp"),
            P(None, "col"),
            P(None, "col"),
            P("dp", None),
            P("dp", None),
        ),
        out_specs=P("dp", None),
        check_vma=False,
    )
```

```python
import functools

import jax
import jax.numpy as jnp
from jax import lax
from jax.experimental import pallas as pl
from jax.experimental.pallas import tpu as pltpu
from jax.sharding import PartitionSpec as P


RLEN = 128
RANK = 32
DIM = 4096
WIDTH = 1024
TOK = 256
RING = 5
PARTS = 8
damping_share = 0.1
ridge_share = 0.05
epsilon_add = 1e-06
BF = jnp.bfloat16
F32 = jnp.float32
MESH = pl.DeviceIdType.MESH
HIGH = lax.Precision.HIGHEST


def dot(a, b, dims, precision=None):
    return lax.dot_general(a, b, (dims, ((), ())), preferred_element_type=F32, precision=precision)


NN = ((1,), (0,))
TN = ((0,), (0,))
NT = ((1,), (1,))


class Slots:
    def __init__(self):
        self.count = 0

    def take(self, n):
        first = self.count
        self.count += n
        return first


SL = Slots()
S_SWAP_I = SL.take(2)
S_SWAP_A = SL.take(1)
S_SWAP_G = SL.take(1)
S_Y_I = SL.take(6)
S_L1 = SL.take(3)
S_L2 = SL.take(3)
S_LS = SL.take(1)
S_A1 = SL.take(3)
S_A2 = SL.take(3)
S_AY = SL.take(3)
S_FAR = SL.take(2 * PARTS)
S_NEAR = SL.take(2 * PARTS)
S_OUT2 = SL.take(3 * PARTS)
S_GRAM = SL.take(3)
S_LEFT = SL.take(3)
S_LEFTS = SL.take(1)
S_D1 = SL.take(7)
S_D2 = SL.take(3)
S_D3 = SL.take(3)
S_PROJ = SL.take(6)
S_S1 = SL.take(6)
S_S2 = SL.take(6)
S_FIN = SL.take(7)
N_SEM = SL.count


def kernel(
    act, grad, lens, b_in, b_out, q_act, q_grad,
    out,
    xin, xout, basis, send_i, ibuf, gbuf, lb, at_send, a_own, a_mid, a_recv, a4,
    acc, snd, far, near, snd2, got2, corr,
    gram_s, gram_r, left_s, left_r, left_f, damp_1, damp_2, damp_3, inv_w, inv_bd, rotated, proj_s, proj_r, sb, pick, fin,
    load_sem, ss, rs,
):
    dp = lax.axis_index("dp")
    y = lax.axis_index("col")
    x, z, h = dp // 8, (dp // 2) % 4, dp % 2
    u = x * (1 - h) + z * h
    v = z * (1 - h) + x * h
    me = u * 4 + v

    def dev_xz(xx, zz, hh, yy):
        return ((xx % 4) * 8 + (zz % 4) * 2 + hh, yy % 4)

    def dev(du, dv):
        uu, vv = u + du, v + dv
        return dev_xz(uu * (1 - h) + vv * h, vv * (1 - h) + uu * h, h, y)

    def dev_y(dy, dh=0):
        return dev_xz(x, z, (h + dh) % 2, y + dy)

    sibling = dev_y(0, 1)
    pending = []

    def copy(src, dst, idx, to):
        return pltpu.make_async_remote_copy(
            src_ref=src, dst_ref=dst, send_sem=ss.at[idx], recv_sem=rs.at[idx], device_id=to, device_id_type=MESH
        )

    def send(src, dst, idx, to):
        c = copy(src, dst, idx, to)
        c.start()
        pending.append(c)

    def tile_in(k):
        half = (1 - h) * (1 - k // 2) + h * (k // 2)
        return half * 2 + k % 2

    def load_in(k):
        cols = pl.ds(pl.multiple_of(tile_in(k) * 256, 256), 256)
        return pltpu.make_async_copy(b_in.at[:, cols], basis.at[k], load_sem.at[4 + k])

    def load_out(k):
        cols = pl.ds(pl.multiple_of(k * 256, 256), 256)
        return pltpu.make_async_copy(b_out.at[:, cols], basis.at[k], load_sem.at[8 + k])

    rows_of = [
        pltpu.make_async_copy(act, xin.at[pl.ds(0, TOK)], load_sem.at[0]),
        pltpu.make_async_copy(q_act, xin.at[pl.ds(TOK, RANK)], load_sem.at[1]),
        pltpu.make_async_copy(grad, xout.at[pl.ds(0, TOK)], load_sem.at[2]),
        pltpu.make_async_copy(q_grad, xout.at[pl.ds(TOK, RANK)], load_sem.at[3]),
    ]
    rows_of[2].start()
    rows_of[3].start()
    for k in range(4):
        load_out(k).start()
    rows_of[0].start()
    rows_of[1].start()

    line = [(dy, dh) for dy in range(4) for dh in range(2) if dy or dh]
    barrier = pltpu.get_barrier_semaphore()
    peers = [dev(d, 0) for d in range(1, 4)] + [dev(0, d) for d in range(1, 4)] + [dev_y(dy, dh) for dy, dh in line]
    for to in peers:
        pl.semaphore_signal(barrier, inc=1, device_id=to, device_id_type=MESH)

    lane = lax.broadcasted_iota(jnp.int32, (RANK, 128), 1)
    spread = (lane == lax.broadcasted_iota(jnp.int32, (RANK, 128), 0) + RANK * u).astype(BF)

    own_rows = pl.ds(pl.multiple_of(h * TOK, TOK), TOK)

    rows_of[2].wait()
    rows_of[3].wait()
    row = lax.broadcasted_iota(jnp.int32, (TOK, 256), 0)
    live = (row < lens[0]) | ((row >= RLEN) & (row < RLEN + lens[1]))

    def step_out(k, carry):
        load_out(k).wait()
        cols = pl.ds(pl.multiple_of(k * 256, 256), 256)
        r = dot(xout[...], basis[k], NN)
        gbuf[own_rows, cols] = jnp.where(live, r[:TOK], 0.0).astype(BF)
        lb[h, v, u, :, cols] = r[TOK:].astype(BF)
        load_in(k).start()
        return carry

    lax.fori_loop(0, 4, step_out, 0)
    pl.semaphore_wait(barrier, len(peers))
    for d in range(1, 4):
        part = lb.at[h, v, u]
        send(part, part, S_L1 + d - 1, dev(d, 0))
    send(gbuf.at[own_rows], gbuf.at[own_rows], S_SWAP_G, sibling)

    rows_of[0].wait()
    rows_of[1].wait()

    def swap_i(k):
        return copy(send_i.at[k], ibuf.at[k, own_rows], S_SWAP_I + k, sibling)

    def step_in(k, carry):
        load_in(k).wait()
        r = dot(xin[...], basis[k], NN).astype(BF)
        at = dot(r[TOK:], spread, TN).astype(BF).reshape(16, 16, 128)

        @pl.when(k < 2)
        def _():
            send_i[k] = r[:TOK]
            at_send[k] = at

        @pl.when(k >= 2)
        def _():
            ibuf[k - 2, own_rows] = r[:TOK]
            a_own[h, k - 2] = at

        return carry

    lax.fori_loop(0, 2, step_in, 0)
    for k in range(2):
        pending.append(swap_i(k))
        pending[-1].start()
    send(at_send, a_own.at[h], S_SWAP_A, sibling)
    lax.fori_loop(2, 4, step_in, 0)
    for d in range(1, 4):
        part = lb.at[h, v, u]
        copy(part, part, S_L1 + d - 1, dev(d, 0)).wait_recv()
    for d in range(1, 4):
        send(lb.at[h, v], lb.at[h, v], S_L2 + d - 1, dev(0, d))
    for k in range(2):
        swap_i(k).wait_recv()
    send(ibuf.at[0], ibuf.at[2], S_Y_I + 0, dev_y(1))
    send(ibuf.at[1], ibuf.at[3], S_Y_I + 1, dev_y(3))
    send(ibuf.at[1], ibuf.at[4], S_Y_I + 2, dev_y(1))
    send(ibuf.at[0], ibuf.at[5], S_Y_I + 3, dev_y(3))

    copy(at_send, a_own.at[1 - h], S_SWAP_A, sibling).wait_recv()
    for d in range(1, 4):
        there = pl.ds(((u + d) % 4) * 4, 4)
        send(a_own.at[:, :, there], a_mid.at[u], S_A1 + d - 1, dev(d, 0))
    a_mid[u] = a_own[:, :, pl.ds(u * 4, 4)]
    copy(gbuf.at[own_rows], gbuf.at[own_rows], S_SWAP_G, sibling).wait_recv()

    damp_1[0] = jnp.zeros((8, 128), F32)
    group = lax.broadcasted_iota(jnp.int32, (128, 128), 1) // RANK

    def place(i):
        first = (i < 2) * 1
        last = (i >= 6) * 1
        mid = 1 - first - last
        back = 1 - i % 2
        sigma = (y + last * 2 + mid * (back * 3 + (1 - back))) % 4
        k = (first + last) * (i % 2) + mid * ((i == 3) * 1 + (i == 4) * 1)
        return sigma * 2 + k

    def rows64(uu):
        return pl.ds(pl.multiple_of((uu % 4) * 64, 64), 64)

    def far_copies(i):
        over = (u + 2) % 4
        return (
            copy(snd.at[i, pl.ds(pl.multiple_of(over * 64, 64), 32)], far.at[i, 0], S_FAR + 2 * i, dev(1, 0)),
            copy(snd.at[i, pl.ds(pl.multiple_of(over * 64 + 32, 32), 32)], far.at[i, 1], S_FAR + 2 * i + 1, dev(3, 0)),
        )

    def near_copies(i):
        return (
            copy(snd.at[i, rows64(u + 1)], near.at[i, 0], S_NEAR + 2 * i, dev(1, 0)),
            copy(snd.at[i, rows64(u + 3)], near.at[i, 1], S_NEAR + 2 * i + 1, dev(3, 0)),
        )

    def out2_copies(i):
        return [
            copy(snd2.at[i, (v + d) % 4], got2.at[i, d - 1], S_OUT2 + 3 * i + d - 1, dev(0, d)) for d in (2, 1, 3)
        ]

    def relay(i):
        return copy(ibuf.at[i], ibuf.at[i + 4], S_Y_I + i + 2, dev_y(1 + 2 * (i - 2)))

    def stage_squares(i):
        @pl.when(i >= 2)
        def _():
            copy(ibuf.at[i], ibuf.at[i], S_Y_I + i - 2, dev_y(1)).wait_recv()

        @pl.when((i == 2) | (i == 3))
        def _():
            relay(i).start()

        for n in range(4):
            r = dot(ibuf[i, n * RLEN : (n + 1) * RLEN], gbuf[n * RLEN : (n + 1) * RLEN], TN)
            if n == 0:
                acc[i % RING] = r * r
            else:
                acc[i % RING] += r * r
        total = acc[i % RING].reshape(32, 8, WIDTH).sum(axis=0)
        for n in range(WIDTH // 128):
            damp_1[0] += total[:, n * 128 : (n + 1) * 128]
        over = rows64(u + 2)
        snd[i, over] = acc[i % RING, over].astype(BF)
        for c in far_copies(i):
            c.start()

    def stage_near(i):
        for c in far_copies(i):
            c.wait_recv()
        a = pl.multiple_of(((u + 1) % 4) * 64, 64)
        snd[i, pl.ds(a, 32)] = (acc[i % RING, pl.ds(a, 32)] + far[i, 0].astype(F32)).astype(BF)
        snd[i, pl.ds(a + 32, 32)] = acc[i % RING, pl.ds(a + 32, 32)].astype(BF)
        b = pl.multiple_of(((u + 3) % 4) * 64, 64)
        snd[i, pl.ds(b, 32)] = acc[i % RING, pl.ds(b, 32)].astype(BF)
        snd[i, pl.ds(b + 32, 32)] = (acc[i % RING, pl.ds(b + 32, 32)] + far[i, 1].astype(F32)).astype(BF)
        for c in near_copies(i):
            c.start()

    def own16(vv):
        return pl.ds(pl.multiple_of(u * 64 + (vv % 4) * 16, 16), 16)

    def stage_out2(i):
        for c in near_copies(i):
            c.wait_recv()
        mine64 = rows64(u)
        total = acc[i % RING, mine64] + near[i, 0].astype(F32) + near[i, 1].astype(F32)
        acc[i % RING, mine64] = total
        corr[place(i)] = acc[i % RING, own16(v)]
        snd2[i] = total.astype(BF).reshape(4, 16, WIDTH)
        for c in out2_copies(i):
            c.start()

    def stage_last(i, carry):
        for c in out2_copies(i):
            c.wait_recv()
        got = got2[i, 0].astype(F32) + got2[i, 1].astype(F32) + got2[i, 2].astype(F32)
        corr[place(i)] = 1.0 / ((corr[place(i)] + got) / 64.0 + damping)
        return carry

    def query_second():
        for d in range(1, 4):
            copy(a_own.at[:, :, pl.ds(0, 4)], a_mid.at[u], S_A1 + d - 1, dev(d, 0)).wait_recv()
        for d in range(1, 4):
            copy(a_mid.at[:, :, :, (v + d) % 4], a_recv.at[v], S_A2 + d - 1, dev(0, d)).start()
        a_recv[v] = a_mid[:, :, :, v]

    def query_third():
        for d in range(1, 4):
            copy(lb.at[h, v], lb.at[h, v], S_L2 + d - 1, dev(0, d)).wait_recv()
        copy(lb.at[h], lb.at[h], S_LS, sibling).start()
        for d in range(1, 4):
            copy(a_mid.at[:, :, :, v], a_recv.at[v], S_A2 + d - 1, dev(0, d)).wait_recv()
        for other in range(2):
            for vv in range(4):
                same = 1 - (other - h) * (other - h)
                total = jnp.zeros((32, 128), F32)
                for uu in range(4):
                    first = same * vv + (1 - same) * uu
                    second = same * uu + (1 - same) * vv
                    total = total + a_recv[first, second, other].reshape(32, 128).astype(F32)
                a4[y, other * 4 + vv] = total.astype(BF)
        for d in range(1, 4):
            copy(a4.at[y], a4.at[y], S_AY + d - 1, dev_y(d)).start()

    def plane_rows(yy):
        return lb[yy // 2, pl.ds((yy % 2) * 2, 2)].reshape(256, WIDTH)

    def gram_products():
        copy(lb.at[h], lb.at[1 - h], S_LS, sibling).wait_recv()

        def one(yy, carry):
            rows = plane_rows(yy)
            full = dot(rows, rows, NT)
            for e in range(2):
                packed = jnp.zeros((RANK, 128), F32)
                for q in range(4):
                    at = e * 128 + q * RANK
                    packed = packed + jnp.where(lane // RANK == q, full[at : at + RANK, e * 128 : e * 128 + 128], 0.0)
                gram_s[yy, e] = packed
            return carry

        lax.fori_loop(0, 4, one, 0)
        for d in (2, 1, 3):
            there = (y + d) % 4
            copy(gram_s.at[there], gram_r.at[d - 1], S_GRAM + d - 1, dev_y(d)).start()

    def left_products():
        def one(yy, carry):
            left_s[yy] = dot(gbuf[own_rows], plane_rows(yy), NT)
            return carry

        lax.fori_loop(0, 4, one, 0)
        for d in (2, 1, 3):
            there = (y + d) % 4
            copy(left_s.at[there], left_r.at[d - 1], S_LEFT + d - 1, dev_y(d)).start()

    def rotate(g):
        a = a4[:, g].reshape(128, 128)
        a_all = jnp.concatenate([jnp.where(group == q, a, jnp.zeros_like(a)) for q in range(4)], axis=0)
        rotated[g] = dot(a_all, lb[g // 4, g % 4].reshape(128, WIDTH), NN)

    def damping_first():
        for n, (dy, dh) in enumerate(line):
            copy(damp_1.at[0], damp_1.at[1 + n], S_D1 + n, dev_y(dy, dh)).start()

    def damping_second():
        for n, (dy, dh) in enumerate(line):
            copy(damp_1.at[0], damp_1.at[1 + n], S_D1 + n, dev_y(dy, dh)).wait_recv()
        damp_2[0] = damp_1[...].sum(axis=0)
        for d in range(1, 4):
            copy(damp_2.at[0], damp_2.at[d], S_D2 + d - 1, dev(d, 0)).start()

    def damping_third():
        for d in range(1, 4):
            copy(damp_2.at[0], damp_2.at[d], S_D2 + d - 1, dev(d, 0)).wait_recv()
        damp_3[0] = damp_2[...].sum(axis=0)
        for d in range(1, 4):
            copy(damp_3.at[0], damp_3.at[d], S_D3 + d - 1, dev(0, d)).start()

    lane2 = lax.broadcasted_iota(jnp.int32, (128, 128), 1)
    sub2 = lax.broadcasted_iota(jnp.int32, (128, 128), 0)

    def fold_block():
        fold = ((sub2 % RANK == lane2) & (lane2 < RANK)).astype(F32)
        return fold, sub2 // RANK == lane2 // RANK

    def gram_begin():
        for d in range(1, 4):
            copy(gram_s.at[y], gram_r.at[d - 1], S_GRAM + d - 1, dev_y(d)).wait_recv()
        gram = gram_s[y] + gram_r[0] + gram_r[1] + gram_r[2]
        fold, block = fold_block()
        wide = []
        for e in range(2):
            tall = jnp.concatenate([gram[e]] * 4, axis=0)
            wide.append(dot(jnp.where(block, tall, 0.0), fold, NN, HIGH).reshape(4, RANK, 128))
        w = jnp.concatenate(wide, axis=0)
        li = lax.broadcasted_iota(jnp.int32, (8, RANK, 128), 2)
        ri = lax.broadcasted_iota(jnp.int32, (8, RANK, 128), 1)
        inv_w[...] = w + jnp.where(li == ri, ridge_share * DIM, 0.0)

    def gram_sweep(first):
        li = lax.broadcasted_iota(jnp.int32, (8, RANK, 128), 2)
        ri = lax.broadcasted_iota(jnp.int32, (8, RANK, 128), 1)

        def sweep(k, w):
            at_k = li == k
            col = jnp.where(at_k, w, 0.0).sum(axis=2, keepdims=True)
            rowk = jnp.where(ri == k, w, 0.0).sum(axis=1, keepdims=True)
            pivot = jnp.where(at_k[:, :1], rowk, 0.0).sum(axis=2, keepdims=True)
            rowk = jnp.where(at_k[:, :1], 1.0, rowk) / pivot
            return jnp.where(ri == k, rowk, jnp.where(at_k, 0.0, w) - col * rowk)

        inv_w[...] = lax.fori_loop(first, first + 8, sweep, inv_w[...])

    def gram_end():
        fold, block = fold_block()
        for e in range(2):
            flat = inv_w[e * 4 : (e + 1) * 4].reshape(128, 128)
            inv_bd[e] = jnp.where(block, dot(flat, fold, NT, HIGH), 0.0)

    def left_sum():
        for d in range(1, 4):
            copy(left_s.at[y], left_r.at[d - 1], S_LEFT + d - 1, dev_y(d)).wait_recv()
        left_f[own_rows] = left_s[y] + left_r[0] + left_r[1] + left_r[2]
        copy(left_f.at[own_rows], left_f.at[own_rows], S_LEFTS, sibling).start()

    def selection():
        p = lax.broadcasted_iota(jnp.int32, (256, 128), 0) // RANK + y * 8
        hh, first, second = p // 16, p % 4, (p // 4) % 4
        xx = first * (1 - hh) + second * hh
        zz = second * (1 - hh) + first * hh
        pick[...] = (lax.broadcasted_iota(jnp.int32, (256, 128), 1) == xx * 8 + zz * 2 + hh).astype(F32)

    def step(i, carry):
        @pl.when((i >= 2) & (i < PARTS + 2))
        def _():
            stage_near(i - 2)

        @pl.when(i >= 4)
        def _():
            stage_out2(i - 4)

        @pl.when(i < PARTS)
        def _():
            stage_squares(i)

        pl.when(i == 1)(query_second)
        pl.when(i == 3)(query_third)
        pl.when(i == 5)(gram_products)
        pl.when(i == 6)(left_products)
        pl.when(i == 7)(damping_first)
        pl.when(i == 7)(gram_begin)

        @pl.when((i >= 7) & (i < 11))
        def _():
            gram_sweep((i - 7) * 8)

        pl.when(i == 8)(damping_second)
        pl.when(i == 9)(damping_third)

        @pl.when(i == 7)
        def _():
            for d in range(1, 4):
                copy(a4.at[y], a4.at[y], S_AY + d - 1, dev_y(d)).wait_recv()

        @pl.when((i >= 7) & (i < 11))
        def _():
            rotate((i - 7) * 2)
            rotate((i - 7) * 2 + 1)

        @pl.when(i == 11)
        def _():
            gram_end()
            selection()

        return carry

    lax.fori_loop(0, PARTS + 4, step, 0)

    for d in range(1, 4):
        copy(damp_3.at[0], damp_3.at[d], S_D3 + d - 1, dev(0, d)).wait_recv()
    damping = damping_share * (jnp.sum(damp_3[...]) / 64.0 / (DIM * DIM)) + epsilon_add
    lax.fori_loop(0, PARTS, stage_last, 0)

    def proj_copy(e, d):
        there = (y + d) % 4
        return copy(proj_s.at[there, e], proj_r.at[d - 1, e], S_PROJ + 3 * e + d - 1, dev_y(d))

    def solve_group(n, carry):
        e, m = n // 4, n % 4
        d = (m == 0) * 2 + (m == 1) * 1 + (m == 2) * 3
        there = (y + d) % 4
        g = there * 2 + e
        rows = lb[g // 4, g % 4].reshape(128, WIDTH)
        weight = corr[...].reshape(1, 128, WIDTH)
        scaled = (rotated[g].reshape(4, 128, WIDTH) * weight).reshape(512, WIDTH).astype(BF)
        p = dot(scaled, rows, NT)
        packed = jnp.zeros((128, 128), F32)
        for q in range(4):
            packed = packed + jnp.where(group == q, p[q * 128 : (q + 1) * 128], 0.0)
        proj_s[there, e] = packed

        @pl.when(m < 3)
        def _():
            proj_copy(e, d).start()

        return carry

    lax.fori_loop(0, 8, solve_group, 0)
    left_sum()

    mine = pl.ds(pl.multiple_of(me * 16, 16), 16)

    def solved_first(e, d):
        return copy(sb.at[e, :, mine], sb.at[e, :, mine], S_S1 + 3 * e + d - 1, dev(0, d))

    def solved_second(e, d):
        part = sb.at[e, :, pl.ds(pl.multiple_of(u * 64, 64), 64)]
        return copy(part, part, S_S2 + 3 * e + d - 1, dev(d, 0))

    for e in range(2):
        for d in range(1, 4):
            proj_copy(e, d).wait_recv()
        whole = proj_s[y, e] + proj_r[0, e] + proj_r[1, e] + proj_r[2, e]
        solved = dot(whole, inv_bd[e], NN, HIGH).astype(BF)
        sb[e, :, mine] = solved.reshape(PARTS, 16, 128)
        for d in (2, 1, 3):
            solved_first(e, d).start()
    for e in range(2):
        for d in range(1, 4):
            solved_first(e, d).wait_recv()
        for d in (2, 1, 3):
            solved_second(e, d).start()

    for c in pending:
        c.wait_send()

    def leave(k, carry):
        @pl.when(k < 2)
        def _():
            relay(k + 2).wait_send()

        for c in far_copies(k) + near_copies(k):
            c.wait_send()
        for c in out2_copies(k):
            c.wait_send()
        return carry

    lax.fori_loop(0, PARTS, leave, 0)
    for d in range(1, 4):
        copy(a_mid.at[:, :, :, (v + d) % 4], a_recv.at[v], S_A2 + d - 1, dev(0, d)).wait_send()
        copy(a4.at[y], a4.at[y], S_AY + d - 1, dev_y(d)).wait_send()
        copy(gram_s.at[y], gram_r.at[d - 1], S_GRAM + d - 1, dev_y(d)).wait_send()
        copy(left_s.at[y], left_r.at[d - 1], S_LEFT + d - 1, dev_y(d)).wait_send()
        copy(damp_2.at[0], damp_2.at[d], S_D2 + d - 1, dev(d, 0)).wait_send()
        copy(damp_3.at[0], damp_3.at[d], S_D3 + d - 1, dev(0, d)).wait_send()
        for e in range(2):
            proj_copy(e, d).wait_send()
            solved_first(e, d).wait_send()
    copy(lb.at[h], lb.at[h], S_LS, sibling).wait_send()
    copy(left_f.at[own_rows], left_f.at[own_rows], S_LEFTS, sibling).wait_send()
    for n, (dy, dh) in enumerate(line):
        copy(damp_1.at[0], damp_1.at[1 + n], S_D1 + n, dev_y(dy, dh)).wait_send()

    copy(left_f.at[own_rows], left_f.at[own_rows], S_LEFTS, sibling).wait_recv()
    joined = []
    for e in range(2):
        for d in range(1, 4):
            solved_second(e, d).wait_recv()

        right = jnp.zeros((2 * TOK, 128), F32)
        for i in range(PARTS):
            right = right + dot(ibuf[i], sb[e, place(i)], NN)
        joined.append((left_f[:, e * 128 : (e + 1) * 128] * right).reshape(4, RLEN, 128).sum(axis=1))
    joined = jnp.concatenate([jnp.concatenate(joined, axis=1), jnp.zeros((4, 256), F32)], axis=0)
    fin[y, h] = dot(joined, pick[...], NN, HIGH)
    for n, (dy, dh) in enumerate(line):
        copy(fin.at[y, h], fin.at[y, h], S_FIN + n, dev_y(dy, dh)).start()
    for n, (dy, dh) in enumerate(line):
        copy(fin.at[y, h], fin.at[y, h], S_FIN + n, dev_y(dy, dh)).wait_recv()
    scores = fin[...].reshape(8, 8, 128).sum(axis=0) / RLEN
    out[...] = jnp.where(h == 0, scores[0:2, :32], scores[2:4, :32])
    for e in range(2):
        for d in range(1, 4):
            solved_second(e, d).wait_send()
    for n, (dy, dh) in enumerate(line):
        copy(fin.at[y, h], fin.at[y, h], S_FIN + n, dev_y(dy, dh)).wait_send()


def shards(act, grad, lengths, basis_in, basis_out, query_act, query_grad):
    vm = pltpu.VMEM
    anywhere = pl.BlockSpec(memory_space=pl.ANY)
    return pl.pallas_call(
        kernel,
        out_shape=jax.ShapeDtypeStruct((2, 32), F32),
        in_specs=[anywhere, anywhere, pl.BlockSpec(memory_space=pltpu.SMEM)] + [anywhere] * 4,
        out_specs=pl.BlockSpec(memory_space=pltpu.VMEM),
        scratch_shapes=[
            vm((TOK + RANK, DIM), BF),
            vm((TOK + RANK, DIM), BF),
            vm((4, DIM, 256), BF),
            vm((2, TOK, 256), BF),
            vm((PARTS, 2 * TOK, 256), BF),
            vm((2 * TOK, WIDTH), BF),
            vm((2, 4, 4, RANK, WIDTH), BF),
            vm((2, 16, 16, 128), BF),
            vm((2, 2, 16, 16, 128), BF),
            vm((4, 2, 2, 4, 16, 128), BF),
            vm((4, 4, 2, 2, 16, 128), BF),
            vm((4, 8, 32, 128), BF),
            vm((RING, 256, WIDTH), F32),
            vm((PARTS, 256, WIDTH), BF),
            vm((PARTS, 2, 32, WIDTH), BF),
            vm((PARTS, 2, 64, WIDTH), BF),
            vm((PARTS, 4, 16, WIDTH), BF),
            vm((PARTS, 3, 16, WIDTH), BF),
            vm((PARTS, 16, WIDTH), F32),
            vm((4, 2, RANK, 128), F32),
            vm((3, 2, RANK, 128), F32),
            vm((4, TOK, 256), F32),
            vm((3, TOK, 256), F32),
            vm((2 * TOK, 256), F32),
            vm((8, 8, 128), F32),
            vm((4, 8, 128), F32),
            vm((4, 8, 128), F32),
            vm((8, RANK, 128), F32),
            vm((2, 128, 128), F32),
            vm((8, 512, WIDTH), F32),
            vm((4, 2, 128, 128), F32),
            vm((3, 2, 128, 128), F32),
            vm((2, PARTS, 256, 128), BF),
            vm((256, 128), F32),
            vm((4, 2, 8, 128), F32),
            pltpu.SemaphoreType.DMA((12,)),
            pltpu.SemaphoreType.DMA((N_SEM,)),
            pltpu.SemaphoreType.DMA((N_SEM,)),
        ],
        compiler_params=pltpu.CompilerParams(
            collective_id=0, has_side_effects=True, vmem_limit_bytes=60 * 2**20
        ),
    )(act, grad, lengths, basis_in, basis_out, query_act, query_grad)


def solution(mesh):
    return jax.shard_map(
        shards,
        mesh=mesh,
        in_specs=(
            P("dp", None),
            P("dp", None),
            P("dp"),
            P(None, "col"),
            P(None, "col"),
            P("dp", None),
            P("dp", None),
        ),
        out_specs=P("dp", None),
        check_vma=False,
    )
```

```python
import functools

import jax
import jax.numpy as jnp
from jax import lax
from jax.experimental import pallas as pl
from jax.experimental.pallas import tpu as pltpu
from jax.sharding import PartitionSpec as P


RLEN = 128
RANK = 32
DIM = 4096
WIDTH = 1024
TOK = 256
RING = 5
PARTS = 8
damping_share = 0.1
ridge_share = 0.05
epsilon_add = 1e-06
BF = jnp.bfloat16
F32 = jnp.float32
MESH = pl.DeviceIdType.MESH
HIGH = lax.Precision.HIGHEST


def dot(a, b, dims, precision=None):
    return lax.dot_general(a, b, (dims, ((), ())), preferred_element_type=F32, precision=precision)


NN = ((1,), (0,))
TN = ((0,), (0,))
NT = ((1,), (1,))


class Slots:
    def __init__(self):
        self.count = 0

    def take(self, n):
        first = self.count
        self.count += n
        return first


SL = Slots()
S_SWAP_I = SL.take(2)
S_SWAP_A = SL.take(1)
S_SWAP_G = SL.take(1)
S_Y_I = SL.take(6)
S_L1 = SL.take(3)
S_L2 = SL.take(3)
S_LS = SL.take(1)
S_A1 = SL.take(3)
S_A2 = SL.take(3)
S_AY = SL.take(3)
S_FAR = SL.take(2 * PARTS)
S_NEAR = SL.take(2 * PARTS)
S_OUT2 = SL.take(3 * PARTS)
S_GRAM = SL.take(3)
S_LEFT = SL.take(3)
S_LEFTS = SL.take(1)
S_D1 = SL.take(7)
S_D2 = SL.take(3)
S_D3 = SL.take(3)
S_PROJ = SL.take(6)
S_S1 = SL.take(6)
S_S2 = SL.take(6)
S_FIN = SL.take(7)
N_SEM = SL.count


def kernel(
    act, grad, lens, b_in, b_out, q_act, q_grad,
    out,
    xin, xout, basis, send_i, ibuf, gbuf, lb, at_send, a_own, a_mid, a_recv, a4,
    acc, snd, far, near, snd2, got2, corr,
    gram_s, gram_r, left_s, left_r, left_f, damp_1, damp_2, damp_3, inv_w, inv_bd, rotated, proj_s, proj_r, sb, pick, fin,
    load_sem, ss, rs,
):
    dp = lax.axis_index("dp")
    y = lax.axis_index("col")
    x, z, h = dp // 8, (dp // 2) % 4, dp % 2
    u = x * (1 - h) + z * h
    v = z * (1 - h) + x * h
    me = u * 4 + v

    def dev_xz(xx, zz, hh, yy):
        return ((xx % 4) * 8 + (zz % 4) * 2 + hh, yy % 4)

    def dev(du, dv):
        uu, vv = u + du, v + dv
        return dev_xz(uu * (1 - h) + vv * h, vv * (1 - h) + uu * h, h, y)

    def dev_y(dy, dh=0):
        return dev_xz(x, z, (h + dh) % 2, y + dy)

    sibling = dev_y(0, 1)
    pending = []

    def copy(src, dst, idx, to):
        return pltpu.make_async_remote_copy(
            src_ref=src, dst_ref=dst, send_sem=ss.at[idx], recv_sem=rs.at[idx], device_id=to, device_id_type=MESH
        )

    def send(src, dst, idx, to):
        c = copy(src, dst, idx, to)
        c.start()
        pending.append(c)

    def tile_in(k):
        half = (1 - h) * (1 - k // 2) + h * (k // 2)
        return half * 2 + k % 2

    def load_in(k):
        cols = pl.ds(pl.multiple_of(tile_in(k) * 256, 256), 256)
        return pltpu.make_async_copy(b_in.at[:, cols], basis.at[k], load_sem.at[4 + k])

    def load_out(k):
        cols = pl.ds(pl.multiple_of(k * 256, 256), 256)
        return pltpu.make_async_copy(b_out.at[:, cols], basis.at[k], load_sem.at[8 + k])

    rows_of = [
        pltpu.make_async_copy(act, xin.at[pl.ds(0, TOK)], load_sem.at[0]),
        pltpu.make_async_copy(q_act, xin.at[pl.ds(TOK, RANK)], load_sem.at[1]),
        pltpu.make_async_copy(grad, xout.at[pl.ds(0, TOK)], load_sem.at[2]),
        pltpu.make_async_copy(q_grad, xout.at[pl.ds(TOK, RANK)], load_sem.at[3]),
    ]
    rows_of[2].start()
    rows_of[3].start()
    for k in range(4):
        load_out(k).start()
    rows_of[0].start()
    rows_of[1].start()

    line = [(dy, dh) for dy in range(4) for dh in range(2) if dy or dh]
    barrier = pltpu.get_barrier_semaphore()
    peers = [dev(d, 0) for d in range(1, 4)] + [dev(0, d) for d in range(1, 4)] + [dev_y(dy, dh) for dy, dh in line]
    for to in peers:
        pl.semaphore_signal(barrier, inc=1, device_id=to, device_id_type=MESH)

    lane = lax.broadcasted_iota(jnp.int32, (RANK, 128), 1)
    spread = (lane == lax.broadcasted_iota(jnp.int32, (RANK, 128), 0) + RANK * u).astype(BF)

    own_rows = pl.ds(pl.multiple_of(h * TOK, TOK), TOK)

    rows_of[2].wait()
    rows_of[3].wait()
    row = lax.broadcasted_iota(jnp.int32, (TOK, 256), 0)
    live = (row < lens[0]) | ((row >= RLEN) & (row < RLEN + lens[1]))

    def step_out(k, carry):
        load_out(k).wait()
        cols = pl.ds(pl.multiple_of(k * 256, 256), 256)
        r = dot(xout[...], basis[k], NN)
        gbuf[own_rows, cols] = jnp.where(live, r[:TOK], 0.0).astype(BF)
        lb[h, v, u, :, cols] = r[TOK:].astype(BF)
        load_in(k).start()
        return carry

    lax.fori_loop(0, 4, step_out, 0)
    pl.semaphore_wait(barrier, len(peers))
    for d in range(1, 4):
        part = lb.at[h, v, u]
        send(part, part, S_L1 + d - 1, dev(d, 0))
    send(gbuf.at[own_rows], gbuf.at[own_rows], S_SWAP_G, sibling)

    rows_of[0].wait()
    rows_of[1].wait()

    def swap_i(k):
        return copy(send_i.at[k], ibuf.at[k, own_rows], S_SWAP_I + k, sibling)

    def step_in(k, carry):
        load_in(k).wait()
        r = dot(xin[...], basis[k], NN).astype(BF)
        at = dot(r[TOK:], spread, TN).astype(BF).reshape(16, 16, 128)

        @pl.when(k < 2)
        def _():
            send_i[k] = r[:TOK]
            at_send[k] = at

        @pl.when(k >= 2)
        def _():
            ibuf[k - 2, own_rows] = r[:TOK]
            a_own[h, k - 2] = at

        return carry

    lax.fori_loop(0, 2, step_in, 0)
    for k in range(2):
        pending.append(swap_i(k))
        pending[-1].start()
    send(at_send, a_own.at[h], S_SWAP_A, sibling)
    lax.fori_loop(2, 4, step_in, 0)
    for d in range(1, 4):
        part = lb.at[h, v, u]
        copy(part, part, S_L1 + d - 1, dev(d, 0)).wait_recv()
    for d in range(1, 4):
        send(lb.at[h, v], lb.at[h, v], S_L2 + d - 1, dev(0, d))
    for k in range(2):
        swap_i(k).wait_recv()
    send(ibuf.at[0], ibuf.at[2], S_Y_I + 0, dev_y(1))
    send(ibuf.at[1], ibuf.at[3], S_Y_I + 1, dev_y(3))
    send(ibuf.at[1], ibuf.at[4], S_Y_I + 2, dev_y(1))
    send(ibuf.at[0], ibuf.at[5], S_Y_I + 3, dev_y(3))

    copy(at_send, a_own.at[1 - h], S_SWAP_A, sibling).wait_recv()
    for d in range(1, 4):
        there = pl.ds(((u + d) % 4) * 4, 4)
        send(a_own.at[:, :, there], a_mid.at[u], S_A1 + d - 1, dev(d, 0))
    a_mid[u] = a_own[:, :, pl.ds(u * 4, 4)]
    copy(gbuf.at[own_rows], gbuf.at[own_rows], S_SWAP_G, sibling).wait_recv()

    damp_1[0] = jnp.zeros((8, 128), F32)
    group = lax.broadcasted_iota(jnp.int32, (128, 128), 1) // RANK

    def place(i):
        first = (i < 2) * 1
        last = (i >= 6) * 1
        mid = 1 - first - last
        back = 1 - i % 2
        sigma = (y + last * 2 + mid * (back * 3 + (1 - back))) % 4
        k = (first + last) * (i % 2) + mid * ((i == 3) * 1 + (i == 4) * 1)
        return sigma * 2 + k

    def rows64(uu):
        return pl.ds(pl.multiple_of((uu % 4) * 64, 64), 64)

    def far_copies(i):
        over = (u + 2) % 4
        return (
            copy(snd.at[i, pl.ds(pl.multiple_of(over * 64, 64), 32)], far.at[i, 0], S_FAR + 2 * i, dev(1, 0)),
            copy(snd.at[i, pl.ds(pl.multiple_of(over * 64 + 32, 32), 32)], far.at[i, 1], S_FAR + 2 * i + 1, dev(3, 0)),
        )

    def near_copies(i):
        return (
            copy(snd.at[i, rows64(u + 1)], near.at[i, 0], S_NEAR + 2 * i, dev(1, 0)),
            copy(snd.at[i, rows64(u + 3)], near.at[i, 1], S_NEAR + 2 * i + 1, dev(3, 0)),
        )

    def out2_copies(i):
        return [
            copy(snd2.at[i, (v + d) % 4], got2.at[i, d - 1], S_OUT2 + 3 * i + d - 1, dev(0, d)) for d in (2, 1, 3)
        ]

    def relay(i):
        return copy(ibuf.at[i], ibuf.at[i + 4], S_Y_I + i + 2, dev_y(1 + 2 * (i - 2)))

    def stage_squares(i):
        @pl.when(i >= 2)
        def _():
            copy(ibuf.at[i], ibuf.at[i], S_Y_I + i - 2, dev_y(1)).wait_recv()

        @pl.when((i == 2) | (i == 3))
        def _():
            relay(i).start()

        for n in range(4):
            r = dot(ibuf[i, n * RLEN : (n + 1) * RLEN], gbuf[n * RLEN : (n + 1) * RLEN], TN)
            if n == 0:
                acc[i % RING] = r * r
            else:
                acc[i % RING] += r * r
        total = acc[i % RING].reshape(32, 8, WIDTH).sum(axis=0)
        for n in range(WIDTH // 128):
            damp_1[0] += total[:, n * 128 : (n + 1) * 128]
        over = rows64(u + 2)
        snd[i, over] = acc[i % RING, over].astype(BF)
        for c in far_copies(i):
            c.start()

    def stage_near(i):
        for c in far_copies(i):
            c.wait_recv()
        a = pl.multiple_of(((u + 1) % 4) * 64, 64)
        snd[i, pl.ds(a, 32)] = (acc[i % RING, pl.ds(a, 32)] + far[i, 0].astype(F32)).astype(BF)
        snd[i, pl.ds(a + 32, 32)] = acc[i % RING, pl.ds(a + 32, 32)].astype(BF)
        b = pl.multiple_of(((u + 3) % 4) * 64, 64)
        snd[i, pl.ds(b, 32)] = acc[i % RING, pl.ds(b, 32)].astype(BF)
        snd[i, pl.ds(b + 32, 32)] = (acc[i % RING, pl.ds(b + 32, 32)] + far[i, 1].astype(F32)).astype(BF)
        for c in near_copies(i):
            c.start()

    def own16(vv):
        return pl.ds(pl.multiple_of(u * 64 + (vv % 4) * 16, 16), 16)

    def stage_out2(i):
        for c in near_copies(i):
            c.wait_recv()
        mine64 = rows64(u)
        total = acc[i % RING, mine64] + near[i, 0].astype(F32) + near[i, 1].astype(F32)
        acc[i % RING, mine64] = total
        corr[place(i)] = acc[i % RING, own16(v)]
        snd2[i] = total.astype(BF).reshape(4, 16, WIDTH)
        for c in out2_copies(i):
            c.start()

    def stage_last(i, carry):
        for c in out2_copies(i):
            c.wait_recv()
        got = got2[i, 0].astype(F32) + got2[i, 1].astype(F32) + got2[i, 2].astype(F32)
        corr[place(i)] = 1.0 / ((corr[place(i)] + got) / 64.0 + damping)
        return carry

    def query_second():
        for d in range(1, 4):
            copy(a_own.at[:, :, pl.ds(0, 4)], a_mid.at[u], S_A1 + d - 1, dev(d, 0)).wait_recv()
        for d in range(1, 4):
            copy(a_mid.at[:, :, :, (v + d) % 4], a_recv.at[v], S_A2 + d - 1, dev(0, d)).start()
        a_recv[v] = a_mid[:, :, :, v]

    def query_third():
        for d in range(1, 4):
            copy(lb.at[h, v], lb.at[h, v], S_L2 + d - 1, dev(0, d)).wait_recv()
        copy(lb.at[h], lb.at[h], S_LS, sibling).start()
        for d in range(1, 4):
            copy(a_mid.at[:, :, :, v], a_recv.at[v], S_A2 + d - 1, dev(0, d)).wait_recv()
        for other in range(2):
            for vv in range(4):
                same = 1 - (other - h) * (other - h)
                total = jnp.zeros((32, 128), F32)
                for uu in range(4):
                    first = same * vv + (1 - same) * uu
                    second = same * uu + (1 - same) * vv
                    total = total + a_recv[first, second, other].reshape(32, 128).astype(F32)
                a4[y, other * 4 + vv] = total.astype(BF)
        for d in range(1, 4):
            copy(a4.at[y], a4.at[y], S_AY + d - 1, dev_y(d)).start()

    def plane_rows(yy):
        return lb[yy // 2, pl.ds((yy % 2) * 2, 2)].reshape(256, WIDTH)

    def gram_products():
        copy(lb.at[h], lb.at[1 - h], S_LS, sibling).wait_recv()

        def one(yy, carry):
            rows = plane_rows(yy)
            full = dot(rows, rows, NT)
            for e in range(2):
                packed = jnp.zeros((RANK, 128), F32)
                for q in range(4):
                    at = e * 128 + q * RANK
                    packed = packed + jnp.where(lane // RANK == q, full[at : at + RANK, e * 128 : e * 128 + 128], 0.0)
                gram_s[yy, e] = packed
            return carry

        lax.fori_loop(0, 4, one, 0)
        for d in (2, 1, 3):
            there = (y + d) % 4
            copy(gram_s.at[there], gram_r.at[d - 1], S_GRAM + d - 1, dev_y(d)).start()

    def left_products():
        def one(yy, carry):
            left_s[yy] = dot(gbuf[own_rows], plane_rows(yy), NT)
            return carry

        lax.fori_loop(0, 4, one, 0)
        for d in (2, 1, 3):
            there = (y + d) % 4
            copy(left_s.at[there], left_r.at[d - 1], S_LEFT + d - 1, dev_y(d)).start()

    def rotate(g):
        a = a4[:, g].reshape(128, 128)
        a_all = jnp.concatenate([jnp.where(group == q, a, jnp.zeros_like(a)) for q in range(4)], axis=0)
        rotated[g] = dot(a_all, lb[g // 4, g % 4].reshape(128, WIDTH), NN)

    def damping_first():
        for n, (dy, dh) in enumerate(line):
            copy(damp_1.at[0], damp_1.at[1 + n], S_D1 + n, dev_y(dy, dh)).start()

    def damping_second():
        for n, (dy, dh) in enumerate(line):
            copy(damp_1.at[0], damp_1.at[1 + n], S_D1 + n, dev_y(dy, dh)).wait_recv()
        damp_2[0] = damp_1[...].sum(axis=0)
        for d in range(1, 4):
            copy(damp_2.at[0], damp_2.at[d], S_D2 + d - 1, dev(d, 0)).start()

    def damping_third():
        for d in range(1, 4):
            copy(damp_2.at[0], damp_2.at[d], S_D2 + d - 1, dev(d, 0)).wait_recv()
        damp_3[0] = damp_2[...].sum(axis=0)
        for d in range(1, 4):
            copy(damp_3.at[0], damp_3.at[d], S_D3 + d - 1, dev(0, d)).start()

    lane2 = lax.broadcasted_iota(jnp.int32, (128, 128), 1)
    sub2 = lax.broadcasted_iota(jnp.int32, (128, 128), 0)

    def fold_block():
        fold = ((sub2 % RANK == lane2) & (lane2 < RANK)).astype(F32)
        return fold, sub2 // RANK == lane2 // RANK

    def gram_begin():
        for d in range(1, 4):
            copy(gram_s.at[y], gram_r.at[d - 1], S_GRAM + d - 1, dev_y(d)).wait_recv()
        gram = gram_s[y] + gram_r[0] + gram_r[1] + gram_r[2]
        fold, block = fold_block()
        wide = []
        for e in range(2):
            tall = jnp.concatenate([gram[e]] * 4, axis=0)
            wide.append(dot(jnp.where(block, tall, 0.0), fold, NN, HIGH).reshape(4, RANK, 128))
        w = jnp.concatenate(wide, axis=0)
        li = lax.broadcasted_iota(jnp.int32, (8, RANK, 128), 2)
        ri = lax.broadcasted_iota(jnp.int32, (8, RANK, 128), 1)
        inv_w[...] = w + jnp.where(li == ri, ridge_share * DIM, 0.0)

    def gram_sweep(first):
        li = lax.broadcasted_iota(jnp.int32, (8, RANK, 128), 2)
        ri = lax.broadcasted_iota(jnp.int32, (8, RANK, 128), 1)

        def sweep(k, w):
            at_k = li == k
            col = jnp.where(at_k, w, 0.0).sum(axis=2, keepdims=True)
            rowk = jnp.where(ri == k, w, 0.0).sum(axis=1, keepdims=True)
            pivot = jnp.where(at_k[:, :1], rowk, 0.0).sum(axis=2, keepdims=True)
            rowk = jnp.where(at_k[:, :1], 1.0, rowk) / pivot
            return jnp.where(ri == k, rowk, jnp.where(at_k, 0.0, w) - col * rowk)

        inv_w[...] = lax.fori_loop(first, first + 8, sweep, inv_w[...])

    def gram_end():
        fold, block = fold_block()
        for e in range(2):
            flat = inv_w[e * 4 : (e + 1) * 4].reshape(128, 128)
            inv_bd[e] = jnp.where(block, dot(flat, fold, NT, HIGH), 0.0)

    def left_sum():
        for d in range(1, 4):
            copy(left_s.at[y], left_r.at[d - 1], S_LEFT + d - 1, dev_y(d)).wait_recv()
        left_f[own_rows] = left_s[y] + left_r[0] + left_r[1] + left_r[2]
        copy(left_f.at[own_rows], left_f.at[own_rows], S_LEFTS, sibling).start()

    def selection():
        p = lax.broadcasted_iota(jnp.int32, (256, 128), 0) // RANK + y * 8
        hh, first, second = p // 16, p % 4, (p // 4) % 4
        xx = first * (1 - hh) + second * hh
        zz = second * (1 - hh) + first * hh
        pick[...] = (lax.broadcasted_iota(jnp.int32, (256, 128), 1) == xx * 8 + zz * 2 + hh).astype(F32)

    def rotate_ready():
        for d in range(1, 4):
            copy(a4.at[y], a4.at[y], S_AY + d - 1, dev_y(d)).wait_recv()

    def step(i, carry):
        @pl.when(i >= 2)
        def _():
            stage_near(i - 2)

        @pl.when(i >= 4)
        def _():
            stage_out2(i - 4)

        stage_squares(i)
        pl.when(i == 1)(query_second)
        pl.when(i == 3)(query_third)
        pl.when(i == 4)(gram_products)

        @pl.when(i == 5)
        def _():
            left_products()
            rotate_ready()

        pl.when(i == 6)(gram_begin)
        pl.when(i == 7)(damping_first)

        @pl.when(i >= 6)
        def _():
            gram_sweep((i - 6) * 8)
            rotate((i - 6) * 2)
            rotate((i - 6) * 2 + 1)

        return carry

    lax.fori_loop(0, PARTS, step, 0)
    stage_near(PARTS - 2)
    stage_out2(PARTS - 4)
    gram_sweep(16)
    stage_near(PARTS - 1)
    stage_out2(PARTS - 3)
    damping_second()
    gram_sweep(24)
    stage_out2(PARTS - 2)
    damping_third()

    def rotate_rest(g, carry):
        rotate(g)
        return carry

    lax.fori_loop(4, 6, rotate_rest, 0)
    stage_out2(PARTS - 1)
    lax.fori_loop(6, 8, rotate_rest, 0)
    gram_end()
    selection()

    for d in range(1, 4):
        copy(damp_3.at[0], damp_3.at[d], S_D3 + d - 1, dev(0, d)).wait_recv()
    damping = damping_share * (jnp.sum(damp_3[...]) / 64.0 / (DIM * DIM)) + epsilon_add
    lax.fori_loop(0, PARTS, stage_last, 0)

    def proj_copy(e, d):
        there = (y + d) % 4
        return copy(proj_s.at[there, e], proj_r.at[d - 1, e], S_PROJ + 3 * e + d - 1, dev_y(d))

    def solve_group(n, carry):
        e, m = n // 4, n % 4
        d = (m == 0) * 2 + (m == 1) * 1 + (m == 2) * 3
        there = (y + d) % 4
        g = there * 2 + e
        rows = lb[g // 4, g % 4].reshape(128, WIDTH)
        weight = corr[...].reshape(1, 128, WIDTH)
        scaled = (rotated[g].reshape(4, 128, WIDTH) * weight).reshape(512, WIDTH).astype(BF)
        p = dot(scaled, rows, NT)
        packed = jnp.zeros((128, 128), F32)
        for q in range(4):
            packed = packed + jnp.where(group == q, p[q * 128 : (q + 1) * 128], 0.0)
        proj_s[there, e] = packed

        @pl.when(m < 3)
        def _():
            proj_copy(e, d).start()

        return carry

    lax.fori_loop(0, 8, solve_group, 0)
    left_sum()

    mine = pl.ds(pl.multiple_of(me * 16, 16), 16)

    def solved_first(e, d):
        return copy(sb.at[e, :, mine], sb.at[e, :, mine], S_S1 + 3 * e + d - 1, dev(0, d))

    def solved_second(e, d):
        part = sb.at[e, :, pl.ds(pl.multiple_of(u * 64, 64), 64)]
        return copy(part, part, S_S2 + 3 * e + d - 1, dev(d, 0))

    for e in range(2):
        for d in range(1, 4):
            proj_copy(e, d).wait_recv()
        whole = proj_s[y, e] + proj_r[0, e] + proj_r[1, e] + proj_r[2, e]
        solved = dot(whole, inv_bd[e], NN, HIGH).astype(BF)
        sb[e, :, mine] = solved.reshape(PARTS, 16, 128)
        for d in (2, 1, 3):
            solved_first(e, d).start()
    for e in range(2):
        for d in range(1, 4):
            solved_first(e, d).wait_recv()
        for d in (2, 1, 3):
            solved_second(e, d).start()

    for c in pending:
        c.wait_send()

    def leave(k, carry):
        @pl.when(k < 2)
        def _():
            relay(k + 2).wait_send()

        for c in far_copies(k) + near_copies(k):
            c.wait_send()
        for c in out2_copies(k):
            c.wait_send()
        return carry

    lax.fori_loop(0, PARTS, leave, 0)
    for d in range(1, 4):
        copy(a_mid.at[:, :, :, (v + d) % 4], a_recv.at[v], S_A2 + d - 1, dev(0, d)).wait_send()
        copy(a4.at[y], a4.at[y], S_AY + d - 1, dev_y(d)).wait_send()
        copy(gram_s.at[y], gram_r.at[d - 1], S_GRAM + d - 1, dev_y(d)).wait_send()
        copy(left_s.at[y], left_r.at[d - 1], S_LEFT + d - 1, dev_y(d)).wait_send()
        copy(damp_2.at[0], damp_2.at[d], S_D2 + d - 1, dev(d, 0)).wait_send()
        copy(damp_3.at[0], damp_3.at[d], S_D3 + d - 1, dev(0, d)).wait_send()
        for e in range(2):
            proj_copy(e, d).wait_send()
            solved_first(e, d).wait_send()
    copy(lb.at[h], lb.at[h], S_LS, sibling).wait_send()
    copy(left_f.at[own_rows], left_f.at[own_rows], S_LEFTS, sibling).wait_send()
    for n, (dy, dh) in enumerate(line):
        copy(damp_1.at[0], damp_1.at[1 + n], S_D1 + n, dev_y(dy, dh)).wait_send()

    copy(left_f.at[own_rows], left_f.at[own_rows], S_LEFTS, sibling).wait_recv()
    joined = []
    for e in range(2):
        for d in range(1, 4):
            solved_second(e, d).wait_recv()

        right = jnp.zeros((2 * TOK, 128), F32)
        for i in range(PARTS):
            right = right + dot(ibuf[i], sb[e, place(i)], NN)
        joined.append((left_f[:, e * 128 : (e + 1) * 128] * right).reshape(4, RLEN, 128).sum(axis=1))
    joined = jnp.concatenate([jnp.concatenate(joined, axis=1), jnp.zeros((4, 256), F32)], axis=0)
    fin[y, h] = dot(joined, pick[...], NN, HIGH)
    for n, (dy, dh) in enumerate(line):
        copy(fin.at[y, h], fin.at[y, h], S_FIN + n, dev_y(dy, dh)).start()
    for n, (dy, dh) in enumerate(line):
        copy(fin.at[y, h], fin.at[y, h], S_FIN + n, dev_y(dy, dh)).wait_recv()
    scores = fin[...].reshape(8, 8, 128).sum(axis=0) / RLEN
    out[...] = jnp.where(h == 0, scores[0:2, :32], scores[2:4, :32])
    for e in range(2):
        for d in range(1, 4):
            solved_second(e, d).wait_send()
    for n, (dy, dh) in enumerate(line):
        copy(fin.at[y, h], fin.at[y, h], S_FIN + n, dev_y(dy, dh)).wait_send()


def shards(act, grad, lengths, basis_in, basis_out, query_act, query_grad):
    vm = pltpu.VMEM
    anywhere = pl.BlockSpec(memory_space=pl.ANY)
    return pl.pallas_call(
        kernel,
        out_shape=jax.ShapeDtypeStruct((2, 32), F32),
        in_specs=[anywhere, anywhere, pl.BlockSpec(memory_space=pltpu.SMEM)] + [anywhere] * 4,
        out_specs=pl.BlockSpec(memory_space=pltpu.VMEM),
        scratch_shapes=[
            vm((TOK + RANK, DIM), BF),
            vm((TOK + RANK, DIM), BF),
            vm((4, DIM, 256), BF),
            vm((2, TOK, 256), BF),
            vm((PARTS, 2 * TOK, 256), BF),
            vm((2 * TOK, WIDTH), BF),
            vm((2, 4, 4, RANK, WIDTH), BF),
            vm((2, 16, 16, 128), BF),
            vm((2, 2, 16, 16, 128), BF),
            vm((4, 2, 2, 4, 16, 128), BF),
            vm((4, 4, 2, 2, 16, 128), BF),
            vm((4, 8, 32, 128), BF),
            vm((RING, 256, WIDTH), F32),
            vm((PARTS, 256, WIDTH), BF),
            vm((PARTS, 2, 32, WIDTH), BF),
            vm((PARTS, 2, 64, WIDTH), BF),
            vm((PARTS, 4, 16, WIDTH), BF),
            vm((PARTS, 3, 16, WIDTH), BF),
            vm((PARTS, 16, WIDTH), F32),
            vm((4, 2, RANK, 128), F32),
            vm((3, 2, RANK, 128), F32),
            vm((4, TOK, 256), F32),
            vm((3, TOK, 256), F32),
            vm((2 * TOK, 256), F32),
            vm((8, 8, 128), F32),
            vm((4, 8, 128), F32),
            vm((4, 8, 128), F32),
            vm((8, RANK, 128), F32),
            vm((2, 128, 128), F32),
            vm((8, 512, WIDTH), F32),
            vm((4, 2, 128, 128), F32),
            vm((3, 2, 128, 128), F32),
            vm((2, PARTS, 256, 128), BF),
            vm((256, 128), F32),
            vm((4, 2, 8, 128), F32),
            pltpu.SemaphoreType.DMA((12,)),
            pltpu.SemaphoreType.DMA((N_SEM,)),
            pltpu.SemaphoreType.DMA((N_SEM,)),
        ],
        compiler_params=pltpu.CompilerParams(
            collective_id=0, has_side_effects=True, vmem_limit_bytes=60 * 2**20
        ),
    )(act, grad, lengths, basis_in, basis_out, query_act, query_grad)


def solution(mesh):
    return jax.shard_map(
        shards,
        mesh=mesh,
        in_specs=(
            P("dp", None),
            P("dp", None),
            P("dp"),
            P(None, "col"),
            P(None, "col"),
            P("dp", None),
            P("dp", None),
        ),
        out_specs=P("dp", None),
        check_vma=False,
    )
```

```python
import functools

import jax
import jax.numpy as jnp
from jax import lax
from jax.experimental import pallas as pl
from jax.experimental.pallas import tpu as pltpu
from jax.sharding import PartitionSpec as P


RLEN = 128
RANK = 32
DIM = 4096
WIDTH = 1024
TOK = 256
RING = 5
PARTS = 8
damping_share = 0.1
ridge_share = 0.05
epsilon_add = 1e-06
BF = jnp.bfloat16
F32 = jnp.float32
MESH = pl.DeviceIdType.MESH
HIGH = lax.Precision.HIGHEST


def dot(a, b, dims, precision=None):
    return lax.dot_general(a, b, (dims, ((), ())), preferred_element_type=F32, precision=precision)


NN = ((1,), (0,))
TN = ((0,), (0,))
NT = ((1,), (1,))


class Slots:
    def __init__(self):
        self.count = 0

    def take(self, n):
        first = self.count
        self.count += n
        return first


SL = Slots()
S_SWAP_I = SL.take(2)
S_SWAP_A = SL.take(1)
S_SWAP_G = SL.take(1)
S_Y_I = SL.take(6)
S_L1 = SL.take(3)
S_L2 = SL.take(3)
S_LS = SL.take(1)
S_A1 = SL.take(3)
S_A2 = SL.take(3)
S_AY = SL.take(3)
S_FAR = SL.take(2 * PARTS)
S_NEAR = SL.take(2 * PARTS)
S_OUT2 = SL.take(3 * PARTS)
S_GRAM = SL.take(3)
S_LEFT = SL.take(3)
S_LEFTS = SL.take(1)
S_D1 = SL.take(7)
S_D2 = SL.take(3)
S_D3 = SL.take(3)
S_PROJ = SL.take(6)
S_S1 = SL.take(6)
S_S2 = SL.take(6)
S_FIN = SL.take(7)
N_SEM = SL.count


def kernel(
    act, grad, lens, b_in, b_out, q_act, q_grad,
    out,
    xin, xout, basis, send_i, ibuf, gbuf, lb, at_send, a_own, a_mid, a_recv, a4,
    acc, snd, far, near, snd2, got2, corr,
    gram_s, gram_r, left_s, left_r, left_f, damp_1, damp_2, damp_3, inv_w, inv_bd, rotated, proj_s, proj_r, sb, pick, fin,
    load_sem, ss, rs,
):
    dp = lax.axis_index("dp")
    y = lax.axis_index("col")
    x, z, h = dp // 8, (dp // 2) % 4, dp % 2
    u = x * (1 - h) + z * h
    v = z * (1 - h) + x * h
    me = u * 4 + v

    def dev_xz(xx, zz, hh, yy):
        return ((xx % 4) * 8 + (zz % 4) * 2 + hh, yy % 4)

    def dev(du, dv):
        uu, vv = u + du, v + dv
        return dev_xz(uu * (1 - h) + vv * h, vv * (1 - h) + uu * h, h, y)

    def dev_y(dy, dh=0):
        return dev_xz(x, z, (h + dh) % 2, y + dy)

    sibling = dev_y(0, 1)
    pending = []

    def copy(src, dst, idx, to):
        return pltpu.make_async_remote_copy(
            src_ref=src, dst_ref=dst, send_sem=ss.at[idx], recv_sem=rs.at[idx], device_id=to, device_id_type=MESH
        )

    def send(src, dst, idx, to):
        c = copy(src, dst, idx, to)
        c.start()
        pending.append(c)

    def tile_in(k):
        half = (1 - h) * (1 - k // 2) + h * (k // 2)
        return half * 2 + k % 2

    def load_in(k):
        cols = pl.ds(pl.multiple_of(tile_in(k) * 256, 256), 256)
        return pltpu.make_async_copy(b_in.at[:, cols], basis.at[k], load_sem.at[4 + k])

    def load_out(k):
        cols = pl.ds(pl.multiple_of(k * 256, 256), 256)
        return pltpu.make_async_copy(b_out.at[:, cols], basis.at[k], load_sem.at[8 + k])

    rows_of = [
        pltpu.make_async_copy(act, xin.at[pl.ds(0, TOK)], load_sem.at[0]),
        pltpu.make_async_copy(q_act, xin.at[pl.ds(TOK, RANK)], load_sem.at[1]),
        pltpu.make_async_copy(grad, xout.at[pl.ds(0, TOK)], load_sem.at[2]),
        pltpu.make_async_copy(q_grad, xout.at[pl.ds(TOK, RANK)], load_sem.at[3]),
    ]
    rows_of[2].start()
    rows_of[3].start()
    for k in range(4):
        load_out(k).start()
    rows_of[0].start()
    rows_of[1].start()

    line = [(dy, dh) for dy in range(4) for dh in range(2) if dy or dh]
    barrier = pltpu.get_barrier_semaphore()
    peers = [dev(d, 0) for d in range(1, 4)] + [dev(0, d) for d in range(1, 4)] + [dev_y(dy, dh) for dy, dh in line]
    for to in peers:
        pl.semaphore_signal(barrier, inc=1, device_id=to, device_id_type=MESH)

    lane = lax.broadcasted_iota(jnp.int32, (RANK, 128), 1)
    spread = (lane == lax.broadcasted_iota(jnp.int32, (RANK, 128), 0) + RANK * u).astype(BF)

    own_rows = pl.ds(pl.multiple_of(h * TOK, TOK), TOK)

    rows_of[2].wait()
    rows_of[3].wait()
    row = lax.broadcasted_iota(jnp.int32, (TOK, 256), 0)
    live = (row < lens[0]) | ((row >= RLEN) & (row < RLEN + lens[1]))

    def step_out(k, carry):
        load_out(k).wait()
        cols = pl.ds(pl.multiple_of(k * 256, 256), 256)
        r = dot(xout[...], basis[k], NN)
        gbuf[own_rows, cols] = jnp.where(live, r[:TOK], 0.0).astype(BF)
        lb[h, v, u, :, cols] = r[TOK:].astype(BF)
        load_in(k).start()
        return carry

    lax.fori_loop(0, 4, step_out, 0)
    pl.semaphore_wait(barrier, len(peers))
    for d in range(1, 4):
        part = lb.at[h, v, u]
        send(part, part, S_L1 + d - 1, dev(d, 0))
    send(gbuf.at[own_rows], gbuf.at[own_rows], S_SWAP_G, sibling)

    rows_of[0].wait()
    rows_of[1].wait()

    def swap_i(k):
        return copy(send_i.at[k], ibuf.at[k, own_rows], S_SWAP_I + k, sibling)

    def step_in(k, carry):
        load_in(k).wait()
        r = dot(xin[...], basis[k], NN).astype(BF)
        at = dot(r[TOK:], spread, TN).astype(BF).reshape(16, 16, 128)

        @pl.when(k < 2)
        def _():
            send_i[k] = r[:TOK]
            at_send[k] = at

        @pl.when(k >= 2)
        def _():
            ibuf[k - 2, own_rows] = r[:TOK]
            a_own[h, k - 2] = at

        return carry

    lax.fori_loop(0, 2, step_in, 0)
    for k in range(2):
        pending.append(swap_i(k))
        pending[-1].start()
    send(at_send, a_own.at[h], S_SWAP_A, sibling)
    lax.fori_loop(2, 4, step_in, 0)
    for d in range(1, 4):
        part = lb.at[h, v, u]
        copy(part, part, S_L1 + d - 1, dev(d, 0)).wait_recv()
    for d in range(1, 4):
        send(lb.at[h, v], lb.at[h, v], S_L2 + d - 1, dev(0, d))
    for k in range(2):
        swap_i(k).wait_recv()
    send(ibuf.at[0], ibuf.at[2], S_Y_I + 0, dev_y(1))
    send(ibuf.at[1], ibuf.at[3], S_Y_I + 1, dev_y(3))
    send(ibuf.at[1], ibuf.at[4], S_Y_I + 2, dev_y(1))
    send(ibuf.at[0], ibuf.at[5], S_Y_I + 3, dev_y(3))

    copy(at_send, a_own.at[1 - h], S_SWAP_A, sibling).wait_recv()
    for d in range(1, 4):
        there = pl.ds(((u + d) % 4) * 4, 4)
        send(a_own.at[:, :, there], a_mid.at[u], S_A1 + d - 1, dev(d, 0))
    a_mid[u] = a_own[:, :, pl.ds(u * 4, 4)]
    copy(gbuf.at[own_rows], gbuf.at[own_rows], S_SWAP_G, sibling).wait_recv()

    damp_1[0] = jnp.zeros((8, 128), F32)
    group = lax.broadcasted_iota(jnp.int32, (128, 128), 1) // RANK

    def place(i):
        first = (i < 2) * 1
        last = (i >= 6) * 1
        mid = 1 - first - last
        back = 1 - i % 2
        sigma = (y + last * 2 + mid * (back * 3 + (1 - back))) % 4
        k = (first + last) * (i % 2) + mid * ((i == 3) * 1 + (i == 4) * 1)
        return sigma * 2 + k

    def rows64(uu):
        return pl.ds(pl.multiple_of((uu % 4) * 64, 64), 64)

    def far_copies(i):
        over = (u + 2) % 4
        return (
            copy(snd.at[i, pl.ds(pl.multiple_of(over * 64, 64), 32)], far.at[i, 0], S_FAR + 2 * i, dev(1, 0)),
            copy(snd.at[i, pl.ds(pl.multiple_of(over * 64 + 32, 32), 32)], far.at[i, 1], S_FAR + 2 * i + 1, dev(3, 0)),
        )

    def near_copies(i):
        return (
            copy(snd.at[i, rows64(u + 1)], near.at[i, 0], S_NEAR + 2 * i, dev(1, 0)),
            copy(snd.at[i, rows64(u + 3)], near.at[i, 1], S_NEAR + 2 * i + 1, dev(3, 0)),
        )

    def out2_copies(i):
        return [
            copy(snd2.at[i, (v + d) % 4], got2.at[i, d - 1], S_OUT2 + 3 * i + d - 1, dev(0, d)) for d in (2, 1, 3)
        ]

    def relay(i):
        return copy(ibuf.at[i], ibuf.at[i + 4], S_Y_I + i + 2, dev_y(1 + 2 * (i - 2)))

    def stage_squares(i):
        @pl.when(i >= 2)
        def _():
            copy(ibuf.at[i], ibuf.at[i], S_Y_I + i - 2, dev_y(1)).wait_recv()

        @pl.when((i == 2) | (i == 3))
        def _():
            relay(i).start()

        for n in range(4):
            r = dot(ibuf[i, n * RLEN : (n + 1) * RLEN], gbuf[n * RLEN : (n + 1) * RLEN], TN)
            if n == 0:
                acc[i % RING] = r * r
            else:
                acc[i % RING] += r * r
        total = acc[i % RING].reshape(32, 8, WIDTH).sum(axis=0)
        for n in range(WIDTH // 128):
            damp_1[0] += total[:, n * 128 : (n + 1) * 128]
        over = rows64(u + 2)
        snd[i, over] = acc[i % RING, over].astype(BF)
        for c in far_copies(i):
            c.start()

    def stage_near(i):
        for c in far_copies(i):
            c.wait_recv()
        a = pl.multiple_of(((u + 1) % 4) * 64, 64)
        snd[i, pl.ds(a, 32)] = (acc[i % RING, pl.ds(a, 32)] + far[i, 0].astype(F32)).astype(BF)
        snd[i, pl.ds(a + 32, 32)] = acc[i % RING, pl.ds(a + 32, 32)].astype(BF)
        b = pl.multiple_of(((u + 3) % 4) * 64, 64)
        snd[i, pl.ds(b, 32)] = acc[i % RING, pl.ds(b, 32)].astype(BF)
        snd[i, pl.ds(b + 32, 32)] = (acc[i % RING, pl.ds(b + 32, 32)] + far[i, 1].astype(F32)).astype(BF)
        for c in near_copies(i):
            c.start()

    def own16(vv):
        return pl.ds(pl.multiple_of(u * 64 + (vv % 4) * 16, 16), 16)

    def stage_out2(i):
        for c in near_copies(i):
            c.wait_recv()
        mine64 = rows64(u)
        total = acc[i % RING, mine64] + near[i, 0].astype(F32) + near[i, 1].astype(F32)
        acc[i % RING, mine64] = total
        corr[place(i)] = acc[i % RING, own16(v)]
        snd2[i] = total.astype(BF).reshape(4, 16, WIDTH)
        for c in out2_copies(i):
            c.start()

    def stage_last(i, carry):
        for c in out2_copies(i):
            c.wait_recv()
        got = got2[i, 0].astype(F32) + got2[i, 1].astype(F32) + got2[i, 2].astype(F32)
        corr[place(i)] = 1.0 / ((corr[place(i)] + got) / 64.0 + damping)
        return carry

    def query_second():
        for d in range(1, 4):
            copy(a_own.at[:, :, pl.ds(0, 4)], a_mid.at[u], S_A1 + d - 1, dev(d, 0)).wait_recv()
        for d in range(1, 4):
            copy(a_mid.at[:, :, :, (v + d) % 4], a_recv.at[v], S_A2 + d - 1, dev(0, d)).start()
        a_recv[v] = a_mid[:, :, :, v]

    def query_third():
        for d in range(1, 4):
            copy(lb.at[h, v], lb.at[h, v], S_L2 + d - 1, dev(0, d)).wait_recv()
        copy(lb.at[h], lb.at[h], S_LS, sibling).start()
        for d in range(1, 4):
            copy(a_mid.at[:, :, :, v], a_recv.at[v], S_A2 + d - 1, dev(0, d)).wait_recv()
        for other in range(2):
            for vv in range(4):
                same = 1 - (other - h) * (other - h)
                total = jnp.zeros((32, 128), F32)
                for uu in range(4):
                    first = same * vv + (1 - same) * uu
                    second = same * uu + (1 - same) * vv
                    total = total + a_recv[first, second, other].reshape(32, 128).astype(F32)
                a4[y, other * 4 + vv] = total.astype(BF)
        for d in range(1, 4):
            copy(a4.at[y], a4.at[y], S_AY + d - 1, dev_y(d)).start()

    def plane_rows(yy):
        return lb[yy // 2, pl.ds((yy % 2) * 2, 2)].reshape(256, WIDTH)

    def gram_products():
        copy(lb.at[h], lb.at[1 - h], S_LS, sibling).wait_recv()

        def one(yy, carry):
            rows = plane_rows(yy)
            full = dot(rows, rows, NT)
            for e in range(2):
                packed = jnp.zeros((RANK, 128), F32)
                for q in range(4):
                    at = e * 128 + q * RANK
                    packed = packed + jnp.where(lane // RANK == q, full[at : at + RANK, e * 128 : e * 128 + 128], 0.0)
                gram_s[yy, e] = packed
            return carry

        lax.fori_loop(0, 4, one, 0)
        for d in (2, 1, 3):
            there = (y + d) % 4
            copy(gram_s.at[there], gram_r.at[d - 1], S_GRAM + d - 1, dev_y(d)).start()

    def left_products():
        def one(yy, carry):
            left_s[yy] = dot(gbuf[own_rows], plane_rows(yy), NT)
            return carry

        lax.fori_loop(0, 4, one, 0)
        for d in (2, 1, 3):
            there = (y + d) % 4
            copy(left_s.at[there], left_r.at[d - 1], S_LEFT + d - 1, dev_y(d)).start()

    def rotate(g):
        a = a4[:, g].reshape(128, 128)
        a_all = jnp.concatenate([jnp.where(group == q, a, jnp.zeros_like(a)) for q in range(4)], axis=0)
        rotated[g] = dot(a_all, lb[g // 4, g % 4].reshape(128, WIDTH), NN)

    def damping_first():
        for n, (dy, dh) in enumerate(line):
            copy(damp_1.at[0], damp_1.at[1 + n], S_D1 + n, dev_y(dy, dh)).start()

    def damping_second():
        for n, (dy, dh) in enumerate(line):
            copy(damp_1.at[0], damp_1.at[1 + n], S_D1 + n, dev_y(dy, dh)).wait_recv()
        damp_2[0] = damp_1[...].sum(axis=0)
        for d in range(1, 4):
            copy(damp_2.at[0], damp_2.at[d], S_D2 + d - 1, dev(d, 0)).start()

    def damping_third():
        for d in range(1, 4):
            copy(damp_2.at[0], damp_2.at[d], S_D2 + d - 1, dev(d, 0)).wait_recv()
        damp_3[0] = damp_2[...].sum(axis=0)
        for d in range(1, 4):
            copy(damp_3.at[0], damp_3.at[d], S_D3 + d - 1, dev(0, d)).start()

    lane2 = lax.broadcasted_iota(jnp.int32, (128, 128), 1)
    sub2 = lax.broadcasted_iota(jnp.int32, (128, 128), 0)

    def fold_block():
        fold = ((sub2 % RANK == lane2) & (lane2 < RANK)).astype(F32)
        return fold, sub2 // RANK == lane2 // RANK

    def gram_begin():
        for d in range(1, 4):
            copy(gram_s.at[y], gram_r.at[d - 1], S_GRAM + d - 1, dev_y(d)).wait_recv()
        gram = gram_s[y] + gram_r[0] + gram_r[1] + gram_r[2]
        fold, block = fold_block()
        wide = []
        for e in range(2):
            tall = jnp.concatenate([gram[e]] * 4, axis=0)
            wide.append(dot(jnp.where(block, tall, 0.0), fold, NN, HIGH).reshape(4, RANK, 128))
        w = jnp.concatenate(wide, axis=0)
        li = lax.broadcasted_iota(jnp.int32, (8, RANK, 128), 2)
        ri = lax.broadcasted_iota(jnp.int32, (8, RANK, 128), 1)
        inv_w[...] = w + jnp.where(li == ri, ridge_share * DIM, 0.0)

    def gram_sweep(first, last):
        li = lax.broadcasted_iota(jnp.int32, (8, RANK, 128), 2)
        ri = lax.broadcasted_iota(jnp.int32, (8, RANK, 128), 1)

        def sweep(k, w):
            at_k = li == k
            col = jnp.where(at_k, w, 0.0).sum(axis=2, keepdims=True)
            rowk = jnp.where(ri == k, w, 0.0).sum(axis=1, keepdims=True)
            pivot = jnp.where(at_k[:, :1], rowk, 0.0).sum(axis=2, keepdims=True)
            rowk = jnp.where(at_k[:, :1], 1.0, rowk) / pivot
            return jnp.where(ri == k, rowk, jnp.where(at_k, 0.0, w) - col * rowk)

        inv_w[...] = lax.fori_loop(first, last, sweep, inv_w[...])

    def gram_end():
        fold, block = fold_block()
        for e in range(2):
            flat = inv_w[e * 4 : (e + 1) * 4].reshape(128, 128)
            inv_bd[e] = jnp.where(block, dot(flat, fold, NT, HIGH), 0.0)

    def left_sum():
        for d in range(1, 4):
            copy(left_s.at[y], left_r.at[d - 1], S_LEFT + d - 1, dev_y(d)).wait_recv()
        left_f[own_rows] = left_s[y] + left_r[0] + left_r[1] + left_r[2]
        copy(left_f.at[own_rows], left_f.at[own_rows], S_LEFTS, sibling).start()

    def selection():
        p = lax.broadcasted_iota(jnp.int32, (256, 128), 0) // RANK + y * 8
        hh, first, second = p // 16, p % 4, (p // 4) % 4
        xx = first * (1 - hh) + second * hh
        zz = second * (1 - hh) + first * hh
        pick[...] = (lax.broadcasted_iota(jnp.int32, (256, 128), 1) == xx * 8 + zz * 2 + hh).astype(F32)

    def rotate_ready():
        for d in range(1, 4):
            copy(a4.at[y], a4.at[y], S_AY + d - 1, dev_y(d)).wait_recv()

    def step(i, carry):
        @pl.when(i >= 2)
        def _():
            stage_near(i - 2)

        @pl.when(i >= 4)
        def _():
            stage_out2(i - 4)

        stage_squares(i)
        pl.when(i == 1)(query_second)
        pl.when(i == 3)(query_third)
        pl.when(i == 5)(gram_products)
        pl.when(i == 7)(damping_first)
        return carry

    def rotate_some(g, carry):
        rotate(g)
        return carry

    lax.fori_loop(0, PARTS, step, 0)
    stage_near(PARTS - 2)
    stage_out2(PARTS - 4)
    left_products()
    stage_near(PARTS - 1)
    stage_out2(PARTS - 3)
    damping_second()
    gram_begin()
    gram_sweep(0, 12)
    stage_out2(PARTS - 2)
    damping_third()
    rotate_ready()
    lax.fori_loop(0, 3, rotate_some, 0)
    stage_out2(PARTS - 1)
    lax.fori_loop(3, 8, rotate_some, 0)
    gram_sweep(12, 32)
    gram_end()
    selection()

    for d in range(1, 4):
        copy(damp_3.at[0], damp_3.at[d], S_D3 + d - 1, dev(0, d)).wait_recv()
    damping = damping_share * (jnp.sum(damp_3[...]) / 64.0 / (DIM * DIM)) + epsilon_add
    lax.fori_loop(0, PARTS, stage_last, 0)

    def proj_copy(e, d):
        there = (y + d) % 4
        return copy(proj_s.at[there, e], proj_r.at[d - 1, e], S_PROJ + 3 * e + d - 1, dev_y(d))

    def solve_group(n, carry):
        e, m = n // 4, n % 4
        d = (m == 0) * 2 + (m == 1) * 1 + (m == 2) * 3
        there = (y + d) % 4
        g = there * 2 + e
        rows = lb[g // 4, g % 4].reshape(128, WIDTH)
        weight = corr[...].reshape(1, 128, WIDTH)
        scaled = (rotated[g].reshape(4, 128, WIDTH) * weight).reshape(512, WIDTH).astype(BF)
        p = dot(scaled, rows, NT)
        packed = jnp.zeros((128, 128), F32)
        for q in range(4):
            packed = packed + jnp.where(group == q, p[q * 128 : (q + 1) * 128], 0.0)
        proj_s[there, e] = packed

        @pl.when(m < 3)
        def _():
            proj_copy(e, d).start()

        return carry

    lax.fori_loop(0, 8, solve_group, 0)
    left_sum()

    mine = pl.ds(pl.multiple_of(me * 16, 16), 16)

    def solved_first(e, d):
        return copy(sb.at[e, :, mine], sb.at[e, :, mine], S_S1 + 3 * e + d - 1, dev(0, d))

    def solved_second(e, d):
        part = sb.at[e, :, pl.ds(pl.multiple_of(u * 64, 64), 64)]
        return copy(part, part, S_S2 + 3 * e + d - 1, dev(d, 0))

    for e in range(2):
        for d in range(1, 4):
            proj_copy(e, d).wait_recv()
        whole = proj_s[y, e] + proj_r[0, e] + proj_r[1, e] + proj_r[2, e]
        solved = dot(whole, inv_bd[e], NN, HIGH).astype(BF)
        sb[e, :, mine] = solved.reshape(PARTS, 16, 128)
        for d in (2, 1, 3):
            solved_first(e, d).start()
    for e in range(2):
        for d in range(1, 4):
            solved_first(e, d).wait_recv()
        for d in (2, 1, 3):
            solved_second(e, d).start()

    for c in pending:
        c.wait_send()

    def leave(k, carry):
        @pl.when(k < 2)
        def _():
            relay(k + 2).wait_send()

        for c in far_copies(k) + near_copies(k):
            c.wait_send()
        for c in out2_copies(k):
            c.wait_send()
        return carry

    lax.fori_loop(0, PARTS, leave, 0)
    for d in range(1, 4):
        copy(a_mid.at[:, :, :, (v + d) % 4], a_recv.at[v], S_A2 + d - 1, dev(0, d)).wait_send()
        copy(a4.at[y], a4.at[y], S_AY + d - 1, dev_y(d)).wait_send()
        copy(gram_s.at[y], gram_r.at[d - 1], S_GRAM + d - 1, dev_y(d)).wait_send()
        copy(left_s.at[y], left_r.at[d - 1], S_LEFT + d - 1, dev_y(d)).wait_send()
        copy(damp_2.at[0], damp_2.at[d], S_D2 + d - 1, dev(d, 0)).wait_send()
        copy(damp_3.at[0], damp_3.at[d], S_D3 + d - 1, dev(0, d)).wait_send()
        for e in range(2):
            proj_copy(e, d).wait_send()
            solved_first(e, d).wait_send()
    copy(lb.at[h], lb.at[h], S_LS, sibling).wait_send()
    copy(left_f.at[own_rows], left_f.at[own_rows], S_LEFTS, sibling).wait_send()
    for n, (dy, dh) in enumerate(line):
        copy(damp_1.at[0], damp_1.at[1 + n], S_D1 + n, dev_y(dy, dh)).wait_send()

    copy(left_f.at[own_rows], left_f.at[own_rows], S_LEFTS, sibling).wait_recv()
    joined = []
    for e in range(2):
        for d in range(1, 4):
            solved_second(e, d).wait_recv()

        right = jnp.zeros((2 * TOK, 128), F32)
        for i in range(PARTS):
            right = right + dot(ibuf[i], sb[e, place(i)], NN)
        joined.append((left_f[:, e * 128 : (e + 1) * 128] * right).reshape(4, RLEN, 128).sum(axis=1))
    joined = jnp.concatenate([jnp.concatenate(joined, axis=1), jnp.zeros((4, 256), F32)], axis=0)
    fin[y, h] = dot(joined, pick[...], NN, HIGH)
    for n, (dy, dh) in enumerate(line):
        copy(fin.at[y, h], fin.at[y, h], S_FIN + n, dev_y(dy, dh)).start()
    for n, (dy, dh) in enumerate(line):
        copy(fin.at[y, h], fin.at[y, h], S_FIN + n, dev_y(dy, dh)).wait_recv()
    scores = fin[...].reshape(8, 8, 128).sum(axis=0) / RLEN
    out[...] = jnp.where(h == 0, scores[0:2, :32], scores[2:4, :32])
    for e in range(2):
        for d in range(1, 4):
            solved_second(e, d).wait_send()
    for n, (dy, dh) in enumerate(line):
        copy(fin.at[y, h], fin.at[y, h], S_FIN + n, dev_y(dy, dh)).wait_send()


def shards(act, grad, lengths, basis_in, basis_out, query_act, query_grad):
    vm = pltpu.VMEM
    anywhere = pl.BlockSpec(memory_space=pl.ANY)
    return pl.pallas_call(
        kernel,
        out_shape=jax.ShapeDtypeStruct((2, 32), F32),
        in_specs=[anywhere, anywhere, pl.BlockSpec(memory_space=pltpu.SMEM)] + [anywhere] * 4,
        out_specs=pl.BlockSpec(memory_space=pltpu.VMEM),
        scratch_shapes=[
            vm((TOK + RANK, DIM), BF),
            vm((TOK + RANK, DIM), BF),
            vm((4, DIM, 256), BF),
            vm((2, TOK, 256), BF),
            vm((PARTS, 2 * TOK, 256), BF),
            vm((2 * TOK, WIDTH), BF),
            vm((2, 4, 4, RANK, WIDTH), BF),
            vm((2, 16, 16, 128), BF),
            vm((2, 2, 16, 16, 128), BF),
            vm((4, 2, 2, 4, 16, 128), BF),
            vm((4, 4, 2, 2, 16, 128), BF),
            vm((4, 8, 32, 128), BF),
            vm((RING, 256, WIDTH), F32),
            vm((PARTS, 256, WIDTH), BF),
            vm((PARTS, 2, 32, WIDTH), BF),
            vm((PARTS, 2, 64, WIDTH), BF),
            vm((PARTS, 4, 16, WIDTH), BF),
            vm((PARTS, 3, 16, WIDTH), BF),
            vm((PARTS, 16, WIDTH), F32),
            vm((4, 2, RANK, 128), F32),
            vm((3, 2, RANK, 128), F32),
            vm((4, TOK, 256), F32),
            vm((3, TOK, 256), F32),
            vm((2 * TOK, 256), F32),
            vm((8, 8, 128), F32),
            vm((4, 8, 128), F32),
            vm((4, 8, 128), F32),
            vm((8, RANK, 128), F32),
            vm((2, 128, 128), F32),
            vm((8, 512, WIDTH), F32),
            vm((4, 2, 128, 128), F32),
            vm((3, 2, 128, 128), F32),
            vm((2, PARTS, 256, 128), BF),
            vm((256, 128), F32),
            vm((4, 2, 8, 128), F32),
            pltpu.SemaphoreType.DMA((12,)),
            pltpu.SemaphoreType.DMA((N_SEM,)),
            pltpu.SemaphoreType.DMA((N_SEM,)),
        ],
        compiler_params=pltpu.CompilerParams(
            collective_id=0, has_side_effects=True, vmem_limit_bytes=60 * 2**20
        ),
    )(act, grad, lengths, basis_in, basis_out, query_act, query_grad)


def solution(mesh):
    return jax.shard_map(
        shards,
        mesh=mesh,
        in_specs=(
            P("dp", None),
            P("dp", None),
            P("dp"),
            P(None, "col"),
            P(None, "col"),
            P("dp", None),
            P("dp", None),
        ),
        out_specs=P("dp", None),
        check_vma=False,
    )
```

```python
import functools

import jax
import jax.numpy as jnp
from jax import lax
from jax.experimental import pallas as pl
from jax.experimental.pallas import tpu as pltpu
from jax.sharding import PartitionSpec as P


RLEN = 128
RANK = 32
DIM = 4096
WIDTH = 1024
TOK = 256
RING = 5
PARTS = 8
damping_share = 0.1
ridge_share = 0.05
epsilon_add = 1e-06
BF = jnp.bfloat16
F32 = jnp.float32
MESH = pl.DeviceIdType.MESH
HIGH = lax.Precision.HIGHEST


def dot(a, b, dims, precision=None):
    return lax.dot_general(a, b, (dims, ((), ())), preferred_element_type=F32, precision=precision)


NN = ((1,), (0,))
TN = ((0,), (0,))
NT = ((1,), (1,))


class Slots:
    def __init__(self):
        self.count = 0

    def take(self, n):
        first = self.count
        self.count += n
        return first


SL = Slots()
S_SWAP_I = SL.take(2)
S_SWAP_A = SL.take(1)
S_SWAP_G = SL.take(1)
S_Y_I = SL.take(6)
S_L1 = SL.take(3)
S_L2 = SL.take(3)
S_LS = SL.take(1)
S_A1 = SL.take(3)
S_A2 = SL.take(3)
S_AY = SL.take(3)
S_FAR = SL.take(2 * PARTS)
S_NEAR = SL.take(2 * PARTS)
S_OUT2 = SL.take(3 * PARTS)
S_GRAM = SL.take(3)
S_LEFT = SL.take(3)
S_LEFTS = SL.take(1)
S_D1 = SL.take(7)
S_D2 = SL.take(3)
S_D3 = SL.take(3)
S_PROJ = SL.take(6)
S_S1 = SL.take(6)
S_S2 = SL.take(6)
S_FIN = SL.take(7)
N_SEM = SL.count


def kernel(
    act, grad, lens, b_in, b_out, q_act, q_grad,
    out,
    xin, xout, basis, send_i, ibuf, gbuf, lb, at_send, a_own, a_mid, a_recv, a4,
    acc, snd, far, near, snd2, got2, corr,
    gram_s, gram_r, left_s, left_r, left_f, damp_1, damp_2, damp_3, inv_w, inv_bd, rotated, proj_s, proj_r, sb, pick, fin,
    load_sem, ss, rs,
):
    dp = lax.axis_index("dp")
    y = lax.axis_index("col")
    x, z, h = dp // 8, (dp // 2) % 4, dp % 2
    u = x * (1 - h) + z * h
    v = z * (1 - h) + x * h
    me = u * 4 + v

    def dev_xz(xx, zz, hh, yy):
        return ((xx % 4) * 8 + (zz % 4) * 2 + hh, yy % 4)

    def dev(du, dv):
        uu, vv = u + du, v + dv
        return dev_xz(uu * (1 - h) + vv * h, vv * (1 - h) + uu * h, h, y)

    def dev_y(dy, dh=0):
        return dev_xz(x, z, (h + dh) % 2, y + dy)

    sibling = dev_y(0, 1)
    pending = []

    def copy(src, dst, idx, to):
        return pltpu.make_async_remote_copy(
            src_ref=src, dst_ref=dst, send_sem=ss.at[idx], recv_sem=rs.at[idx], device_id=to, device_id_type=MESH
        )

    def send(src, dst, idx, to):
        c = copy(src, dst, idx, to)
        c.start()
        pending.append(c)

    def tile_in(k):
        half = (1 - h) * (1 - k // 2) + h * (k // 2)
        return half * 2 + k % 2

    def load_in(k):
        cols = pl.ds(pl.multiple_of(tile_in(k) * 256, 256), 256)
        return pltpu.make_async_copy(b_in.at[:, cols], basis.at[k], load_sem.at[4 + k])

    def load_out(k):
        cols = pl.ds(pl.multiple_of(k * 256, 256), 256)
        return pltpu.make_async_copy(b_out.at[:, cols], basis.at[k], load_sem.at[8 + k])

    rows_of = [
        pltpu.make_async_copy(act, xin.at[pl.ds(0, TOK)], load_sem.at[0]),
        pltpu.make_async_copy(q_act, xin.at[pl.ds(TOK, RANK)], load_sem.at[1]),
        pltpu.make_async_copy(grad, xout.at[pl.ds(0, TOK)], load_sem.at[2]),
        pltpu.make_async_copy(q_grad, xout.at[pl.ds(TOK, RANK)], load_sem.at[3]),
    ]
    rows_of[2].start()
    rows_of[3].start()
    for k in range(4):
        load_out(k).start()
    rows_of[0].start()
    rows_of[1].start()

    line = [(dy, dh) for dy in range(4) for dh in range(2) if dy or dh]
    barrier = pltpu.get_barrier_semaphore()
    peers = [dev(d, 0) for d in range(1, 4)] + [dev(0, d) for d in range(1, 4)] + [dev_y(dy, dh) for dy, dh in line]
    for to in peers:
        pl.semaphore_signal(barrier, inc=1, device_id=to, device_id_type=MESH)

    lane = lax.broadcasted_iota(jnp.int32, (RANK, 128), 1)
    spread = (lane == lax.broadcasted_iota(jnp.int32, (RANK, 128), 0) + RANK * u).astype(BF)

    own_rows = pl.ds(pl.multiple_of(h * TOK, TOK), TOK)

    rows_of[2].wait()
    rows_of[3].wait()
    row = lax.broadcasted_iota(jnp.int32, (TOK, 256), 0)
    live = (row < lens[0]) | ((row >= RLEN) & (row < RLEN + lens[1]))

    def step_out(k, carry):
        load_out(k).wait()
        cols = pl.ds(pl.multiple_of(k * 256, 256), 256)
        r = dot(xout[...], basis[k], NN)
        gbuf[own_rows, cols] = jnp.where(live, r[:TOK], 0.0).astype(BF)
        lb[h, v, u, :, cols] = r[TOK:].astype(BF)
        load_in(k).start()
        return carry

    lax.fori_loop(0, 4, step_out, 0)
    pl.semaphore_wait(barrier, len(peers))
    for d in range(1, 4):
        part = lb.at[h, v, u]
        send(part, part, S_L1 + d - 1, dev(d, 0))
    send(gbuf.at[own_rows], gbuf.at[own_rows], S_SWAP_G, sibling)

    rows_of[0].wait()
    rows_of[1].wait()

    def swap_i(k):
        return copy(send_i.at[k], ibuf.at[k, own_rows], S_SWAP_I + k, sibling)

    def step_in(k, carry):
        load_in(k).wait()
        r = dot(xin[...], basis[k], NN).astype(BF)
        at = dot(r[TOK:], spread, TN).astype(BF).reshape(16, 16, 128)

        @pl.when(k < 2)
        def _():
            send_i[k] = r[:TOK]
            at_send[k] = at

        @pl.when(k >= 2)
        def _():
            ibuf[k - 2, own_rows] = r[:TOK]
            a_own[h, k - 2] = at

        return carry

    lax.fori_loop(0, 2, step_in, 0)
    for k in range(2):
        pending.append(swap_i(k))
        pending[-1].start()
    send(at_send, a_own.at[h], S_SWAP_A, sibling)
    lax.fori_loop(2, 4, step_in, 0)
    for d in range(1, 4):
        part = lb.at[h, v, u]
        copy(part, part, S_L1 + d - 1, dev(d, 0)).wait_recv()
    for d in range(1, 4):
        send(lb.at[h, v], lb.at[h, v], S_L2 + d - 1, dev(0, d))
    for k in range(2):
        swap_i(k).wait_recv()
    send(ibuf.at[0], ibuf.at[2], S_Y_I + 0, dev_y(1))
    send(ibuf.at[1], ibuf.at[3], S_Y_I + 1, dev_y(3))
    send(ibuf.at[1], ibuf.at[4], S_Y_I + 2, dev_y(1))
    send(ibuf.at[0], ibuf.at[5], S_Y_I + 3, dev_y(3))

    copy(at_send, a_own.at[1 - h], S_SWAP_A, sibling).wait_recv()
    for d in range(1, 4):
        there = pl.ds(((u + d) % 4) * 4, 4)
        send(a_own.at[:, :, there], a_mid.at[u], S_A1 + d - 1, dev(d, 0))
    a_mid[u] = a_own[:, :, pl.ds(u * 4, 4)]
    copy(gbuf.at[own_rows], gbuf.at[own_rows], S_SWAP_G, sibling).wait_recv()

    damp_1[0] = jnp.zeros((8, 128), F32)
    group = lax.broadcasted_iota(jnp.int32, (128, 128), 1) // RANK

    def place(i):
        first = (i < 2) * 1
        last = (i >= 6) * 1
        mid = 1 - first - last
        back = 1 - i % 2
        sigma = (y + last * 2 + mid * (back * 3 + (1 - back))) % 4
        k = (first + last) * (i % 2) + mid * ((i == 3) * 1 + (i == 4) * 1)
        return sigma * 2 + k

    def rows64(uu):
        return pl.ds(pl.multiple_of((uu % 4) * 64, 64), 64)

    def far_copies(i):
        over = (u + 2) % 4
        return (
            copy(snd.at[i, pl.ds(pl.multiple_of(over * 64, 64), 32)], far.at[i, 0], S_FAR + 2 * i, dev(1, 0)),
            copy(snd.at[i, pl.ds(pl.multiple_of(over * 64 + 32, 32), 32)], far.at[i, 1], S_FAR + 2 * i + 1, dev(3, 0)),
        )

    def near_copies(i):
        return (
            copy(snd.at[i, rows64(u + 1)], near.at[i, 0], S_NEAR + 2 * i, dev(1, 0)),
            copy(snd.at[i, rows64(u + 3)], near.at[i, 1], S_NEAR + 2 * i + 1, dev(3, 0)),
        )

    def out2_copies(i):
        return [
            copy(snd2.at[i, (v + d) % 4], got2.at[i, d - 1], S_OUT2 + 3 * i + d - 1, dev(0, d)) for d in (2, 1, 3)
        ]

    def relay(i):
        return copy(ibuf.at[i], ibuf.at[i + 4], S_Y_I + i + 2, dev_y(1 + 2 * (i - 2)))

    def stage_squares(i):
        @pl.when(i >= 2)
        def _():
            copy(ibuf.at[i], ibuf.at[i], S_Y_I + i - 2, dev_y(1)).wait_recv()

        @pl.when((i == 2) | (i == 3))
        def _():
            relay(i).start()

        for n in range(4):
            r = dot(ibuf[i, n * RLEN : (n + 1) * RLEN], gbuf[n * RLEN : (n + 1) * RLEN], TN)
            if n == 0:
                acc[i % RING] = r * r
            else:
                acc[i % RING] += r * r
        total = acc[i % RING].reshape(32, 8, WIDTH).sum(axis=0)
        for n in range(WIDTH // 128):
            damp_1[0] += total[:, n * 128 : (n + 1) * 128]
        over = rows64(u + 2)
        snd[i, over] = acc[i % RING, over].astype(BF)
        for c in far_copies(i):
            c.start()

    def stage_near(i):
        for c in far_copies(i):
            c.wait_recv()
        a = pl.multiple_of(((u + 1) % 4) * 64, 64)
        snd[i, pl.ds(a, 32)] = (acc[i % RING, pl.ds(a, 32)] + far[i, 0].astype(F32)).astype(BF)
        snd[i, pl.ds(a + 32, 32)] = acc[i % RING, pl.ds(a + 32, 32)].astype(BF)
        b = pl.multiple_of(((u + 3) % 4) * 64, 64)
        snd[i, pl.ds(b, 32)] = acc[i % RING, pl.ds(b, 32)].astype(BF)
        snd[i, pl.ds(b + 32, 32)] = (acc[i % RING, pl.ds(b + 32, 32)] + far[i, 1].astype(F32)).astype(BF)
        for c in near_copies(i):
            c.start()

    def own16(vv):
        return pl.ds(pl.multiple_of(u * 64 + (vv % 4) * 16, 16), 16)

    def stage_out2(i):
        for c in near_copies(i):
            c.wait_recv()
        mine64 = rows64(u)
        total = acc[i % RING, mine64] + near[i, 0].astype(F32) + near[i, 1].astype(F32)
        acc[i % RING, mine64] = total
        corr[place(i)] = acc[i % RING, own16(v)]
        snd2[i] = total.astype(BF).reshape(4, 16, WIDTH)
        for c in out2_copies(i):
            c.start()

    def stage_last(i, carry):
        for c in out2_copies(i):
            c.wait_recv()
        got = got2[i, 0].astype(F32) + got2[i, 1].astype(F32) + got2[i, 2].astype(F32)
        corr[place(i)] = 1.0 / ((corr[place(i)] + got) / 64.0 + damping)
        return carry

    def query_second():
        for d in range(1, 4):
            copy(a_own.at[:, :, pl.ds(0, 4)], a_mid.at[u], S_A1 + d - 1, dev(d, 0)).wait_recv()
        for d in range(1, 4):
            copy(a_mid.at[:, :, :, (v + d) % 4], a_recv.at[v], S_A2 + d - 1, dev(0, d)).start()
        a_recv[v] = a_mid[:, :, :, v]

    def query_third():
        for d in range(1, 4):
            copy(lb.at[h, v], lb.at[h, v], S_L2 + d - 1, dev(0, d)).wait_recv()
        copy(lb.at[h], lb.at[h], S_LS, sibling).start()
        for d in range(1, 4):
            copy(a_mid.at[:, :, :, v], a_recv.at[v], S_A2 + d - 1, dev(0, d)).wait_recv()
        for other in range(2):
            for vv in range(4):
                same = 1 - (other - h) * (other - h)
                total = jnp.zeros((32, 128), F32)
                for uu in range(4):
                    first = same * vv + (1 - same) * uu
                    second = same * uu + (1 - same) * vv
                    total = total + a_recv[first, second, other].reshape(32, 128).astype(F32)
                a4[y, other * 4 + vv] = total.astype(BF)
        for d in range(1, 4):
            copy(a4.at[y], a4.at[y], S_AY + d - 1, dev_y(d)).start()

    def plane_rows(yy):
        return lb[yy // 2, pl.ds((yy % 2) * 2, 2)].reshape(256, WIDTH)

    def gram_products():
        copy(lb.at[h], lb.at[1 - h], S_LS, sibling).wait_recv()

        def one(yy, carry):
            rows = plane_rows(yy)
            full = dot(rows, rows, NT)
            for e in range(2):
                packed = jnp.zeros((RANK, 128), F32)
                for q in range(4):
                    at = e * 128 + q * RANK
                    packed = packed + jnp.where(lane // RANK == q, full[at : at + RANK, e * 128 : e * 128 + 128], 0.0)
                gram_s[yy, e] = packed
            return carry

        lax.fori_loop(0, 4, one, 0)
        for d in (2, 1, 3):
            there = (y + d) % 4
            copy(gram_s.at[there], gram_r.at[d - 1], S_GRAM + d - 1, dev_y(d)).start()

    def left_products():
        def one(yy, carry):
            left_s[yy] = dot(gbuf[own_rows], plane_rows(yy), NT)
            return carry

        lax.fori_loop(0, 4, one, 0)
        for d in (2, 1, 3):
            there = (y + d) % 4
            copy(left_s.at[there], left_r.at[d - 1], S_LEFT + d - 1, dev_y(d)).start()

    def rotate(g):
        a = a4[:, g].reshape(128, 128)
        a_all = jnp.concatenate([jnp.where(group == q, a, jnp.zeros_like(a)) for q in range(4)], axis=0)
        rotated[g] = dot(a_all, lb[g // 4, g % 4].reshape(128, WIDTH), NN)

    def damping_first():
        for n, (dy, dh) in enumerate(line):
            copy(damp_1.at[0], damp_1.at[1 + n], S_D1 + n, dev_y(dy, dh)).start()

    def damping_second():
        for n, (dy, dh) in enumerate(line):
            copy(damp_1.at[0], damp_1.at[1 + n], S_D1 + n, dev_y(dy, dh)).wait_recv()
        damp_2[0] = damp_1[...].sum(axis=0)
        for d in range(1, 4):
            copy(damp_2.at[0], damp_2.at[d], S_D2 + d - 1, dev(d, 0)).start()

    def damping_third():
        for d in range(1, 4):
            copy(damp_2.at[0], damp_2.at[d], S_D2 + d - 1, dev(d, 0)).wait_recv()
        damp_3[0] = damp_2[...].sum(axis=0)
        for d in range(1, 4):
            copy(damp_3.at[0], damp_3.at[d], S_D3 + d - 1, dev(0, d)).start()

    lane2 = lax.broadcasted_iota(jnp.int32, (128, 128), 1)
    sub2 = lax.broadcasted_iota(jnp.int32, (128, 128), 0)

    def fold_block():
        fold = ((sub2 % RANK == lane2) & (lane2 < RANK)).astype(F32)
        return fold, sub2 // RANK == lane2 // RANK

    def gram_begin():
        for d in range(1, 4):
            copy(gram_s.at[y], gram_r.at[d - 1], S_GRAM + d - 1, dev_y(d)).wait_recv()
        gram = gram_s[y] + gram_r[0] + gram_r[1] + gram_r[2]
        fold, block = fold_block()
        wide = []
        for e in range(2):
            tall = jnp.concatenate([gram[e]] * 4, axis=0)
            wide.append(dot(jnp.where(block, tall, 0.0), fold, NN, HIGH).reshape(4, RANK, 128))
        w = jnp.concatenate(wide, axis=0)
        li = lax.broadcasted_iota(jnp.int32, (8, RANK, 128), 2)
        ri = lax.broadcasted_iota(jnp.int32, (8, RANK, 128), 1)
        inv_w[...] = w + jnp.where(li == ri, ridge_share * DIM, 0.0)

    def gram_sweep(first, last):
        li = lax.broadcasted_iota(jnp.int32, (8, RANK, 128), 2)
        ri = lax.broadcasted_iota(jnp.int32, (8, RANK, 128), 1)

        def sweep(k, w):
            at_k = li == k
            col = jnp.where(at_k, w, 0.0).sum(axis=2, keepdims=True)
            rowk = jnp.where(ri == k, w, 0.0).sum(axis=1, keepdims=True)
            pivot = jnp.where(at_k[:, :1], rowk, 0.0).sum(axis=2, keepdims=True)
            rowk = jnp.where(at_k[:, :1], 1.0, rowk) / pivot
            return jnp.where(ri == k, rowk, jnp.where(at_k, 0.0, w) - col * rowk)

        inv_w[...] = lax.fori_loop(first, last, sweep, inv_w[...])

    def gram_end():
        fold, block = fold_block()
        for e in range(2):
            flat = inv_w[e * 4 : (e + 1) * 4].reshape(128, 128)
            inv_bd[e] = jnp.where(block, dot(flat, fold, NT, HIGH), 0.0)

    def left_sum():
        for d in range(1, 4):
            copy(left_s.at[y], left_r.at[d - 1], S_LEFT + d - 1, dev_y(d)).wait_recv()
        left_f[own_rows] = left_s[y] + left_r[0] + left_r[1] + left_r[2]
        copy(left_f.at[own_rows], left_f.at[own_rows], S_LEFTS, sibling).start()

    def selection():
        p = lax.broadcasted_iota(jnp.int32, (256, 128), 0) // RANK + y * 8
        hh, first, second = p // 16, p % 4, (p // 4) % 4
        xx = first * (1 - hh) + second * hh
        zz = second * (1 - hh) + first * hh
        pick[...] = (lax.broadcasted_iota(jnp.int32, (256, 128), 1) == xx * 8 + zz * 2 + hh).astype(F32)

    def rotate_ready():
        for d in range(1, 4):
            copy(a4.at[y], a4.at[y], S_AY + d - 1, dev_y(d)).wait_recv()

    def rotate_some(g, carry):
        rotate(g)
        return carry

    def step(p, carry):
        stage_squares(2 * p)
        stage_squares(2 * p + 1)

        @pl.when(p >= 1)
        def _():
            stage_out2(2 * p - 2)
            stage_out2(2 * p - 1)

        pl.when(p == 0)(query_second)
        pl.when(p == 1)(query_third)
        pl.when(p == 2)(gram_products)

        @pl.when(p == 3)
        def _():
            damping_first()
            left_products()
            rotate_ready()
            lax.fori_loop(0, 4, rotate_some, 0)

        stage_near(2 * p)
        stage_near(2 * p + 1)
        return carry

    lax.fori_loop(0, PARTS // 2, step, 0)
    damping_second()
    gram_begin()
    gram_sweep(0, 16)
    stage_out2(PARTS - 2)
    stage_out2(PARTS - 1)
    damping_third()
    lax.fori_loop(4, 8, rotate_some, 0)
    gram_sweep(16, 32)
    gram_end()
    selection()

    for d in range(1, 4):
        copy(damp_3.at[0], damp_3.at[d], S_D3 + d - 1, dev(0, d)).wait_recv()
    damping = damping_share * (jnp.sum(damp_3[...]) / 64.0 / (DIM * DIM)) + epsilon_add
    lax.fori_loop(0, PARTS, stage_last, 0)

    def proj_copy(e, d):
        there = (y + d) % 4
        return copy(proj_s.at[there, e], proj_r.at[d - 1, e], S_PROJ + 3 * e + d - 1, dev_y(d))

    def solve_group(n, carry):
        e, m = n // 4, n % 4
        d = (m == 0) * 2 + (m == 1) * 1 + (m == 2) * 3
        there = (y + d) % 4
        g = there * 2 + e
        rows = lb[g // 4, g % 4].reshape(128, WIDTH)
        weight = corr[...].reshape(1, 128, WIDTH)
        scaled = (rotated[g].reshape(4, 128, WIDTH) * weight).reshape(512, WIDTH).astype(BF)
        p = dot(scaled, rows, NT)
        packed = jnp.zeros((128, 128), F32)
        for q in range(4):
            packed = packed + jnp.where(group == q, p[q * 128 : (q + 1) * 128], 0.0)
        proj_s[there, e] = packed

        @pl.when(m < 3)
        def _():
            proj_copy(e, d).start()

        return carry

    lax.fori_loop(0, 8, solve_group, 0)
    left_sum()

    mine = pl.ds(pl.multiple_of(me * 16, 16), 16)

    def solved_first(e, d):
        return copy(sb.at[e, :, mine], sb.at[e, :, mine], S_S1 + 3 * e + d - 1, dev(0, d))

    def solved_second(e, d):
        part = sb.at[e, :, pl.ds(pl.multiple_of(u * 64, 64), 64)]
        return copy(part, part, S_S2 + 3 * e + d - 1, dev(d, 0))

    for e in range(2):
        for d in range(1, 4):
            proj_copy(e, d).wait_recv()
        whole = proj_s[y, e] + proj_r[0, e] + proj_r[1, e] + proj_r[2, e]
        solved = dot(whole, inv_bd[e], NN, HIGH).astype(BF)
        sb[e, :, mine] = solved.reshape(PARTS, 16, 128)
        for d in (2, 1, 3):
            solved_first(e, d).start()
    for e in range(2):
        for d in range(1, 4):
            solved_first(e, d).wait_recv()
        for d in (2, 1, 3):
            solved_second(e, d).start()

    for c in pending:
        c.wait_send()

    def leave(k, carry):
        @pl.when(k < 2)
        def _():
            relay(k + 2).wait_send()

        for c in far_copies(k) + near_copies(k):
            c.wait_send()
        for c in out2_copies(k):
            c.wait_send()
        return carry

    lax.fori_loop(0, PARTS, leave, 0)
    for d in range(1, 4):
        copy(a_mid.at[:, :, :, (v + d) % 4], a_recv.at[v], S_A2 + d - 1, dev(0, d)).wait_send()
        copy(a4.at[y], a4.at[y], S_AY + d - 1, dev_y(d)).wait_send()
        copy(gram_s.at[y], gram_r.at[d - 1], S_GRAM + d - 1, dev_y(d)).wait_send()
        copy(left_s.at[y], left_r.at[d - 1], S_LEFT + d - 1, dev_y(d)).wait_send()
        copy(damp_2.at[0], damp_2.at[d], S_D2 + d - 1, dev(d, 0)).wait_send()
        copy(damp_3.at[0], damp_3.at[d], S_D3 + d - 1, dev(0, d)).wait_send()
        for e in range(2):
            proj_copy(e, d).wait_send()
            solved_first(e, d).wait_send()
    copy(lb.at[h], lb.at[h], S_LS, sibling).wait_send()
    copy(left_f.at[own_rows], left_f.at[own_rows], S_LEFTS, sibling).wait_send()
    for n, (dy, dh) in enumerate(line):
        copy(damp_1.at[0], damp_1.at[1 + n], S_D1 + n, dev_y(dy, dh)).wait_send()

    copy(left_f.at[own_rows], left_f.at[own_rows], S_LEFTS, sibling).wait_recv()
    joined = []
    for e in range(2):
        for d in range(1, 4):
            solved_second(e, d).wait_recv()

        right = jnp.zeros((2 * TOK, 128), F32)
        for i in range(PARTS):
            right = right + dot(ibuf[i], sb[e, place(i)], NN)
        joined.append((left_f[:, e * 128 : (e + 1) * 128] * right).reshape(4, RLEN, 128).sum(axis=1))
    joined = jnp.concatenate([jnp.concatenate(joined, axis=1), jnp.zeros((4, 256), F32)], axis=0)
    fin[y, h] = dot(joined, pick[...], NN, HIGH)
    for n, (dy, dh) in enumerate(line):
        copy(fin.at[y, h], fin.at[y, h], S_FIN + n, dev_y(dy, dh)).start()
    for n, (dy, dh) in enumerate(line):
        copy(fin.at[y, h], fin.at[y, h], S_FIN + n, dev_y(dy, dh)).wait_recv()
    scores = fin[...].reshape(8, 8, 128).sum(axis=0) / RLEN
    out[...] = jnp.where(h == 0, scores[0:2, :32], scores[2:4, :32])
    for e in range(2):
        for d in range(1, 4):
            solved_second(e, d).wait_send()
    for n, (dy, dh) in enumerate(line):
        copy(fin.at[y, h], fin.at[y, h], S_FIN + n, dev_y(dy, dh)).wait_send()


def shards(act, grad, lengths, basis_in, basis_out, query_act, query_grad):
    vm = pltpu.VMEM
    anywhere = pl.BlockSpec(memory_space=pl.ANY)
    return pl.pallas_call(
        kernel,
        out_shape=jax.ShapeDtypeStruct((2, 32), F32),
        in_specs=[anywhere, anywhere, pl.BlockSpec(memory_space=pltpu.SMEM)] + [anywhere] * 4,
        out_specs=pl.BlockSpec(memory_space=pltpu.VMEM),
        scratch_shapes=[
            vm((TOK + RANK, DIM), BF),
            vm((TOK + RANK, DIM), BF),
            vm((4, DIM, 256), BF),
            vm((2, TOK, 256), BF),
            vm((PARTS, 2 * TOK, 256), BF),
            vm((2 * TOK, WIDTH), BF),
            vm((2, 4, 4, RANK, WIDTH), BF),
            vm((2, 16, 16, 128), BF),
            vm((2, 2, 16, 16, 128), BF),
            vm((4, 2, 2, 4, 16, 128), BF),
            vm((4, 4, 2, 2, 16, 128), BF),
            vm((4, 8, 32, 128), BF),
            vm((RING, 256, WIDTH), F32),
            vm((PARTS, 256, WIDTH), BF),
            vm((PARTS, 2, 32, WIDTH), BF),
            vm((PARTS, 2, 64, WIDTH), BF),
            vm((PARTS, 4, 16, WIDTH), BF),
            vm((PARTS, 3, 16, WIDTH), BF),
            vm((PARTS, 16, WIDTH), F32),
            vm((4, 2, RANK, 128), F32),
            vm((3, 2, RANK, 128), F32),
            vm((4, TOK, 256), F32),
            vm((3, TOK, 256), F32),
            vm((2 * TOK, 256), F32),
            vm((8, 8, 128), F32),
            vm((4, 8, 128), F32),
            vm((4, 8, 128), F32),
            vm((8, RANK, 128), F32),
            vm((2, 128, 128), F32),
            vm((8, 512, WIDTH), F32),
            vm((4, 2, 128, 128), F32),
            vm((3, 2, 128, 128), F32),
            vm((2, PARTS, 256, 128), BF),
            vm((256, 128), F32),
            vm((4, 2, 8, 128), F32),
            pltpu.SemaphoreType.DMA((12,)),
            pltpu.SemaphoreType.DMA((N_SEM,)),
            pltpu.SemaphoreType.DMA((N_SEM,)),
        ],
        compiler_params=pltpu.CompilerParams(
            collective_id=0, has_side_effects=True, vmem_limit_bytes=60 * 2**20
        ),
    )(act, grad, lengths, basis_in, basis_out, query_act, query_grad)


def solution(mesh):
    return jax.shard_map(
        shards,
        mesh=mesh,
        in_specs=(
            P("dp", None),
            P("dp", None),
            P("dp"),
            P(None, "col"),
            P(None, "col"),
            P("dp", None),
            P("dp", None),
        ),
        out_specs=P("dp", None),
        check_vma=False,
    )
```

```python
import functools

import jax
import jax.numpy as jnp
from jax import lax
from jax.experimental import pallas as pl
from jax.experimental.pallas import tpu as pltpu
from jax.sharding import PartitionSpec as P


RLEN = 128
RANK = 32
DIM = 4096
WIDTH = 1024
TOK = 256
RING = 5
PARTS = 8
damping_share = 0.1
ridge_share = 0.05
epsilon_add = 1e-06
BF = jnp.bfloat16
F32 = jnp.float32
MESH = pl.DeviceIdType.MESH
HIGH = lax.Precision.HIGHEST


def dot(a, b, dims, precision=None):
    return lax.dot_general(a, b, (dims, ((), ())), preferred_element_type=F32, precision=precision)


NN = ((1,), (0,))
TN = ((0,), (0,))
NT = ((1,), (1,))


class Slots:
    def __init__(self):
        self.count = 0

    def take(self, n):
        first = self.count
        self.count += n
        return first


SL = Slots()
S_SWAP_I = SL.take(2)
S_SWAP_A = SL.take(1)
S_SWAP_G = SL.take(1)
S_Y_I = SL.take(6)
S_L1 = SL.take(3)
S_L2 = SL.take(3)
S_LS = SL.take(1)
S_A1 = SL.take(3)
S_A2 = SL.take(3)
S_AY = SL.take(3)
S_FAR = SL.take(2 * PARTS)
S_NEAR = SL.take(2 * PARTS)
S_OUT2 = SL.take(3 * PARTS)
S_GRAM = SL.take(3)
S_LEFT = SL.take(3)
S_LEFTS = SL.take(1)
S_D1 = SL.take(7)
S_D2 = SL.take(3)
S_D3 = SL.take(3)
S_PROJ = SL.take(6)
S_S1 = SL.take(6)
S_S2 = SL.take(6)
S_FIN = SL.take(7)
N_SEM = SL.count


def kernel(
    act, grad, lens, b_in, b_out, q_act, q_grad,
    out,
    xin, xout, basis, send_i, ibuf, gbuf, lb, at_send, a_own, a_mid, a_recv, a4,
    acc, snd, far, near, snd2, got2, corr,
    gram_s, gram_r, left_s, left_r, left_f, damp_1, damp_2, damp_3, inv_w, inv_bd, rotated, proj_s, proj_r, sb, pick, fin,
    load_sem, ss, rs,
):
    dp = lax.axis_index("dp")
    y = lax.axis_index("col")
    x, z, h = dp // 8, (dp // 2) % 4, dp % 2
    u = x * (1 - h) + z * h
    v = z * (1 - h) + x * h
    me = u * 4 + v

    def dev_xz(xx, zz, hh, yy):
        return ((xx % 4) * 8 + (zz % 4) * 2 + hh, yy % 4)

    def dev(du, dv):
        uu, vv = u + du, v + dv
        return dev_xz(uu * (1 - h) + vv * h, vv * (1 - h) + uu * h, h, y)

    def dev_y(dy, dh=0):
        return dev_xz(x, z, (h + dh) % 2, y + dy)

    sibling = dev_y(0, 1)
    pending = []

    def copy(src, dst, idx, to):
        return pltpu.make_async_remote_copy(
            src_ref=src, dst_ref=dst, send_sem=ss.at[idx], recv_sem=rs.at[idx], device_id=to, device_id_type=MESH
        )

    def send(src, dst, idx, to):
        c = copy(src, dst, idx, to)
        c.start()
        pending.append(c)

    def tile_in(k):
        half = (1 - h) * (1 - k // 2) + h * (k // 2)
        return half * 2 + k % 2

    def load_in(k):
        cols = pl.ds(pl.multiple_of(tile_in(k) * 256, 256), 256)
        return pltpu.make_async_copy(b_in.at[:, cols], basis.at[k], load_sem.at[4 + k])

    def load_out(k):
        cols = pl.ds(pl.multiple_of(k * 256, 256), 256)
        return pltpu.make_async_copy(b_out.at[:, cols], basis.at[k], load_sem.at[8 + k])

    rows_of = [
        pltpu.make_async_copy(act, xin.at[pl.ds(0, TOK)], load_sem.at[0]),
        pltpu.make_async_copy(q_act, xin.at[pl.ds(TOK, RANK)], load_sem.at[1]),
        pltpu.make_async_copy(grad, xout.at[pl.ds(0, TOK)], load_sem.at[2]),
        pltpu.make_async_copy(q_grad, xout.at[pl.ds(TOK, RANK)], load_sem.at[3]),
    ]
    rows_of[2].start()
    rows_of[3].start()
    for k in range(4):
        load_out(k).start()
    rows_of[0].start()
    rows_of[1].start()

    line = [(dy, dh) for dy in range(4) for dh in range(2) if dy or dh]
    barrier = pltpu.get_barrier_semaphore()
    peers = [dev(d, 0) for d in range(1, 4)] + [dev(0, d) for d in range(1, 4)] + [dev_y(dy, dh) for dy, dh in line]
    for to in peers:
        pl.semaphore_signal(barrier, inc=1, device_id=to, device_id_type=MESH)

    lane = lax.broadcasted_iota(jnp.int32, (RANK, 128), 1)
    spread = (lane == lax.broadcasted_iota(jnp.int32, (RANK, 128), 0) + RANK * u).astype(BF)

    own_rows = pl.ds(pl.multiple_of(h * TOK, TOK), TOK)

    rows_of[2].wait()
    rows_of[3].wait()
    row = lax.broadcasted_iota(jnp.int32, (TOK, 256), 0)
    live = (row < lens[0]) | ((row >= RLEN) & (row < RLEN + lens[1]))

    def step_out(k, carry):
        load_out(k).wait()
        cols = pl.ds(pl.multiple_of(k * 256, 256), 256)
        r = dot(xout[...], basis[k], NN)
        gbuf[own_rows, cols] = jnp.where(live, r[:TOK], 0.0).astype(BF)
        lb[h, v, u, :, cols] = r[TOK:].astype(BF)
        load_in(k).start()
        return carry

    lax.fori_loop(0, 4, step_out, 0)
    pl.semaphore_wait(barrier, len(peers))
    for d in range(1, 4):
        part = lb.at[h, v, u]
        send(part, part, S_L1 + d - 1, dev(d, 0))
    send(gbuf.at[own_rows], gbuf.at[own_rows], S_SWAP_G, sibling)

    rows_of[0].wait()
    rows_of[1].wait()

    def swap_i(k):
        return copy(send_i.at[k], ibuf.at[k, own_rows], S_SWAP_I + k, sibling)

    def step_in(k, carry):
        load_in(k).wait()
        r = dot(xin[...], basis[k], NN).astype(BF)
        at = dot(r[TOK:], spread, TN).astype(BF).reshape(16, 16, 128)

        @pl.when(k < 2)
        def _():
            send_i[k] = r[:TOK]
            at_send[k] = at

        @pl.when(k >= 2)
        def _():
            ibuf[k - 2, own_rows] = r[:TOK]
            a_own[h, k - 2] = at

        return carry

    lax.fori_loop(0, 2, step_in, 0)
    for k in range(2):
        pending.append(swap_i(k))
        pending[-1].start()
    send(at_send, a_own.at[h], S_SWAP_A, sibling)
    lax.fori_loop(2, 4, step_in, 0)
    for d in range(1, 4):
        part = lb.at[h, v, u]
        copy(part, part, S_L1 + d - 1, dev(d, 0)).wait_recv()
    for d in range(1, 4):
        send(lb.at[h, v], lb.at[h, v], S_L2 + d - 1, dev(0, d))
    for k in range(2):
        swap_i(k).wait_recv()
    send(ibuf.at[0], ibuf.at[2], S_Y_I + 0, dev_y(1))
    send(ibuf.at[1], ibuf.at[3], S_Y_I + 1, dev_y(3))
    send(ibuf.at[1], ibuf.at[4], S_Y_I + 2, dev_y(1))
    send(ibuf.at[0], ibuf.at[5], S_Y_I + 3, dev_y(3))

    copy(at_send, a_own.at[1 - h], S_SWAP_A, sibling).wait_recv()
    for d in range(1, 4):
        there = pl.ds(((u + d) % 4) * 4, 4)
        send(a_own.at[:, :, there], a_mid.at[u], S_A1 + d - 1, dev(d, 0))
    a_mid[u] = a_own[:, :, pl.ds(u * 4, 4)]
    copy(gbuf.at[own_rows], gbuf.at[own_rows], S_SWAP_G, sibling).wait_recv()

    damp_1[0] = jnp.zeros((8, 128), F32)
    group = lax.broadcasted_iota(jnp.int32, (128, 128), 1) // RANK

    def place(i):
        first = (i < 2) * 1
        last = (i >= 6) * 1
        mid = 1 - first - last
        back = 1 - i % 2
        sigma = (y + last * 2 + mid * (back * 3 + (1 - back))) % 4
        k = (first + last) * (i % 2) + mid * ((i == 3) * 1 + (i == 4) * 1)
        return sigma * 2 + k

    def rows64(uu):
        return pl.ds(pl.multiple_of((uu % 4) * 64, 64), 64)

    def far_copies(i):
        over = (u + 2) % 4
        return (
            copy(snd.at[i, pl.ds(pl.multiple_of(over * 64, 64), 32)], far.at[i, 0], S_FAR + 2 * i, dev(1, 0)),
            copy(snd.at[i, pl.ds(pl.multiple_of(over * 64 + 32, 32), 32)], far.at[i, 1], S_FAR + 2 * i + 1, dev(3, 0)),
        )

    def near_copies(i):
        return (
            copy(snd.at[i, rows64(u + 1)], near.at[i, 0], S_NEAR + 2 * i, dev(1, 0)),
            copy(snd.at[i, rows64(u + 3)], near.at[i, 1], S_NEAR + 2 * i + 1, dev(3, 0)),
        )

    def out2_copies(i):
        return [
            copy(snd2.at[i, (v + d) % 4], got2.at[i, d - 1], S_OUT2 + 3 * i + d - 1, dev(0, d)) for d in (2, 1, 3)
        ]

    def relay(i):
        return copy(ibuf.at[i], ibuf.at[i + 4], S_Y_I + i + 2, dev_y(1 + 2 * (i - 2)))

    def stage_squares(i):
        @pl.when(i >= 2)
        def _():
            copy(ibuf.at[i], ibuf.at[i], S_Y_I + i - 2, dev_y(1)).wait_recv()

        @pl.when((i == 2) | (i == 3))
        def _():
            relay(i).start()

        for n in range(4):
            r = dot(ibuf[i, n * RLEN : (n + 1) * RLEN], gbuf[n * RLEN : (n + 1) * RLEN], TN)
            if n == 0:
                acc[i % RING] = r * r
            else:
                acc[i % RING] += r * r
        total = acc[i % RING].reshape(32, 8, WIDTH).sum(axis=0)
        for n in range(WIDTH // 128):
            damp_1[0] += total[:, n * 128 : (n + 1) * 128]
        over = rows64(u + 2)
        snd[i, over] = acc[i % RING, over].astype(BF)
        for c in far_copies(i):
            c.start()

    def stage_near(i):
        for c in far_copies(i):
            c.wait_recv()
        a = pl.multiple_of(((u + 1) % 4) * 64, 64)
        snd[i, pl.ds(a, 32)] = (acc[i % RING, pl.ds(a, 32)] + far[i, 0].astype(F32)).astype(BF)
        snd[i, pl.ds(a + 32, 32)] = acc[i % RING, pl.ds(a + 32, 32)].astype(BF)
        b = pl.multiple_of(((u + 3) % 4) * 64, 64)
        snd[i, pl.ds(b, 32)] = acc[i % RING, pl.ds(b, 32)].astype(BF)
        snd[i, pl.ds(b + 32, 32)] = (acc[i % RING, pl.ds(b + 32, 32)] + far[i, 1].astype(F32)).astype(BF)
        for c in near_copies(i):
            c.start()

    def own16(vv):
        return pl.ds(pl.multiple_of(u * 64 + (vv % 4) * 16, 16), 16)

    def stage_out2(i):
        for c in near_copies(i):
            c.wait_recv()
        mine64 = rows64(u)
        total = acc[i % RING, mine64] + near[i, 0].astype(F32) + near[i, 1].astype(F32)
        acc[i % RING, mine64] = total
        corr[place(i)] = acc[i % RING, own16(v)]
        snd2[i] = total.astype(BF).reshape(4, 16, WIDTH)
        for c in out2_copies(i):
            c.start()

    def stage_last(i, carry):
        for c in out2_copies(i):
            c.wait_recv()
        got = got2[i, 0].astype(F32) + got2[i, 1].astype(F32) + got2[i, 2].astype(F32)
        corr[place(i)] = 1.0 / ((corr[place(i)] + got) / 64.0 + damping)
        return carry

    def query_second():
        for d in range(1, 4):
            copy(a_own.at[:, :, pl.ds(0, 4)], a_mid.at[u], S_A1 + d - 1, dev(d, 0)).wait_recv()
        for d in range(1, 4):
            copy(a_mid.at[:, :, :, (v + d) % 4], a_recv.at[v], S_A2 + d - 1, dev(0, d)).start()
        a_recv[v] = a_mid[:, :, :, v]

    def query_third():
        for d in range(1, 4):
            copy(lb.at[h, v], lb.at[h, v], S_L2 + d - 1, dev(0, d)).wait_recv()
        copy(lb.at[h], lb.at[h], S_LS, sibling).start()
        for d in range(1, 4):
            copy(a_mid.at[:, :, :, v], a_recv.at[v], S_A2 + d - 1, dev(0, d)).wait_recv()
        for other in range(2):
            for vv in range(4):
                same = 1 - (other - h) * (other - h)
                total = jnp.zeros((32, 128), F32)
                for uu in range(4):
                    first = same * vv + (1 - same) * uu
                    second = same * uu + (1 - same) * vv
                    total = total + a_recv[first, second, other].reshape(32, 128).astype(F32)
                a4[y, other * 4 + vv] = total.astype(BF)
        for d in range(1, 4):
            copy(a4.at[y], a4.at[y], S_AY + d - 1, dev_y(d)).start()

    def plane_rows(yy):
        return lb[yy // 2, pl.ds((yy % 2) * 2, 2)].reshape(256, WIDTH)

    def gram_products():
        copy(lb.at[h], lb.at[1 - h], S_LS, sibling).wait_recv()

        def one(yy, carry):
            rows = plane_rows(yy)
            full = dot(rows, rows, NT)
            for e in range(2):
                packed = jnp.zeros((RANK, 128), F32)
                for q in range(4):
                    at = e * 128 + q * RANK
                    packed = packed + jnp.where(lane // RANK == q, full[at : at + RANK, e * 128 : e * 128 + 128], 0.0)
                gram_s[yy, e] = packed
            return carry

        lax.fori_loop(0, 4, one, 0)
        for d in (2, 1, 3):
            there = (y + d) % 4
            copy(gram_s.at[there], gram_r.at[d - 1], S_GRAM + d - 1, dev_y(d)).start()

    def left_products():
        def one(yy, carry):
            left_s[yy] = dot(gbuf[own_rows], plane_rows(yy), NT)
            return carry

        lax.fori_loop(0, 4, one, 0)
        for d in (2, 1, 3):
            there = (y + d) % 4
            copy(left_s.at[there], left_r.at[d - 1], S_LEFT + d - 1, dev_y(d)).start()

    def rotate(g):
        a = a4[:, g].reshape(128, 128)
        a_all = jnp.concatenate([jnp.where(group == q, a, jnp.zeros_like(a)) for q in range(4)], axis=0)
        rotated[g] = dot(a_all, lb[g // 4, g % 4].reshape(128, WIDTH), NN)

    def damping_first():
        for n, (dy, dh) in enumerate(line):
            copy(damp_1.at[0], damp_1.at[1 + n], S_D1 + n, dev_y(dy, dh)).start()

    def damping_second():
        for n, (dy, dh) in enumerate(line):
            copy(damp_1.at[0], damp_1.at[1 + n], S_D1 + n, dev_y(dy, dh)).wait_recv()
        damp_2[0] = damp_1[...].sum(axis=0)
        for d in range(1, 4):
            copy(damp_2.at[0], damp_2.at[d], S_D2 + d - 1, dev(d, 0)).start()

    def damping_third():
        for d in range(1, 4):
            copy(damp_2.at[0], damp_2.at[d], S_D2 + d - 1, dev(d, 0)).wait_recv()
        damp_3[0] = damp_2[...].sum(axis=0)
        for d in range(1, 4):
            copy(damp_3.at[0], damp_3.at[d], S_D3 + d - 1, dev(0, d)).start()

    lane2 = lax.broadcasted_iota(jnp.int32, (128, 128), 1)
    sub2 = lax.broadcasted_iota(jnp.int32, (128, 128), 0)

    def fold_block():
        fold = ((sub2 % RANK == lane2) & (lane2 < RANK)).astype(F32)
        return fold, sub2 // RANK == lane2 // RANK

    def gram_begin():
        for d in range(1, 4):
            copy(gram_s.at[y], gram_r.at[d - 1], S_GRAM + d - 1, dev_y(d)).wait_recv()
        gram = gram_s[y] + gram_r[0] + gram_r[1] + gram_r[2]
        fold, block = fold_block()
        wide = []
        for e in range(2):
            tall = jnp.concatenate([gram[e]] * 4, axis=0)
            wide.append(dot(jnp.where(block, tall, 0.0), fold, NN, HIGH).reshape(4, RANK, 128))
        w = jnp.concatenate(wide, axis=0)
        li = lax.broadcasted_iota(jnp.int32, (8, RANK, 128), 2)
        ri = lax.broadcasted_iota(jnp.int32, (8, RANK, 128), 1)
        inv_w[...] = w + jnp.where(li == ri, ridge_share * DIM, 0.0)

    def gram_sweep(first, last):
        li = lax.broadcasted_iota(jnp.int32, (8, RANK, 128), 2)
        ri = lax.broadcasted_iota(jnp.int32, (8, RANK, 128), 1)

        def sweep(k, w):
            at_k = li == k
            col = jnp.where(at_k, w, 0.0).sum(axis=2, keepdims=True)
            rowk = jnp.where(ri == k, w, 0.0).sum(axis=1, keepdims=True)
            pivot = jnp.where(at_k[:, :1], rowk, 0.0).sum(axis=2, keepdims=True)
            rowk = jnp.where(at_k[:, :1], 1.0, rowk) / pivot
            return jnp.where(ri == k, rowk, jnp.where(at_k, 0.0, w) - col * rowk)

        inv_w[...] = lax.fori_loop(first, last, sweep, inv_w[...])

    def gram_end():
        fold, block = fold_block()
        for e in range(2):
            flat = inv_w[e * 4 : (e + 1) * 4].reshape(128, 128)
            inv_bd[e] = jnp.where(block, dot(flat, fold, NT, HIGH), 0.0)

    def left_sum():
        for d in range(1, 4):
            copy(left_s.at[y], left_r.at[d - 1], S_LEFT + d - 1, dev_y(d)).wait_recv()
        left_f[own_rows] = left_s[y] + left_r[0] + left_r[1] + left_r[2]
        copy(left_f.at[own_rows], left_f.at[own_rows], S_LEFTS, sibling).start()

    def selection():
        p = lax.broadcasted_iota(jnp.int32, (256, 128), 0) // RANK + y * 8
        hh, first, second = p // 16, p % 4, (p // 4) % 4
        xx = first * (1 - hh) + second * hh
        zz = second * (1 - hh) + first * hh
        pick[...] = (lax.broadcasted_iota(jnp.int32, (256, 128), 1) == xx * 8 + zz * 2 + hh).astype(F32)

    def rotate_ready():
        for d in range(1, 4):
            copy(a4.at[y], a4.at[y], S_AY + d - 1, dev_y(d)).wait_recv()

    def step(i, carry):
        @pl.when(i >= 3)
        def _():
            stage_near(i - 3)

        @pl.when(i >= 5)
        def _():
            stage_out2(i - 5)

        stage_squares(i)

        pl.when(i == 1)(query_second)
        pl.when(i == 3)(query_third)
        pl.when(i == 5)(gram_products)
        pl.when(i == 7)(damping_first)
        return carry

    def rotate_some(g, carry):
        rotate(g)
        return carry

    lax.fori_loop(0, PARTS, step, 0)
    stage_near(PARTS - 3)
    stage_near(PARTS - 2)
    stage_out2(PARTS - 5)
    stage_out2(PARTS - 4)
    left_products()
    stage_near(PARTS - 1)
    stage_out2(PARTS - 3)
    damping_second()
    gram_begin()
    gram_sweep(0, 12)
    stage_out2(PARTS - 2)
    damping_third()
    rotate_ready()
    lax.fori_loop(0, 3, rotate_some, 0)
    stage_out2(PARTS - 1)
    lax.fori_loop(3, 8, rotate_some, 0)
    gram_sweep(12, 32)
    gram_end()
    selection()

    for d in range(1, 4):
        copy(damp_3.at[0], damp_3.at[d], S_D3 + d - 1, dev(0, d)).wait_recv()
    damping = damping_share * (jnp.sum(damp_3[...]) / 64.0 / (DIM * DIM)) + epsilon_add
    lax.fori_loop(0, PARTS, stage_last, 0)

    def proj_copy(e, d):
        there = (y + d) % 4
        return copy(proj_s.at[there, e], proj_r.at[d - 1, e], S_PROJ + 3 * e + d - 1, dev_y(d))

    def solve_group(n, carry):
        e, m = n // 4, n % 4
        d = (m == 0) * 2 + (m == 1) * 1 + (m == 2) * 3
        there = (y + d) % 4
        g = there * 2 + e
        rows = lb[g // 4, g % 4].reshape(128, WIDTH)
        weight = corr[...].reshape(1, 128, WIDTH)
        scaled = (rotated[g].reshape(4, 128, WIDTH) * weight).reshape(512, WIDTH).astype(BF)
        p = dot(scaled, rows, NT)
        packed = jnp.zeros((128, 128), F32)
        for q in range(4):
            packed = packed + jnp.where(group == q, p[q * 128 : (q + 1) * 128], 0.0)
        proj_s[there, e] = packed

        @pl.when(m < 3)
        def _():
            proj_copy(e, d).start()

        return carry

    lax.fori_loop(0, 8, solve_group, 0)
    left_sum()

    mine = pl.ds(pl.multiple_of(me * 16, 16), 16)

    def solved_first(e, d):
        return copy(sb.at[e, :, mine], sb.at[e, :, mine], S_S1 + 3 * e + d - 1, dev(0, d))

    def solved_second(e, d):
        part = sb.at[e, :, pl.ds(pl.multiple_of(u * 64, 64), 64)]
        return copy(part, part, S_S2 + 3 * e + d - 1, dev(d, 0))

    for e in range(2):
        for d in range(1, 4):
            proj_copy(e, d).wait_recv()
        whole = proj_s[y, e] + proj_r[0, e] + proj_r[1, e] + proj_r[2, e]
        solved = dot(whole, inv_bd[e], NN, HIGH).astype(BF)
        sb[e, :, mine] = solved.reshape(PARTS, 16, 128)
        for d in (2, 1, 3):
            solved_first(e, d).start()
    for e in range(2):
        for d in range(1, 4):
            solved_first(e, d).wait_recv()
        for d in (2, 1, 3):
            solved_second(e, d).start()

    for c in pending:
        c.wait_send()

    def leave(k, carry):
        @pl.when(k < 2)
        def _():
            relay(k + 2).wait_send()

        for c in far_copies(k) + near_copies(k):
            c.wait_send()
        for c in out2_copies(k):
            c.wait_send()
        return carry

    lax.fori_loop(0, PARTS, leave, 0)
    for d in range(1, 4):
        copy(a_mid.at[:, :, :, (v + d) % 4], a_recv.at[v], S_A2 + d - 1, dev(0, d)).wait_send()
        copy(a4.at[y], a4.at[y], S_AY + d - 1, dev_y(d)).wait_send()
        copy(gram_s.at[y], gram_r.at[d - 1], S_GRAM + d - 1, dev_y(d)).wait_send()
        copy(left_s.at[y], left_r.at[d - 1], S_LEFT + d - 1, dev_y(d)).wait_send()
        copy(damp_2.at[0], damp_2.at[d], S_D2 + d - 1, dev(d, 0)).wait_send()
        copy(damp_3.at[0], damp_3.at[d], S_D3 + d - 1, dev(0, d)).wait_send()
        for e in range(2):
            proj_copy(e, d).wait_send()
            solved_first(e, d).wait_send()
    copy(lb.at[h], lb.at[h], S_LS, sibling).wait_send()
    copy(left_f.at[own_rows], left_f.at[own_rows], S_LEFTS, sibling).wait_send()
    for n, (dy, dh) in enumerate(line):
        copy(damp_1.at[0], damp_1.at[1 + n], S_D1 + n, dev_y(dy, dh)).wait_send()

    copy(left_f.at[own_rows], left_f.at[own_rows], S_LEFTS, sibling).wait_recv()
    joined = []
    for e in range(2):
        for d in range(1, 4):
            solved_second(e, d).wait_recv()

        right = jnp.zeros((2 * TOK, 128), F32)
        for i in range(PARTS):
            right = right + dot(ibuf[i], sb[e, place(i)], NN)
        joined.append((left_f[:, e * 128 : (e + 1) * 128] * right).reshape(4, RLEN, 128).sum(axis=1))
    joined = jnp.concatenate([jnp.concatenate(joined, axis=1), jnp.zeros((4, 256), F32)], axis=0)
    fin[y, h] = dot(joined, pick[...], NN, HIGH)
    for n, (dy, dh) in enumerate(line):
        copy(fin.at[y, h], fin.at[y, h], S_FIN + n, dev_y(dy, dh)).start()
    for n, (dy, dh) in enumerate(line):
        copy(fin.at[y, h], fin.at[y, h], S_FIN + n, dev_y(dy, dh)).wait_recv()
    scores = fin[...].reshape(8, 8, 128).sum(axis=0) / RLEN
    out[...] = jnp.where(h == 0, scores[0:2, :32], scores[2:4, :32])
    for e in range(2):
        for d in range(1, 4):
            solved_second(e, d).wait_send()
    for n, (dy, dh) in enumerate(line):
        copy(fin.at[y, h], fin.at[y, h], S_FIN + n, dev_y(dy, dh)).wait_send()


def shards(act, grad, lengths, basis_in, basis_out, query_act, query_grad):
    vm = pltpu.VMEM
    anywhere = pl.BlockSpec(memory_space=pl.ANY)
    return pl.pallas_call(
        kernel,
        out_shape=jax.ShapeDtypeStruct((2, 32), F32),
        in_specs=[anywhere, anywhere, pl.BlockSpec(memory_space=pltpu.SMEM)] + [anywhere] * 4,
        out_specs=pl.BlockSpec(memory_space=pltpu.VMEM),
        scratch_shapes=[
            vm((TOK + RANK, DIM), BF),
            vm((TOK + RANK, DIM), BF),
            vm((4, DIM, 256), BF),
            vm((2, TOK, 256), BF),
            vm((PARTS, 2 * TOK, 256), BF),
            vm((2 * TOK, WIDTH), BF),
            vm((2, 4, 4, RANK, WIDTH), BF),
            vm((2, 16, 16, 128), BF),
            vm((2, 2, 16, 16, 128), BF),
            vm((4, 2, 2, 4, 16, 128), BF),
            vm((4, 4, 2, 2, 16, 128), BF),
            vm((4, 8, 32, 128), BF),
            vm((RING, 256, WIDTH), F32),
            vm((PARTS, 256, WIDTH), BF),
            vm((PARTS, 2, 32, WIDTH), BF),
            vm((PARTS, 2, 64, WIDTH), BF),
            vm((PARTS, 4, 16, WIDTH), BF),
            vm((PARTS, 3, 16, WIDTH), BF),
            vm((PARTS, 16, WIDTH), F32),
            vm((4, 2, RANK, 128), F32),
            vm((3, 2, RANK, 128), F32),
            vm((4, TOK, 256), F32),
            vm((3, TOK, 256), F32),
            vm((2 * TOK, 256), F32),
            vm((8, 8, 128), F32),
            vm((4, 8, 128), F32),
            vm((4, 8, 128), F32),
            vm((8, RANK, 128), F32),
            vm((2, 128, 128), F32),
            vm((8, 512, WIDTH), F32),
            vm((4, 2, 128, 128), F32),
            vm((3, 2, 128, 128), F32),
            vm((2, PARTS, 256, 128), BF),
            vm((256, 128), F32),
            vm((4, 2, 8, 128), F32),
            pltpu.SemaphoreType.DMA((12,)),
            pltpu.SemaphoreType.DMA((N_SEM,)),
            pltpu.SemaphoreType.DMA((N_SEM,)),
        ],
        compiler_params=pltpu.CompilerParams(
            collective_id=0, has_side_effects=True, vmem_limit_bytes=60 * 2**20
        ),
    )(act, grad, lengths, basis_in, basis_out, query_act, query_grad)


def solution(mesh):
    return jax.shard_map(
        shards,
        mesh=mesh,
        in_specs=(
            P("dp", None),
            P("dp", None),
            P("dp"),
            P(None, "col"),
            P(None, "col"),
            P("dp", None),
            P("dp", None),
        ),
        out_specs=P("dp", None),
        check_vma=False,
    )
```

```python
import functools

import jax
import jax.numpy as jnp
from jax import lax
from jax.experimental import pallas as pl
from jax.experimental.pallas import tpu as pltpu
from jax.sharding import PartitionSpec as P


RLEN = 128
RANK = 32
DIM = 4096
WIDTH = 1024
TOK = 256
RING = 5
PARTS = 8
damping_share = 0.1
ridge_share = 0.05
epsilon_add = 1e-06
BF = jnp.bfloat16
F32 = jnp.float32
MESH = pl.DeviceIdType.MESH
HIGH = lax.Precision.HIGHEST


def dot(a, b, dims, precision=None):
    return lax.dot_general(a, b, (dims, ((), ())), preferred_element_type=F32, precision=precision)


NN = ((1,), (0,))
TN = ((0,), (0,))
NT = ((1,), (1,))


class Slots:
    def __init__(self):
        self.count = 0

    def take(self, n):
        first = self.count
        self.count += n
        return first


SL = Slots()
S_SWAP_I = SL.take(2)
S_SWAP_A = SL.take(1)
S_SWAP_G = SL.take(1)
S_Y_I = SL.take(6)
S_L1 = SL.take(3)
S_L2 = SL.take(3)
S_LS = SL.take(1)
S_A1 = SL.take(3)
S_A2 = SL.take(3)
S_AY = SL.take(3)
S_FAR = SL.take(2 * PARTS)
S_NEAR = SL.take(2 * PARTS)
S_OUT2 = SL.take(3 * PARTS)
S_GRAM = SL.take(3)
S_LEFT = SL.take(3)
S_LEFTS = SL.take(1)
S_D1 = SL.take(7)
S_D2 = SL.take(3)
S_D3 = SL.take(3)
S_PROJ = SL.take(6)
S_S1 = SL.take(6)
S_S2 = SL.take(6)
S_FIN = SL.take(7)
N_SEM = SL.count


def kernel(
    act, grad, lens, b_in, b_out, q_act, q_grad,
    out,
    xin, xout, basis, send_i, ibuf, gbuf, lb, at_send, a_own, a_mid, a_recv, a4,
    acc, snd, far, near, snd2, got2, corr,
    gram_s, gram_r, left_s, left_r, left_f, damp_1, damp_2, damp_3, inv_w, inv_bd, rotated, proj_s, proj_r, sb, pick, fin,
    load_sem, ss, rs,
):
    dp = lax.axis_index("dp")
    y = lax.axis_index("col")
    x, z, h = dp // 8, (dp // 2) % 4, dp % 2
    u = x * (1 - h) + z * h
    v = z * (1 - h) + x * h
    me = u * 4 + v

    def dev_xz(xx, zz, hh, yy):
        return ((xx % 4) * 8 + (zz % 4) * 2 + hh, yy % 4)

    def dev(du, dv):
        uu, vv = u + du, v + dv
        return dev_xz(uu * (1 - h) + vv * h, vv * (1 - h) + uu * h, h, y)

    def dev_y(dy, dh=0):
        return dev_xz(x, z, (h + dh) % 2, y + dy)

    sibling = dev_y(0, 1)
    pending = []

    def copy(src, dst, idx, to):
        return pltpu.make_async_remote_copy(
            src_ref=src, dst_ref=dst, send_sem=ss.at[idx], recv_sem=rs.at[idx], device_id=to, device_id_type=MESH
        )

    def send(src, dst, idx, to):
        c = copy(src, dst, idx, to)
        c.start()
        pending.append(c)

    def tile_in(k):
        half = (1 - h) * (1 - k // 2) + h * (k // 2)
        return half * 2 + k % 2

    def load_in(k):
        cols = pl.ds(pl.multiple_of(tile_in(k) * 256, 256), 256)
        return pltpu.make_async_copy(b_in.at[:, cols], basis.at[k], load_sem.at[4 + k])

    def load_out(k):
        cols = pl.ds(pl.multiple_of(k * 256, 256), 256)
        return pltpu.make_async_copy(b_out.at[:, cols], basis.at[k], load_sem.at[8 + k])

    rows_of = [
        pltpu.make_async_copy(act, xin.at[pl.ds(0, TOK)], load_sem.at[0]),
        pltpu.make_async_copy(q_act, xin.at[pl.ds(TOK, RANK)], load_sem.at[1]),
        pltpu.make_async_copy(grad, xout.at[pl.ds(0, TOK)], load_sem.at[2]),
        pltpu.make_async_copy(q_grad, xout.at[pl.ds(TOK, RANK)], load_sem.at[3]),
    ]
    rows_of[2].start()
    rows_of[3].start()
    for k in range(4):
        load_out(k).start()
    rows_of[0].start()
    rows_of[1].start()

    line = [(dy, dh) for dy in range(4) for dh in range(2) if dy or dh]
    barrier = pltpu.get_barrier_semaphore()
    peers = [dev(d, 0) for d in range(1, 4)] + [dev(0, d) for d in range(1, 4)] + [dev_y(dy, dh) for dy, dh in line]
    for to in peers:
        pl.semaphore_signal(barrier, inc=1, device_id=to, device_id_type=MESH)

    lane = lax.broadcasted_iota(jnp.int32, (RANK, 128), 1)
    spread = (lane == lax.broadcasted_iota(jnp.int32, (RANK, 128), 0) + RANK * u).astype(BF)

    own_rows = pl.ds(pl.multiple_of(h * TOK, TOK), TOK)

    rows_of[2].wait()
    rows_of[3].wait()
    row = lax.broadcasted_iota(jnp.int32, (TOK, 256), 0)
    live = (row < lens[0]) | ((row >= RLEN) & (row < RLEN + lens[1]))

    def step_out(k, carry):
        load_out(k).wait()
        cols = pl.ds(pl.multiple_of(k * 256, 256), 256)
        r = dot(xout[...], basis[k], NN)
        gbuf[own_rows, cols] = jnp.where(live, r[:TOK], 0.0).astype(BF)
        lb[h, v, u, :, cols] = r[TOK:].astype(BF)
        load_in(k).start()
        return carry

    lax.fori_loop(0, 4, step_out, 0)
    pl.semaphore_wait(barrier, len(peers))
    for d in range(1, 4):
        part = lb.at[h, v, u]
        send(part, part, S_L1 + d - 1, dev(d, 0))
    send(gbuf.at[own_rows], gbuf.at[own_rows], S_SWAP_G, sibling)

    rows_of[0].wait()
    rows_of[1].wait()

    def swap_i(k):
        return copy(send_i.at[k], ibuf.at[k, own_rows], S_SWAP_I + k, sibling)

    def step_in(k, carry):
        load_in(k).wait()
        r = dot(xin[...], basis[k], NN).astype(BF)
        at = dot(r[TOK:], spread, TN).astype(BF).reshape(16, 16, 128)

        @pl.when(k < 2)
        def _():
            send_i[k] = r[:TOK]
            at_send[k] = at

        @pl.when(k >= 2)
        def _():
            ibuf[k - 2, own_rows] = r[:TOK]
            a_own[h, k - 2] = at

        return carry

    lax.fori_loop(0, 2, step_in, 0)
    for k in range(2):
        pending.append(swap_i(k))
        pending[-1].start()
    send(at_send, a_own.at[h], S_SWAP_A, sibling)
    lax.fori_loop(2, 4, step_in, 0)
    for d in range(1, 4):
        part = lb.at[h, v, u]
        copy(part, part, S_L1 + d - 1, dev(d, 0)).wait_recv()
    for d in range(1, 4):
        send(lb.at[h, v], lb.at[h, v], S_L2 + d - 1, dev(0, d))
    for k in range(2):
        swap_i(k).wait_recv()
    send(ibuf.at[0], ibuf.at[2], S_Y_I + 0, dev_y(1))
    send(ibuf.at[1], ibuf.at[3], S_Y_I + 1, dev_y(3))
    send(ibuf.at[1], ibuf.at[4], S_Y_I + 2, dev_y(1))
    send(ibuf.at[0], ibuf.at[5], S_Y_I + 3, dev_y(3))

    copy(at_send, a_own.at[1 - h], S_SWAP_A, sibling).wait_recv()
    for d in range(1, 4):
        there = pl.ds(((u + d) % 4) * 4, 4)
        send(a_own.at[:, :, there], a_mid.at[u], S_A1 + d - 1, dev(d, 0))
    a_mid[u] = a_own[:, :, pl.ds(u * 4, 4)]
    copy(gbuf.at[own_rows], gbuf.at[own_rows], S_SWAP_G, sibling).wait_recv()

    damp_1[0] = jnp.zeros((8, 128), F32)
    group = lax.broadcasted_iota(jnp.int32, (128, 128), 1) // RANK

    def place(i):
        first = (i < 2) * 1
        last = (i >= 6) * 1
        mid = 1 - first - last
        back = 1 - i % 2
        sigma = (y + last * 2 + mid * (back * 3 + (1 - back))) % 4
        k = (first + last) * (i % 2) + mid * ((i == 3) * 1 + (i == 4) * 1)
        return sigma * 2 + k

    def rows64(uu):
        return pl.ds(pl.multiple_of((uu % 4) * 64, 64), 64)

    def far_copies(i):
        over = (u + 2) % 4
        return (
            copy(snd.at[i, pl.ds(pl.multiple_of(over * 64, 64), 32)], far.at[i, 0], S_FAR + 2 * i, dev(1, 0)),
            copy(snd.at[i, pl.ds(pl.multiple_of(over * 64 + 32, 32), 32)], far.at[i, 1], S_FAR + 2 * i + 1, dev(3, 0)),
        )

    def near_copies(i):
        return (
            copy(snd.at[i, rows64(u + 1)], near.at[i, 0], S_NEAR + 2 * i, dev(1, 0)),
            copy(snd.at[i, rows64(u + 3)], near.at[i, 1], S_NEAR + 2 * i + 1, dev(3, 0)),
        )

    def out2_copies(i):
        return [
            copy(snd2.at[i, (v + d) % 4], got2.at[i, d - 1], S_OUT2 + 3 * i + d - 1, dev(0, d)) for d in (2, 1, 3)
        ]

    def relay(i):
        return copy(ibuf.at[i], ibuf.at[i + 4], S_Y_I + i + 2, dev_y(1 + 2 * (i - 2)))

    def stage_squares(i):
        @pl.when(i >= 2)
        def _():
            copy(ibuf.at[i], ibuf.at[i], S_Y_I + i - 2, dev_y(1)).wait_recv()

        @pl.when((i == 2) | (i == 3))
        def _():
            relay(i).start()

        for n in range(4):
            r = dot(ibuf[i, n * RLEN : (n + 1) * RLEN], gbuf[n * RLEN : (n + 1) * RLEN], TN)
            if n == 0:
                acc[i % RING] = r * r
            else:
                acc[i % RING] += r * r
        total = acc[i % RING].reshape(32, 8, WIDTH).sum(axis=0)
        for n in range(WIDTH // 128):
            damp_1[0] += total[:, n * 128 : (n + 1) * 128]
        over = rows64(u + 2)
        snd[i, over] = acc[i % RING, over].astype(BF)
        for c in far_copies(i):
            c.start()

    def stage_near(i):
        for c in far_copies(i):
            c.wait_recv()
        a = pl.multiple_of(((u + 1) % 4) * 64, 64)
        snd[i, pl.ds(a, 32)] = (acc[i % RING, pl.ds(a, 32)] + far[i, 0].astype(F32)).astype(BF)
        snd[i, pl.ds(a + 32, 32)] = acc[i % RING, pl.ds(a + 32, 32)].astype(BF)
        b = pl.multiple_of(((u + 3) % 4) * 64, 64)
        snd[i, pl.ds(b, 32)] = acc[i % RING, pl.ds(b, 32)].astype(BF)
        snd[i, pl.ds(b + 32, 32)] = (acc[i % RING, pl.ds(b + 32, 32)] + far[i, 1].astype(F32)).astype(BF)
        for c in near_copies(i):
            c.start()

    def own16(vv):
        return pl.ds(pl.multiple_of(u * 64 + (vv % 4) * 16, 16), 16)

    def stage_out2(i):
        for c in near_copies(i):
            c.wait_recv()
        mine64 = rows64(u)
        total = acc[i % RING, mine64] + near[i, 0].astype(F32) + near[i, 1].astype(F32)
        acc[i % RING, mine64] = total
        corr[place(i)] = acc[i % RING, own16(v)]
        snd2[i] = total.astype(BF).reshape(4, 16, WIDTH)
        for c in out2_copies(i):
            c.start()

    def stage_last(i, carry):
        for c in out2_copies(i):
            c.wait_recv()
        got = got2[i, 0].astype(F32) + got2[i, 1].astype(F32) + got2[i, 2].astype(F32)
        corr[place(i)] = 1.0 / ((corr[place(i)] + got) / 64.0 + damping)
        return carry

    def query_second():
        for d in range(1, 4):
            copy(a_own.at[:, :, pl.ds(0, 4)], a_mid.at[u], S_A1 + d - 1, dev(d, 0)).wait_recv()
        for d in range(1, 4):
            copy(a_mid.at[:, :, :, (v + d) % 4], a_recv.at[v], S_A2 + d - 1, dev(0, d)).start()
        a_recv[v] = a_mid[:, :, :, v]

    def query_third():
        for d in range(1, 4):
            copy(lb.at[h, v], lb.at[h, v], S_L2 + d - 1, dev(0, d)).wait_recv()
        copy(lb.at[h], lb.at[h], S_LS, sibling).start()
        for d in range(1, 4):
            copy(a_mid.at[:, :, :, v], a_recv.at[v], S_A2 + d - 1, dev(0, d)).wait_recv()
        for other in range(2):
            for vv in range(4):
                same = 1 - (other - h) * (other - h)
                total = jnp.zeros((32, 128), F32)
                for uu in range(4):
                    first = same * vv + (1 - same) * uu
                    second = same * uu + (1 - same) * vv
                    total = total + a_recv[first, second, other].reshape(32, 128).astype(F32)
                a4[y, other * 4 + vv] = total.astype(BF)
        for d in range(1, 4):
            copy(a4.at[y], a4.at[y], S_AY + d - 1, dev_y(d)).start()

    def plane_rows(yy):
        return lb[yy // 2, pl.ds((yy % 2) * 2, 2)].reshape(256, WIDTH)

    def gram_products():
        copy(lb.at[h], lb.at[1 - h], S_LS, sibling).wait_recv()

        def one(yy, carry):
            rows = plane_rows(yy)
            full = dot(rows, rows, NT)
            for e in range(2):
                packed = jnp.zeros((RANK, 128), F32)
                for q in range(4):
                    at = e * 128 + q * RANK
                    packed = packed + jnp.where(lane // RANK == q, full[at : at + RANK, e * 128 : e * 128 + 128], 0.0)
                gram_s[yy, e] = packed
            return carry

        lax.fori_loop(0, 4, one, 0)
        for d in (2, 1, 3):
            there = (y + d) % 4
            copy(gram_s.at[there], gram_r.at[d - 1], S_GRAM + d - 1, dev_y(d)).start()

    def left_products():
        def one(yy, carry):
            left_s[yy] = dot(gbuf[own_rows], plane_rows(yy), NT)
            return carry

        lax.fori_loop(0, 4, one, 0)
        for d in (2, 1, 3):
            there = (y + d) % 4
            copy(left_s.at[there], left_r.at[d - 1], S_LEFT + d - 1, dev_y(d)).start()

    def rotate(g):
        a = a4[:, g].reshape(128, 128)
        a_all = jnp.concatenate([jnp.where(group == q, a, jnp.zeros_like(a)) for q in range(4)], axis=0)
        rotated[g] = dot(a_all, lb[g // 4, g % 4].reshape(128, WIDTH), NN)

    def damping_first():
        for n, (dy, dh) in enumerate(line):
            copy(damp_1.at[0], damp_1.at[1 + n], S_D1 + n, dev_y(dy, dh)).start()

    def damping_second():
        for n, (dy, dh) in enumerate(line):
            copy(damp_1.at[0], damp_1.at[1 + n], S_D1 + n, dev_y(dy, dh)).wait_recv()
        damp_2[0] = damp_1[...].sum(axis=0)
        for d in range(1, 4):
            copy(damp_2.at[0], damp_2.at[d], S_D2 + d - 1, dev(d, 0)).start()

    def damping_third():
        for d in range(1, 4):
            copy(damp_2.at[0], damp_2.at[d], S_D2 + d - 1, dev(d, 0)).wait_recv()
        damp_3[0] = damp_2[...].sum(axis=0)
        for d in range(1, 4):
            copy(damp_3.at[0], damp_3.at[d], S_D3 + d - 1, dev(0, d)).start()

    lane2 = lax.broadcasted_iota(jnp.int32, (128, 128), 1)
    sub2 = lax.broadcasted_iota(jnp.int32, (128, 128), 0)

    def fold_block():
        fold = ((sub2 % RANK == lane2) & (lane2 < RANK)).astype(F32)
        return fold, sub2 // RANK == lane2 // RANK

    def gram_begin():
        for d in range(1, 4):
            copy(gram_s.at[y], gram_r.at[d - 1], S_GRAM + d - 1, dev_y(d)).wait_recv()
        gram = gram_s[y] + gram_r[0] + gram_r[1] + gram_r[2]
        fold, block = fold_block()
        wide = []
        for e in range(2):
            tall = jnp.concatenate([gram[e]] * 4, axis=0)
            wide.append(dot(jnp.where(block, tall, 0.0), fold, NN, HIGH).reshape(4, RANK, 128))
        w = jnp.concatenate(wide, axis=0)
        li = lax.broadcasted_iota(jnp.int32, (8, RANK, 128), 2)
        ri = lax.broadcasted_iota(jnp.int32, (8, RANK, 128), 1)
        inv_w[...] = w + jnp.where(li == ri, ridge_share * DIM, 0.0)

    def gram_sweep(first, last):
        li = lax.broadcasted_iota(jnp.int32, (8, RANK, 128), 2)
        ri = lax.broadcasted_iota(jnp.int32, (8, RANK, 128), 1)

        def sweep(k, w):
            at_k = li == k
            col = jnp.where(at_k, w, 0.0).sum(axis=2, keepdims=True)
            rowk = jnp.where(ri == k, w, 0.0).sum(axis=1, keepdims=True)
            pivot = jnp.where(at_k[:, :1], rowk, 0.0).sum(axis=2, keepdims=True)
            rowk = jnp.where(at_k[:, :1], 1.0, rowk) / pivot
            return jnp.where(ri == k, rowk, jnp.where(at_k, 0.0, w) - col * rowk)

        inv_w[...] = lax.fori_loop(first, last, sweep, inv_w[...])

    def gram_end():
        fold, block = fold_block()
        for e in range(2):
            flat = inv_w[e * 4 : (e + 1) * 4].reshape(128, 128)
            inv_bd[e] = jnp.where(block, dot(flat, fold, NT, HIGH), 0.0)

    def left_sum():
        for d in range(1, 4):
            copy(left_s.at[y], left_r.at[d - 1], S_LEFT + d - 1, dev_y(d)).wait_recv()
        left_f[own_rows] = left_s[y] + left_r[0] + left_r[1] + left_r[2]
        copy(left_f.at[own_rows], left_f.at[own_rows], S_LEFTS, sibling).start()

    def selection():
        p = lax.broadcasted_iota(jnp.int32, (256, 128), 0) // RANK + y * 8
        hh, first, second = p // 16, p % 4, (p // 4) % 4
        xx = first * (1 - hh) + second * hh
        zz = second * (1 - hh) + first * hh
        pick[...] = (lax.broadcasted_iota(jnp.int32, (256, 128), 1) == xx * 8 + zz * 2 + hh).astype(F32)

    def rotate_ready():
        for d in range(1, 4):
            copy(a4.at[y], a4.at[y], S_AY + d - 1, dev_y(d)).wait_recv()

    def step(i, carry):
        @pl.when(i >= 3)
        def _():
            stage_near(i - 3)

        @pl.when(i >= 5)
        def _():
            stage_out2(i - 5)

        stage_squares(i)

        pl.when(i == 1)(query_second)
        pl.when(i == 3)(query_third)
        pl.when(i == 5)(gram_products)
        pl.when(i == 7)(damping_first)
        return carry

    def rotate_some(g, carry):
        rotate(g)
        return carry

    lax.fori_loop(0, PARTS, step, 0)
    stage_near(PARTS - 3)
    stage_near(PARTS - 2)
    stage_out2(PARTS - 5)
    stage_out2(PARTS - 4)
    stage_near(PARTS - 1)
    stage_out2(PARTS - 3)
    damping_second()
    left_products()
    gram_begin()
    gram_sweep(0, 12)
    stage_out2(PARTS - 2)
    damping_third()
    rotate_ready()
    lax.fori_loop(0, 3, rotate_some, 0)
    stage_out2(PARTS - 1)
    lax.fori_loop(3, 8, rotate_some, 0)
    gram_sweep(12, 32)
    gram_end()
    selection()

    for d in range(1, 4):
        copy(damp_3.at[0], damp_3.at[d], S_D3 + d - 1, dev(0, d)).wait_recv()
    damping = damping_share * (jnp.sum(damp_3[...]) / 64.0 / (DIM * DIM)) + epsilon_add
    lax.fori_loop(0, PARTS, stage_last, 0)

    def proj_copy(e, d):
        there = (y + d) % 4
        return copy(proj_s.at[there, e], proj_r.at[d - 1, e], S_PROJ + 3 * e + d - 1, dev_y(d))

    def solve_group(n, carry):
        e, m = n // 4, n % 4
        d = (m == 0) * 2 + (m == 1) * 1 + (m == 2) * 3
        there = (y + d) % 4
        g = there * 2 + e
        rows = lb[g // 4, g % 4].reshape(128, WIDTH)
        weight = corr[...].reshape(1, 128, WIDTH)
        scaled = (rotated[g].reshape(4, 128, WIDTH) * weight).reshape(512, WIDTH).astype(BF)
        p = dot(scaled, rows, NT)
        packed = jnp.zeros((128, 128), F32)
        for q in range(4):
            packed = packed + jnp.where(group == q, p[q * 128 : (q + 1) * 128], 0.0)
        proj_s[there, e] = packed

        @pl.when(m < 3)
        def _():
            proj_copy(e, d).start()

        return carry

    lax.fori_loop(0, 8, solve_group, 0)
    left_sum()

    mine = pl.ds(pl.multiple_of(me * 16, 16), 16)

    def solved_first(e, d):
        return copy(sb.at[e, :, mine], sb.at[e, :, mine], S_S1 + 3 * e + d - 1, dev(0, d))

    def solved_second(e, d):
        part = sb.at[e, :, pl.ds(pl.multiple_of(u * 64, 64), 64)]
        return copy(part, part, S_S2 + 3 * e + d - 1, dev(d, 0))

    for e in range(2):
        for d in range(1, 4):
            proj_copy(e, d).wait_recv()
        whole = proj_s[y, e] + proj_r[0, e] + proj_r[1, e] + proj_r[2, e]
        solved = dot(whole, inv_bd[e], NN, HIGH).astype(BF)
        sb[e, :, mine] = solved.reshape(PARTS, 16, 128)
        for d in (2, 1, 3):
            solved_first(e, d).start()
    for e in range(2):
        for d in range(1, 4):
            solved_first(e, d).wait_recv()
        for d in (2, 1, 3):
            solved_second(e, d).start()

    for c in pending:
        c.wait_send()

    def leave(k, carry):
        @pl.when(k < 2)
        def _():
            relay(k + 2).wait_send()

        for c in far_copies(k) + near_copies(k):
            c.wait_send()
        for c in out2_copies(k):
            c.wait_send()
        return carry

    lax.fori_loop(0, PARTS, leave, 0)
    for d in range(1, 4):
        copy(a_mid.at[:, :, :, (v + d) % 4], a_recv.at[v], S_A2 + d - 1, dev(0, d)).wait_send()
        copy(a4.at[y], a4.at[y], S_AY + d - 1, dev_y(d)).wait_send()
        copy(gram_s.at[y], gram_r.at[d - 1], S_GRAM + d - 1, dev_y(d)).wait_send()
        copy(left_s.at[y], left_r.at[d - 1], S_LEFT + d - 1, dev_y(d)).wait_send()
        copy(damp_2.at[0], damp_2.at[d], S_D2 + d - 1, dev(d, 0)).wait_send()
        copy(damp_3.at[0], damp_3.at[d], S_D3 + d - 1, dev(0, d)).wait_send()
        for e in range(2):
            proj_copy(e, d).wait_send()
            solved_first(e, d).wait_send()
    copy(lb.at[h], lb.at[h], S_LS, sibling).wait_send()
    copy(left_f.at[own_rows], left_f.at[own_rows], S_LEFTS, sibling).wait_send()
    for n, (dy, dh) in enumerate(line):
        copy(damp_1.at[0], damp_1.at[1 + n], S_D1 + n, dev_y(dy, dh)).wait_send()

    copy(left_f.at[own_rows], left_f.at[own_rows], S_LEFTS, sibling).wait_recv()
    joined = []
    for e in range(2):
        for d in range(1, 4):
            solved_second(e, d).wait_recv()

        right = jnp.zeros((2 * TOK, 128), F32)
        for i in range(PARTS):
            right = right + dot(ibuf[i], sb[e, place(i)], NN)
        joined.append((left_f[:, e * 128 : (e + 1) * 128] * right).reshape(4, RLEN, 128).sum(axis=1))
    joined = jnp.concatenate([jnp.concatenate(joined, axis=1), jnp.zeros((4, 256), F32)], axis=0)
    fin[y, h] = dot(joined, pick[...], NN, HIGH)
    for n, (dy, dh) in enumerate(line):
        copy(fin.at[y, h], fin.at[y, h], S_FIN + n, dev_y(dy, dh)).start()
    for n, (dy, dh) in enumerate(line):
        copy(fin.at[y, h], fin.at[y, h], S_FIN + n, dev_y(dy, dh)).wait_recv()
    scores = fin[...].reshape(8, 8, 128).sum(axis=0) / RLEN
    out[...] = jnp.where(h == 0, scores[0:2, :32], scores[2:4, :32])
    for e in range(2):
        for d in range(1, 4):
            solved_second(e, d).wait_send()
    for n, (dy, dh) in enumerate(line):
        copy(fin.at[y, h], fin.at[y, h], S_FIN + n, dev_y(dy, dh)).wait_send()


def shards(act, grad, lengths, basis_in, basis_out, query_act, query_grad):
    vm = pltpu.VMEM
    anywhere = pl.BlockSpec(memory_space=pl.ANY)
    return pl.pallas_call(
        kernel,
        out_shape=jax.ShapeDtypeStruct((2, 32), F32),
        in_specs=[anywhere, anywhere, pl.BlockSpec(memory_space=pltpu.SMEM)] + [anywhere] * 4,
        out_specs=pl.BlockSpec(memory_space=pltpu.VMEM),
        scratch_shapes=[
            vm((TOK + RANK, DIM), BF),
            vm((TOK + RANK, DIM), BF),
            vm((4, DIM, 256), BF),
            vm((2, TOK, 256), BF),
            vm((PARTS, 2 * TOK, 256), BF),
            vm((2 * TOK, WIDTH), BF),
            vm((2, 4, 4, RANK, WIDTH), BF),
            vm((2, 16, 16, 128), BF),
            vm((2, 2, 16, 16, 128), BF),
            vm((4, 2, 2, 4, 16, 128), BF),
            vm((4, 4, 2, 2, 16, 128), BF),
            vm((4, 8, 32, 128), BF),
            vm((RING, 256, WIDTH), F32),
            vm((PARTS, 256, WIDTH), BF),
            vm((PARTS, 2, 32, WIDTH), BF),
            vm((PARTS, 2, 64, WIDTH), BF),
            vm((PARTS, 4, 16, WIDTH), BF),
            vm((PARTS, 3, 16, WIDTH), BF),
            vm((PARTS, 16, WIDTH), F32),
            vm((4, 2, RANK, 128), F32),
            vm((3, 2, RANK, 128), F32),
            vm((4, TOK, 256), F32),
            vm((3, TOK, 256), F32),
            vm((2 * TOK, 256), F32),
            vm((8, 8, 128), F32),
            vm((4, 8, 128), F32),
            vm((4, 8, 128), F32),
            vm((8, RANK, 128), F32),
            vm((2, 128, 128), F32),
            vm((8, 512, WIDTH), F32),
            vm((4, 2, 128, 128), F32),
            vm((3, 2, 128, 128), F32),
            vm((2, PARTS, 256, 128), BF),
            vm((256, 128), F32),
            vm((4, 2, 8, 128), F32),
            pltpu.SemaphoreType.DMA((12,)),
            pltpu.SemaphoreType.DMA((N_SEM,)),
            pltpu.SemaphoreType.DMA((N_SEM,)),
        ],
        compiler_params=pltpu.CompilerParams(
            collective_id=0, has_side_effects=True, vmem_limit_bytes=60 * 2**20
        ),
    )(act, grad, lengths, basis_in, basis_out, query_act, query_grad)


def solution(mesh):
    return jax.shard_map(
        shards,
        mesh=mesh,
        in_specs=(
            P("dp", None),
            P("dp", None),
            P("dp"),
            P(None, "col"),
            P(None, "col"),
            P("dp", None),
            P("dp", None),
        ),
        out_specs=P("dp", None),
        check_vma=False,
    )
```
